32 devices in a mesh: groups: 2 (over y), aux: 16 (over z, x, core).
Axes of the slice: x: 2, y: 2, z: 4, core: 2. Of those that a mesh axis runs over, the one named last changes fastest.
Arguments:
- block_values: bfloat16 [8192, 4096], P(('groups', 'aux')), parts along dimension 0
- block_pairs: int32 [8192, 2], P(('groups', 'aux')), parts along dimension 0, may hold values from 0 to 319, as said below
- live_counts: int32 [32], P(('groups', 'aux')), parts along dimension 0, may hold values from 64 to 256, as said below
- occupied: bfloat16 [40960, 256], P(('groups', 'aux')), parts along dimension 0, may hold values from -6 to 6
Outputs:
- exchange_window: float32 [40960, 128], P(('groups', 'aux')), parts along dimension 0
The draws below stay inside these ranges and needn't reach their ends.
There are 2 independent parts, one for each index of `groups`. The reference program is written for one: setup_inputs(seed, part) draws one part's arguments, and reference() takes and returns one part's arrays. A program takes and returns all parts, laid end to end along the dimension named above; each array names one. Nothing has to cross between parts.
Inputs may be any that keep to these rules, and one draw needn't show every extreme that they name: `block_pairs`: row j holds the (row block, column block) of tile j; the tiles of auxiliary index p are rows p * 256 to (p + 1) * 256 - 1. The live tiles of index p are its first live_counts[p] slots; some index uses all 256 slots.
All inputs are finite; a program needn't handle non-finite values.
Results may differ from the reference program's by a relative error of at most 0.0037.
Values may be sent and summed in bfloat16 or wider, within the bound.
No kernel may reach another device: no remote copies, remote signals or barrier semaphores. Data moves between devices by JAX's collectives and lax.ppermute only.
A program may use at most 128 MiB of HBM per device.

```python
import math
import jax
import jax.numpy as jnp
from jax import lax

NAO = 20480
NOCC = 256
BLK = 64
WIN = 128
NB_DEV = 256
NBLK = 320
NAUX = 16
NTILES = 4096


def draw_block_values(key, part):
    key = jax.random.fold_in(key, 11)
    key_base, key_tile, key_index = jax.random.split(key, 3)
    index_count = NTILES // NB_DEV
    tile_scale = jnp.exp(jax.random.uniform(key_tile, (NTILES, 1, 1), jnp.float32, math.log(0.5), math.log(2.0)))
    index_scale = jnp.exp(jax.random.uniform(key_index, (index_count, 1, 1, 1), jnp.float32, math.log(0.5), math.log(2.0)))
    base = jax.random.normal(key_base, (NTILES, BLK, BLK), jnp.float32)
    values = base * tile_scale / math.sqrt(2.0 * BLK)
    values = values.reshape(index_count, NB_DEV, BLK, BLK) * index_scale
    return values.reshape(NTILES, BLK * BLK).astype(jnp.bfloat16)


def draw_block_pairs(key, part):
    key = jax.random.fold_in(key, 12)
    pair_rows = jax.random.randint(key, (NTILES, 2), 0, NBLK, dtype=jnp.int32)
    pair_rows = pair_rows.at[0].set(NBLK - 1)
    pair_rows = pair_rows.at[1].set(0)
    return pair_rows.astype(jnp.int32)


def draw_live_counts(key, part):
    key = jax.random.fold_in(key, 13)
    key_count, key_full = jax.random.split(key, 2)
    index_count = NTILES // NB_DEV
    count_rows = jax.random.randint(key_count, (index_count,), max(1, NB_DEV // 4), NB_DEV + 1, dtype=jnp.int32)
    full_index = jax.random.randint(key_full, (), 0, index_count, dtype=jnp.int32)
    count_rows = jnp.where(jnp.arange(index_count, dtype=jnp.int32) == full_index, NB_DEV, count_rows)
    return count_rows.astype(jnp.int32)


def block_levels(stream_key, extent, shards, smallest, top_value):
    def one(position, blocks):
        steps = jax.random.uniform(jax.random.fold_in(jax.random.fold_in(stream_key, 6), position), (blocks,), jnp.float32, smallest / len(shards), top_value / len(shards))
        return jnp.repeat(jnp.exp(steps), extent[position] // blocks).reshape((-1,) + (1,) * (len(extent) - position - 1))

    factor_of = one(*shards[0])
    for cut in shards[1:]:
        factor_of = factor_of * one(*cut)
    return factor_of


def normal_values(rng, extent, width, reach, cuts=(), kind=jnp.bfloat16):
    drawn = jax.random.normal(rng, extent, jnp.float32) * width
    if len(cuts) > 0:
        drawn = block_levels(rng, extent, cuts, -0.22, 0.18) * drawn
    return jnp.clip(drawn, min=-reach, max=reach).astype(kind)


def setup_inputs(seed: int = 0, part: int = 0) -> dict:
    keys = jax.random.split(jax.random.key(seed), 5)
    own_keys = jax.random.split(jax.random.fold_in(keys[4], part), 5)
    block_values = draw_block_values(jax.random.fold_in(jax.random.fold_in(keys[4], part), 71), part)
    block_pairs = draw_block_pairs(jax.random.fold_in(jax.random.fold_in(keys[4], part), 71), part)
    live_counts = draw_live_counts(jax.random.fold_in(jax.random.fold_in(keys[4], part), 71), part)
    occupied = normal_values(own_keys[3], (NAO, NOCC), 1.0, 6.0, ((0, 16),))
    return dict(block_values=block_values, block_pairs=block_pairs, live_counts=live_counts, occupied=occupied)


def reference(block_values, block_pairs, live_counts, occupied):
    occ_blocks = occupied.reshape(NBLK, BLK, NOCC)
    values_by = block_values.reshape(NAUX, NB_DEV, BLK, BLK)
    pairs_by = block_pairs.reshape(NAUX, NB_DEV, 2)
    slot_index = jnp.arange(NB_DEV, dtype=jnp.int32)

    def one_index(total, inputs):
        tile_set, pair_set, count_one = inputs
        live_mask = (slot_index < count_one).astype(jnp.float32)
        picked = occ_blocks[pair_set[:, 1]].astype(jnp.float32)
        product = jnp.einsum('gab,gbk->gak', tile_set.astype(jnp.float32), picked)
        product = product * live_mask[:, None, None]
        half_sum = jnp.zeros((NBLK, BLK, NOCC), jnp.float32).at[pair_set[:, 0]].add(product)
        half_rows = half_sum.reshape(NAO, NOCC).astype(jnp.bfloat16)
        half_rows = lax.optimization_barrier(half_rows).astype(jnp.float32)
        term = jnp.dot(half_rows, half_rows[:WIN].T, preferred_element_type=jnp.float32)
        return (total + term, None)
    start_total = jnp.zeros((NAO, WIN), jnp.float32)
    total, _ = lax.scan(one_index, start_total, (values_by, pairs_by, live_counts))
    factor = 1.0 / math.sqrt(NAUX * NOCC)
    return total * factor
```

```python
import functools
import math

import jax
import jax.numpy as jnp
from jax import lax
from jax.experimental import pallas as pl
from jax.experimental.pallas import tpu as pltpu
from jax.sharding import PartitionSpec as P

BLK = 64
WIN = 128
LANES = 128
UNROLL = 8
VMEM_BYTES = 56 * 1024 * 1024


def gather_half(mine, theirs, occ, sem):
    rows = mine.shape[0]
    copies = [
        pltpu.make_async_copy(mine, occ.at[pl.ds(0, rows)], sem.at[0]),
        pltpu.make_async_copy(theirs, occ.at[pl.ds(rows, rows)], sem.at[1]),
    ]
    for copy in copies:
        copy.start()
    return copies


def clear(half):
    rows = half.shape[0]

    @pl.loop(0, rows // BLK)
    def _(index):
        half[pl.ds(pl.multiple_of(index * BLK, BLK), BLK), :] = jnp.zeros((BLK, LANES), jnp.float32)


def add_tiles(rows_ref, spots_ref, meta_ref, tiles, occ, half, piece):
    pieces = BLK // piece

    @pl.loop(0, meta_ref[0])
    def _(group):
        products = []
        for lane in range(UNROLL):
            slot = group * UNROLL + lane
            parts = [
                occ[pl.ds(pl.multiple_of(spots_ref[slot * pieces + cut], piece), piece), :]
                for cut in range(pieces)
            ]
            block = parts[0] if pieces == 1 else jnp.concatenate(parts, axis=0)
            products.append(jnp.dot(tiles[slot], block, preferred_element_type=jnp.float32))
        for lane in range(UNROLL):
            start = pl.multiple_of(rows_ref[group * UNROLL + lane], BLK)
            half[pl.ds(start, BLK), :] += products[lane]


def first_kernel(piece, rows_ref, spots_ref, meta_ref, mine, theirs, values, out, occ, tiles, half, sem):
    copies = gather_half(mine, theirs, occ, sem)
    load = pltpu.make_async_copy(values, tiles, sem.at[2])
    load.start()
    clear(half)
    load.wait()
    for copy in copies:
        copy.wait()
    add_tiles(rows_ref, spots_ref, meta_ref, tiles, occ, half, piece)
    total = out.shape[0]

    @pl.loop(0, total // 256)
    def _(index):
        span = pl.ds(pl.multiple_of(index * 256, 256), 256)
        out[span, :] = half[span, :].astype(jnp.bfloat16)


def last_kernel(
    piece, shard, rows_ref, spots_ref, meta_ref, mine, theirs, values, before, keep, send,
    occ, tiles, half, earlier, weights, keep_buf, send_buf, sem,
):
    copies = gather_half(mine, theirs, occ, sem)
    load = pltpu.make_async_copy(values, tiles, sem.at[2])
    load.start()
    fetch = pltpu.make_async_copy(before, earlier, sem.at[3])
    fetch.start()
    clear(half)
    load.wait()
    for copy in copies:
        copy.wait()
    add_tiles(rows_ref, spots_ref, meta_ref, tiles, occ, half, piece)
    fetch.wait()
    window = earlier[pl.ds(0, WIN), :].astype(jnp.float32)
    weights[pl.ds(0, LANES), :] = window.T.astype(jnp.bfloat16)
    weights[pl.ds(LANES, LANES), :] = half[pl.ds(0, WIN), :].T.astype(jnp.bfloat16)
    core = meta_ref[1]
    count = keep.shape[0]

    def rows_of(owner):
        span = pl.ds(pl.multiple_of(owner * shard, 32), shard)
        both = jnp.concatenate([earlier[span, :], half[span, :].astype(jnp.bfloat16)], axis=1)
        return jnp.dot(both, weights[...], preferred_element_type=jnp.float32)

    @pl.loop(0, count)
    def _(index):
        send_buf[index] = rows_of(2 * index + 1 - core).astype(jnp.bfloat16)
        pltpu.make_async_copy(send_buf.at[index], send.at[index], sem.at[0]).start()

    @pl.loop(0, count)
    def _(index):
        keep_buf[index] = rows_of(2 * index + core)
        pltpu.make_async_copy(keep_buf.at[index], keep.at[index], sem.at[1]).start()

    pltpu.make_async_copy(send_buf, send, sem.at[0]).wait()
    pltpu.make_async_copy(keep_buf, keep, sem.at[1]).wait()


def local(block_values, block_pairs, live_counts, occupied):
    owners = lax.axis_size("aux")
    core = lax.axis_index("aux") % 2
    shard, width = occupied.shape
    total = owners * shard
    slots = block_values.shape[0]
    piece = math.gcd(BLK, shard)
    same_core = [[2 * i + k for i in range(owners // 2)] for k in range(2)]
    swap = [(i, i ^ 1) for i in range(owners)]

    tiles = block_values.reshape(slots, BLK, BLK)
    live = live_counts[0]
    slot_ids = jnp.arange(slots, dtype=jnp.int32)
    row_starts = jnp.where(slot_ids < live, block_pairs[:, 0] * BLK, total)
    first = block_pairs[:, 1][:, None] * BLK + jnp.arange(BLK // piece, dtype=jnp.int32) * piece
    owner = first // shard
    other = (owner % 2) ^ core
    spots = (other * (total // 2) + owner // 2 * shard + first % shard).reshape(-1)
    meta = jnp.stack([(live + UNROLL - 1) // UNROLL, core]).astype(jnp.int32)

    smem = pl.BlockSpec(memory_space=pltpu.SMEM)
    hbm = pl.BlockSpec(memory_space=pl.ANY)
    vmem = pl.BlockSpec(memory_space=pltpu.VMEM)
    work = [
        pltpu.VMEM((total, LANES), jnp.bfloat16),
        pltpu.VMEM((slots, BLK, BLK), jnp.bfloat16),
        pltpu.VMEM((total + BLK, LANES), jnp.float32),
    ]
    params = pltpu.CompilerParams(vmem_limit_bytes=VMEM_BYTES)

    held = []
    for cut in range(width // LANES):
        mine = lax.all_gather(
            occupied[:, cut * LANES : (cut + 1) * LANES],
            "aux", axis_index_groups=same_core, axis=0, tiled=True,
        )
        held.append((mine, lax.ppermute(mine, "aux", swap)))

    before = pl.pallas_call(
        functools.partial(first_kernel, piece),
        out_shape=jax.ShapeDtypeStruct((total, LANES), jnp.bfloat16),
        in_specs=[smem] * 3 + [hbm] * 3,
        out_specs=vmem,
        scratch_shapes=work + [pltpu.SemaphoreType.DMA((3,))],
        compiler_params=params,
        cost_estimate=pl.CostEstimate(flops=2 * slots * BLK * BLK * LANES, bytes_accessed=15 << 20, transcendentals=0),
    )(row_starts, spots, meta, *held[0], tiles)

    keep, send = pl.pallas_call(
        functools.partial(last_kernel, piece, shard),
        out_shape=(
            jax.ShapeDtypeStruct((owners // 2, shard, WIN), jnp.float32),
            jax.ShapeDtypeStruct((owners // 2, shard, WIN), jnp.bfloat16),
        ),
        in_specs=[smem] * 3 + [hbm] * 4,
        out_specs=(hbm, hbm),
        scratch_shapes=work
        + [
            pltpu.VMEM((total, LANES), jnp.bfloat16),
            pltpu.VMEM((2 * LANES, WIN), jnp.bfloat16),
            pltpu.VMEM((owners // 2, shard, WIN), jnp.float32),
            pltpu.VMEM((owners // 2, shard, WIN), jnp.bfloat16),
            pltpu.SemaphoreType.DMA((4,)),
        ],
        compiler_params=params,
        cost_estimate=pl.CostEstimate(flops=2 * total * width * WIN, bytes_accessed=25 << 20, transcendentals=0),
    )(row_starts, spots, meta, *held[1], tiles, before)

    arrived = lax.ppermute(send, "aux", swap)
    pair_sum = (keep + arrived.astype(jnp.float32)).astype(jnp.bfloat16)
    block_sum = lax.psum_scatter(
        pair_sum.reshape(total // 2, WIN), "aux", axis_index_groups=same_core, scatter_dimension=0, tiled=True
    )
    factor = 1.0 / math.sqrt(owners * width)
    return block_sum.astype(jnp.float32) * factor


def solution(mesh):
    placed = (
        P(("groups", "aux"), None),
        P(("groups", "aux"), None),
        P(("groups", "aux")),
        P(("groups", "aux"), None),
    )
    return jax.shard_map(
        local, mesh=mesh, in_specs=placed, out_specs=P(("groups", "aux"), None), check_vma=False
    )
```

```python
import functools
import math

import jax
import jax.numpy as jnp
from jax import lax
from jax.experimental import pallas as pl
from jax.experimental.pallas import tpu as pltpu
from jax.sharding import PartitionSpec as P

BLK = 64
WIN = 128
LANES = 128
UNROLL = 8
VMEM_BYTES = 60 * 1024 * 1024
LINE = 4


def place(z, x, core):
    return (z * 2 + x) * 2 + core


def pairs_of(step, levels=range(LINE)):
    found = []
    for z in levels:
        for x in range(2):
            for core in range(2):
                found.append((place(z, x, core), place(*step(z, x), core)))
    return found


def spread(own):
    ends, middles = (0, LINE - 1), (1, 2)
    near = pairs_of(lambda z, x: (z ^ 1, x))
    inner = pairs_of(lambda z, x: (3 - z, x), middles)
    outward = pairs_of(lambda z, x: (0 if z == 1 else 3, x), middles)
    across = pairs_of(lambda z, x: (z, 1 - x))
    across_ends = pairs_of(lambda z, x: (z, 1 - x), ends)
    across_middles = pairs_of(lambda z, x: (z, 1 - x), middles)

    def move(array, pairs):
        return lax.ppermute(array, "aux", pairs)

    x_own = move(own, across)
    z1 = move(own, near)
    z3_mid = move(own, inner)
    x1 = move(z1, across)
    z2_mid = move(z1, inner)
    z2_end = move(z3_mid, outward)
    x3_mid = move(z3_mid, across_middles)
    x2_end = move(z2_end, across_ends)
    z3_end = move(z2_mid, outward)
    x2_mid = move(z2_mid, across_middles)
    x3_end = move(z3_end, across_ends)
    return [own, z1, (z2_end, z2_mid), (z3_end, z3_mid), x_own, x1, (x2_end, x2_mid), (x3_end, x3_mid)]


def start_when(condition, source, target, sem):
    @pl.when(condition)
    def _():
        pltpu.make_async_copy(source, target, sem).start()


def work_kernel(
    piece, shard, kinds, rows_ref, spots_ref, meta_ref, *refs,
):
    sources = refs[: sum(kinds)]
    values, other_values, keep, send, occ, tiles, half, weights, keep_buf, send_buf, sem = refs[sum(kinds):]
    core, at_end = meta_ref[2], meta_ref[3]
    slot_rows = occ.shape[0] // len(kinds)
    first = 0
    for index, kind in enumerate(kinds):
        target = occ.at[pl.ds(index * slot_rows, slot_rows)]
        if kind == 1:
            pltpu.make_async_copy(sources[first], target, sem.at[0]).start()
        else:
            start_when(at_end == 1, sources[first], target, sem.at[0])
            start_when(at_end == 0, sources[first + 1], target, sem.at[0])
        first += kind
    loads = [
        pltpu.make_async_copy(values, tiles.at[0], sem.at[1]),
        pltpu.make_async_copy(other_values, tiles.at[1], sem.at[2]),
    ]
    for load in loads:
        load.start()

    @pl.loop(0, half.shape[1] // BLK)
    def _(index):
        span = pl.ds(pl.multiple_of(index * BLK, BLK), BLK)
        for side in range(2):
            half[side, span, :] = jnp.zeros((BLK, LANES), jnp.float32)

    pltpu.make_async_copy(occ, occ, sem.at[0]).wait()
    slots = tiles.shape[1]
    pieces = BLK // piece

    for side in range(2):
        loads[side].wait()

        @pl.loop(0, meta_ref[side])
        def _(group):
            products = []
            for lane in range(UNROLL):
                slot = group * UNROLL + lane
                table = side * slots + slot
                parts = [
                    occ[pl.ds(pl.multiple_of(spots_ref[table * pieces + cut], piece), piece), :]
                    for cut in range(pieces)
                ]
                block = parts[0] if pieces == 1 else jnp.concatenate(parts, axis=0)
                products.append(jnp.dot(tiles[side, slot], block, preferred_element_type=jnp.float32))
            for lane in range(UNROLL):
                start = pl.multiple_of(rows_ref[side * slots + group * UNROLL + lane], BLK)
                half[side, pl.ds(start, BLK), :] += products[lane]

        weights[pl.ds(side * LANES, LANES), :] = half[side, pl.ds(0, WIN), :].T.astype(jnp.bfloat16)

    count = keep.shape[0]

    def rows_of(owner):
        span = pl.ds(pl.multiple_of(owner * shard, 32), shard)
        both = jnp.concatenate([half[side, span, :].astype(jnp.bfloat16) for side in range(2)], axis=1)
        return jnp.dot(both, weights[...], preferred_element_type=jnp.float32)

    @pl.loop(0, count)
    def _(index):
        send_buf[index] = rows_of(2 * index + 1 - core).astype(jnp.bfloat16)
        pltpu.make_async_copy(send_buf.at[index], send.at[index], sem.at[3]).start()

    @pl.loop(0, count)
    def _(index):
        keep_buf[index] = rows_of(2 * index + core)
        pltpu.make_async_copy(keep_buf.at[index], keep.at[index], sem.at[4]).start()

    pltpu.make_async_copy(send_buf, send, sem.at[3]).wait()
    pltpu.make_async_copy(keep_buf, keep, sem.at[4]).wait()


def local(block_values, block_pairs, live_counts, occupied):
    owners = lax.axis_size("aux")
    me = lax.axis_index("aux")
    core, chip = me % 2, me // 2
    shard, width = occupied.shape
    total = owners * shard
    slots = block_values.shape[0]
    piece = math.gcd(BLK, shard)
    same_core = [[2 * i + k for i in range(owners // 2)] for k in range(2)]
    swap = [(i, i ^ 1) for i in range(owners)]

    mine = lax.dynamic_slice_in_dim(occupied, core * LANES, LANES, 1)
    given = lax.dynamic_slice_in_dim(occupied, (1 - core) * LANES, LANES, 1)
    own = jnp.concatenate([mine, lax.ppermute(given, "aux", swap)], axis=0)

    if owners == 4 * LINE:
        held = spread(own)
    else:
        held = [lax.all_gather(own, "aux", axis_index_groups=same_core, axis=0, tiled=True)]
    kinds = [len(entry) if isinstance(entry, tuple) else 1 for entry in held]
    sources = [array for entry in held for array in (entry if isinstance(entry, tuple) else (entry,))]

    live = live_counts[0]
    slot_ids = jnp.arange(slots, dtype=jnp.int32)
    row_starts = jnp.where(slot_ids < live, block_pairs[:, 0] * BLK, total)
    groups = jnp.full((slots,), (live + UNROLL - 1) // UNROLL, jnp.int32)
    table = jnp.stack([row_starts, block_pairs[:, 1], groups])
    other_table = lax.ppermute(table, "aux", swap)
    other_values = lax.ppermute(block_values, "aux", swap)
    tiles = block_values.reshape(slots, BLK, BLK)
    other_tiles = other_values.reshape(slots, BLK, BLK)

    rows = jnp.concatenate([table[0], other_table[0]])
    columns = jnp.concatenate([table[1], other_table[1]])
    first = columns[:, None] * BLK + jnp.arange(BLK // piece, dtype=jnp.int32) * piece
    owner = first // shard
    owner_chip = owner // 2
    slot_of = owner_chip
    if len(held) > 1:
        slot_of = ((owner_chip // 2) ^ (chip // 2)) + LINE * ((owner_chip % 2) ^ (chip % 2))
    spots = (slot_of * (2 * shard) + ((owner % 2) ^ core) * shard + first % shard).reshape(-1)
    level = chip // 2
    at_end = ((level == 0) | (level == LINE - 1)).astype(jnp.int32)
    meta = jnp.stack([table[2, 0], other_table[2, 0], core, at_end]).astype(jnp.int32)

    smem = pl.BlockSpec(memory_space=pltpu.SMEM)
    hbm = pl.BlockSpec(memory_space=pl.ANY)
    keep, send = pl.pallas_call(
        functools.partial(work_kernel, piece, shard, kinds),
        out_shape=(
            jax.ShapeDtypeStruct((owners // 2, shard, WIN), jnp.float32),
            jax.ShapeDtypeStruct((owners // 2, shard, WIN), jnp.bfloat16),
        ),
        in_specs=[smem] * 3 + [hbm] * (len(sources) + 2),
        out_specs=(hbm, hbm),
        scratch_shapes=[
            pltpu.VMEM((total, LANES), jnp.bfloat16),
            pltpu.VMEM((2, slots, BLK, BLK), jnp.bfloat16),
            pltpu.VMEM((2, total + BLK, LANES), jnp.float32),
            pltpu.VMEM((2 * LANES, WIN), jnp.bfloat16),
            pltpu.VMEM((owners // 2, shard, WIN), jnp.float32),
            pltpu.VMEM((owners // 2, shard, WIN), jnp.bfloat16),
            pltpu.SemaphoreType.DMA((5,)),
        ],
        compiler_params=pltpu.CompilerParams(vmem_limit_bytes=VMEM_BYTES),
        cost_estimate=pl.CostEstimate(
            flops=2 * total * width * (WIN + BLK), bytes_accessed=25 << 20, transcendentals=0
        ),
    )(rows, spots, meta, *sources, tiles, other_tiles)

    arrived = lax.ppermute(send, "aux", swap)
    pair_sum = (keep + arrived.astype(jnp.float32)).astype(jnp.bfloat16)
    block_sum = lax.psum_scatter(
        pair_sum.reshape(total // 2, WIN), "aux", axis_index_groups=same_core, scatter_dimension=0, tiled=True
    )
    factor = 1.0 / math.sqrt(owners * width)
    return block_sum.astype(jnp.float32) * factor


def solution(mesh):
    placed = (
        P(("groups", "aux"), None),
        P(("groups", "aux"), None),
        P(("groups", "aux")),
        P(("groups", "aux"), None),
    )
    return jax.shard_map(
        local, mesh=mesh, in_specs=placed, out_specs=P(("groups", "aux"), None), check_vma=False
    )
```

```python
import functools
import math

import jax
import jax.numpy as jnp
from jax import lax
from jax.experimental import pallas as pl
from jax.experimental.pallas import tpu as pltpu
from jax.sharding import PartitionSpec as P

BLK = 64
WIN = 128
LANES = 128
UNROLL = 8
VMEM_BYTES = 60 * 1024 * 1024
LINE = 4


def place(z, x, core):
    return (z * 2 + x) * 2 + core


def pairs_of(step, levels=range(LINE)):
    found = []
    for z in levels:
        for x in range(2):
            for core in range(2):
                found.append((place(z, x, core), place(*step(z, x), core)))
    return found


def after(array, *others):
    return lax.optimization_barrier((array, *others))[0]


def move(array, pairs):
    return lax.ppermute(array, "aux", pairs)


ENDS, MIDDLES = (0, LINE - 1), (1, 2)
NEAR = pairs_of(lambda z, x: (z ^ 1, x))
INNER = pairs_of(lambda z, x: (3 - z, x), MIDDLES)
OUTWARD = pairs_of(lambda z, x: (0 if z == 1 else 3, x), MIDDLES)
INWARD = pairs_of(lambda z, x: (1 if z == 0 else 2, x), ENDS)
ACROSS = pairs_of(lambda z, x: (z, 1 - x))


def spread(own):
    x_own = move(own, ACROSS)
    z1 = move(own, NEAR)
    inner1 = move(own, INNER)
    x1 = move(after(z1, x_own), ACROSS)
    inner2 = move(z1, INNER)
    outward1 = move(inner1, OUTWARD)
    early = inner1 + outward1
    x_early = move(after(early, x1), ACROSS)
    late = inner2 + move(inner2, OUTWARD)
    x_late = move(after(late, x_early), ACROSS)
    return [own, z1, early, late, x_own, x1, x_early, x_late]


def collect(keep, send_far, send_near, swap):
    far = move(send_far, swap)
    near = move(send_near, swap)

    def narrow(array):
        return array.astype(jnp.bfloat16)

    crossed = {}
    last = None
    for step in (3, 2, 1, 0):
        part = narrow(keep[LINE + step] + far[step].astype(jnp.float32))
        if last is not None:
            part = after(part, last)
        last = crossed[step] = move(part, ACROSS)
    held = {
        step: keep[step] + near[step].astype(jnp.float32) + crossed[step].astype(jnp.float32) for step in range(LINE)
    }
    held[2] = held[2] + (from_end := move(narrow(held[3]), INWARD)).astype(jnp.float32)
    inner2 = move(narrow(held[2]), INNER)
    held[3] = held[3] + move(after(narrow(held[2]), from_end), INWARD).astype(jnp.float32)
    inner3 = move(narrow(held[3]), INNER)
    held[1] = held[1] + inner2.astype(jnp.float32)
    beside = move(narrow(held[1]), NEAR)
    return held[0] + beside.astype(jnp.float32) + inner3.astype(jnp.float32)


def work_kernel(piece, shard, chips_ref, rows_ref, spots_ref, meta_ref, *refs):
    count = len(refs) - 13
    sources = refs[:count]
    values, other_values, keep, send_far, send_near = refs[count : count + 5]
    occ, tiles, half, weights, keep_buf, far_buf, near_buf, sem = refs[count + 5 :]
    core = meta_ref[2]
    slot_rows = occ.shape[0] // count
    for index in range(count):
        pltpu.make_async_copy(sources[index], occ.at[pl.ds(index * slot_rows, slot_rows)], sem.at[0]).start()
    loads = [
        pltpu.make_async_copy(values, tiles.at[0], sem.at[1]),
        pltpu.make_async_copy(other_values, tiles.at[1], sem.at[2]),
    ]
    for load in loads:
        load.start()

    @pl.loop(0, half.shape[1] // BLK)
    def _(index):
        span = pl.ds(pl.multiple_of(index * BLK, BLK), BLK)
        for side in range(2):
            half[side, span, :] = jnp.zeros((BLK, LANES), jnp.float32)

    pltpu.make_async_copy(occ, occ, sem.at[0]).wait()
    slots = tiles.shape[1]
    pieces = BLK // piece

    for side in range(2):
        loads[side].wait()

        @pl.loop(0, meta_ref[side])
        def _(group):
            products = []
            for lane in range(UNROLL):
                slot = group * UNROLL + lane
                table = side * slots + slot
                parts = [
                    occ[pl.ds(pl.multiple_of(spots_ref[table * pieces + cut], piece), piece), :]
                    for cut in range(pieces)
                ]
                block = parts[0] if pieces == 1 else jnp.concatenate(parts, axis=0)
                products.append(jnp.dot(tiles[side, slot], block, preferred_element_type=jnp.float32))
            for lane in range(UNROLL):
                start = pl.multiple_of(rows_ref[side * slots + group * UNROLL + lane], BLK)
                half[side, pl.ds(start, BLK), :] += products[lane]

        weights[pl.ds(side * LANES, LANES), :] = half[side, pl.ds(0, WIN), :].T.astype(jnp.bfloat16)

    def rows_of(owner):
        span = pl.ds(pl.multiple_of(owner * shard, 32), shard)
        both = jnp.concatenate([half[side, span, :].astype(jnp.bfloat16) for side in range(2)], axis=1)
        return jnp.dot(both, weights[...], preferred_element_type=jnp.float32)

    near_count = near_buf.shape[0]
    for buf, out, base, copied in ((far_buf, send_far, near_count, 3), (near_buf, send_near, 0, 4)):

        @pl.loop(0, buf.shape[0])
        def _(index):
            chip = chips_ref[base + index]
            buf[index] = rows_of(2 * chip + 1 - core).astype(jnp.bfloat16)
            pltpu.make_async_copy(buf.at[index], out.at[index], sem.at[copied]).start()

    @pl.loop(0, keep.shape[0])
    def _(index):
        keep_buf[index] = rows_of(2 * chips_ref[index] + core)
        pltpu.make_async_copy(keep_buf.at[index], keep.at[index], sem.at[5]).start()

    pltpu.make_async_copy(far_buf, send_far, sem.at[3]).wait()
    pltpu.make_async_copy(near_buf, send_near, sem.at[4]).wait()
    pltpu.make_async_copy(keep_buf, keep, sem.at[5]).wait()


def local(block_values, block_pairs, live_counts, occupied):
    owners = lax.axis_size("aux")
    me = lax.axis_index("aux")
    core, chip = me % 2, me // 2
    shard, width = occupied.shape
    total = owners * shard
    slots = block_values.shape[0]
    piece = math.gcd(BLK, shard)
    same_core = [[2 * i + k for i in range(owners // 2)] for k in range(2)]
    swap = [(i, i ^ 1) for i in range(owners)]

    mine = lax.dynamic_slice_in_dim(occupied, core * LANES, LANES, 1)
    given = lax.dynamic_slice_in_dim(occupied, (1 - core) * LANES, LANES, 1)
    own = jnp.concatenate([mine, lax.ppermute(given, "aux", swap)], axis=0)

    chips = owners // 2
    slot_ids = jnp.arange(chips, dtype=jnp.int32)
    lined = chips == 2 * LINE
    if lined:
        held = spread(own)
        chip_of_slot = ((slot_ids % LINE) ^ (chip // 2)) * 2 + ((slot_ids // LINE) ^ (chip % 2))
    else:
        held = [lax.all_gather(own, "aux", axis_index_groups=same_core, axis=0, tiled=True)]
        chip_of_slot = slot_ids

    live = live_counts[0]
    tile_ids = jnp.arange(slots, dtype=jnp.int32)
    row_starts = jnp.where(tile_ids < live, block_pairs[:, 0] * BLK, total)
    groups = jnp.full((slots,), (live + UNROLL - 1) // UNROLL, jnp.int32)
    table = jnp.stack([row_starts, block_pairs[:, 1], groups])
    other_table = lax.ppermute(table, "aux", swap)
    block_values = after(block_values, own)
    tiles = block_values.reshape(slots, BLK, BLK)
    other_values = lax.ppermute(block_values, "aux", swap)
    other_tiles = other_values.reshape(slots, BLK, BLK)

    rows = jnp.concatenate([table[0], other_table[0]])
    columns = jnp.concatenate([table[1], other_table[1]])
    first = columns[:, None] * BLK + jnp.arange(BLK // piece, dtype=jnp.int32) * piece
    owner = first // shard
    owner_chip = owner // 2
    slot_of = owner_chip
    if lined:
        level = chip // 2
        apart = (owner_chip // 2) ^ level
        in_middle = ((level == 1) | (level == 2)).astype(jnp.int32)
        slot_of = (apart ^ (apart // 2 * in_middle)) + LINE * ((owner_chip % 2) ^ (chip % 2))
    spots = (slot_of * (2 * shard) + ((owner % 2) ^ core) * shard + first % shard).reshape(-1)
    meta = jnp.stack([table[2, 0], other_table[2, 0], core]).astype(jnp.int32)

    smem = pl.BlockSpec(memory_space=pltpu.SMEM)
    hbm = pl.BlockSpec(memory_space=pl.ANY)
    sizes = (chips, chips // 2, chips - chips // 2)
    keep, send_far, send_near = pl.pallas_call(
        functools.partial(work_kernel, piece, shard),
        out_shape=(
            jax.ShapeDtypeStruct((chips, shard, WIN), jnp.float32),
            jax.ShapeDtypeStruct((sizes[1], shard, WIN), jnp.bfloat16),
            jax.ShapeDtypeStruct((sizes[2], shard, WIN), jnp.bfloat16),
        ),
        in_specs=[smem] * 4 + [hbm] * (len(held) + 2),
        out_specs=(hbm, hbm, hbm),
        scratch_shapes=[
            pltpu.VMEM((total, LANES), jnp.bfloat16),
            pltpu.VMEM((2, slots, BLK, BLK), jnp.bfloat16),
            pltpu.VMEM((2, total + BLK, LANES), jnp.float32),
            pltpu.VMEM((2 * LANES, WIN), jnp.bfloat16),
            pltpu.VMEM((sizes[0], shard, WIN), jnp.float32),
            pltpu.VMEM((sizes[1], shard, WIN), jnp.bfloat16),
            pltpu.VMEM((sizes[2], shard, WIN), jnp.bfloat16),
            pltpu.SemaphoreType.DMA((6,)),
        ],
        compiler_params=pltpu.CompilerParams(vmem_limit_bytes=VMEM_BYTES),
        cost_estimate=pl.CostEstimate(
            flops=2 * total * width * (WIN + BLK), bytes_accessed=25 << 20, transcendentals=0
        ),
    )(chip_of_slot, rows, spots, meta, *held, tiles, other_tiles)

    factor = 1.0 / math.sqrt(owners * width)
    if lined:
        return collect(keep, send_far, send_near, swap) * factor
    send = jnp.concatenate([send_near, send_far], axis=0)
    pair_sum = (keep + move(send, swap).astype(jnp.float32)).astype(jnp.bfloat16)
    block_sum = lax.psum_scatter(
        pair_sum.reshape(total // 2, WIN), "aux", axis_index_groups=same_core, scatter_dimension=0, tiled=True
    )
    return block_sum.astype(jnp.float32) * factor


def solution(mesh):
    placed = (
        P(("groups", "aux"), None),
        P(("groups", "aux"), None),
        P(("groups", "aux")),
        P(("groups", "aux"), None),
    )
    return jax.shard_map(
        local, mesh=mesh, in_specs=placed, out_specs=P(("groups", "aux"), None), check_vma=False
    )
```

```python
import functools
import math

import jax
import jax.numpy as jnp
from jax import lax
from jax.experimental import pallas as pl
from jax.experimental.pallas import tpu as pltpu
from jax.sharding import PartitionSpec as P

BLK = 64
WIN = 128
LANES = 128
UNROLL = 8
VMEM_BYTES = 60 * 1024 * 1024
LINE = 4


def place(z, x, core):
    return (z * 2 + x) * 2 + core


def pairs_of(step, levels=range(LINE)):
    found = []
    for z in levels:
        for x in range(2):
            for core in range(2):
                found.append((place(z, x, core), place(*step(z, x), core)))
    return found


def after(array, *others):
    return lax.optimization_barrier((array, *others))[0]


def move(array, pairs):
    return lax.ppermute(array, "aux", pairs)


ENDS, MIDDLES = (0, LINE - 1), (1, 2)
NEAR = pairs_of(lambda z, x: (z ^ 1, x))
INNER = pairs_of(lambda z, x: (3 - z, x), MIDDLES)
OUTWARD = pairs_of(lambda z, x: (0 if z == 1 else 3, x), MIDDLES)
INWARD = pairs_of(lambda z, x: (1 if z == 0 else 2, x), ENDS)
ACROSS = pairs_of(lambda z, x: (z, 1 - x))


class Queue:
    def __init__(self, pairs):
        self.pairs = pairs
        self.done = []

    def move(self, array):
        if len(self.done) > 1:
            array = after(array, self.done[-2])
        self.done.append(move(array, self.pairs))
        return self.done[-1]


def spread(parts):
    across = Queue(ACROSS)
    x_own = [across.move(own) for own in parts]
    z1 = [move(own, NEAR) for own in parts]
    inner1 = [move(own, INNER) for own in parts]
    x1 = [across.move(part) for part in z1]
    outward1 = [move(part, OUTWARD) for part in inner1]
    inner2 = [move(part, INNER) for part in z1]
    early = [one + two for one, two in zip(inner1, outward1)]
    x_early = [across.move(part) for part in early]
    outward2 = [move(part, OUTWARD) for part in inner2]
    late = [one + two for one, two in zip(inner2, outward2)]
    x_late = [across.move(part) for part in late]
    return [array for part in zip(parts, z1, early, late, x_own, x1, x_early, x_late) for array in part]


def collect(keep, send_far, send_near, swap):
    far = move(send_far, swap)
    near = move(send_near, swap)

    def narrow(array):
        return array.astype(jnp.bfloat16)

    across = Queue(ACROSS)
    crossed = {}
    for step in (3, 2, 1, 0):
        crossed[step] = across.move(narrow(keep[LINE + step] + far[step].astype(jnp.float32)))
    held = {
        step: keep[step] + near[step].astype(jnp.float32) + crossed[step].astype(jnp.float32) for step in range(LINE)
    }
    held[2] = held[2] + (from_end := move(narrow(held[3]), INWARD)).astype(jnp.float32)
    inner2 = move(narrow(held[2]), INNER)
    held[3] = held[3] + move(after(narrow(held[2]), from_end), INWARD).astype(jnp.float32)
    inner3 = move(narrow(held[3]), INNER)
    held[1] = held[1] + inner2.astype(jnp.float32)
    beside = move(narrow(held[1]), NEAR)
    return held[0] + beside.astype(jnp.float32) + inner3.astype(jnp.float32)


def work_kernel(piece, shard, chips_ref, rows_ref, spots_ref, meta_ref, *refs):
    count = len(refs) - 13
    sources = refs[:count]
    values, other_values, keep, send_far, send_near = refs[count : count + 5]
    occ, tiles, half, weights, keep_buf, far_buf, near_buf, sem = refs[count + 5 :]
    core = meta_ref[2]
    slot_rows = occ.shape[0] // count
    for index in range(count):
        pltpu.make_async_copy(sources[index], occ.at[pl.ds(index * slot_rows, slot_rows)], sem.at[0]).start()
    loads = [
        pltpu.make_async_copy(values, tiles.at[0], sem.at[1]),
        pltpu.make_async_copy(other_values, tiles.at[1], sem.at[2]),
    ]
    for load in loads:
        load.start()

    @pl.loop(0, half.shape[1] // BLK)
    def _(index):
        span = pl.ds(pl.multiple_of(index * BLK, BLK), BLK)
        for side in range(2):
            half[side, span, :] = jnp.zeros((BLK, LANES), jnp.float32)

    pltpu.make_async_copy(occ, occ, sem.at[0]).wait()
    slots = tiles.shape[1]
    pieces = BLK // piece

    for side in range(2):
        loads[side].wait()

        @pl.loop(0, meta_ref[side])
        def _(group):
            products = []
            for lane in range(UNROLL):
                slot = group * UNROLL + lane
                table = side * slots + slot
                parts = [
                    occ[pl.ds(pl.multiple_of(spots_ref[table * pieces + cut], piece), piece), :]
                    for cut in range(pieces)
                ]
                block = parts[0] if pieces == 1 else jnp.concatenate(parts, axis=0)
                products.append(jnp.dot(tiles[side, slot], block, preferred_element_type=jnp.float32))
            for lane in range(UNROLL):
                start = pl.multiple_of(rows_ref[side * slots + group * UNROLL + lane], BLK)
                half[side, pl.ds(start, BLK), :] += products[lane]

        weights[pl.ds(side * LANES, LANES), :] = half[side, pl.ds(0, WIN), :].T.astype(jnp.bfloat16)

    def rows_of(owner):
        span = pl.ds(pl.multiple_of(owner * shard, 32), shard)
        both = jnp.concatenate([half[side, span, :].astype(jnp.bfloat16) for side in range(2)], axis=1)
        return jnp.dot(both, weights[...], preferred_element_type=jnp.float32)

    near_count = near_buf.shape[0]
    for buf, out, base, copied in ((far_buf, send_far, near_count, 3), (near_buf, send_near, 0, 4)):

        @pl.loop(0, buf.shape[0])
        def _(index):
            chip = chips_ref[base + index]
            buf[index] = rows_of(2 * chip + 1 - core).astype(jnp.bfloat16)
            pltpu.make_async_copy(buf.at[index], out.at[index], sem.at[copied]).start()

    @pl.loop(0, keep.shape[0])
    def _(index):
        keep_buf[index] = rows_of(2 * chips_ref[index] + core)
        pltpu.make_async_copy(keep_buf.at[index], keep.at[index], sem.at[5]).start()

    pltpu.make_async_copy(far_buf, send_far, sem.at[3]).wait()
    pltpu.make_async_copy(near_buf, send_near, sem.at[4]).wait()
    pltpu.make_async_copy(keep_buf, keep, sem.at[5]).wait()


def local(block_values, block_pairs, live_counts, occupied):
    owners = lax.axis_size("aux")
    me = lax.axis_index("aux")
    core, chip = me % 2, me // 2
    shard, width = occupied.shape
    total = owners * shard
    slots = block_values.shape[0]
    piece = math.gcd(BLK, shard)
    same_core = [[2 * i + k for i in range(owners // 2)] for k in range(2)]
    swap = [(i, i ^ 1) for i in range(owners)]

    mine = lax.dynamic_slice_in_dim(occupied, core * LANES, LANES, 1)
    given = lax.dynamic_slice_in_dim(occupied, (1 - core) * LANES, LANES, 1)
    parts = (mine, move(given, swap))

    chips = owners // 2
    slot_ids = jnp.arange(chips, dtype=jnp.int32)
    lined = chips == 2 * LINE
    if lined:
        held = spread(parts)
        chip_of_slot = ((slot_ids % LINE) ^ (chip // 2)) * 2 + ((slot_ids // LINE) ^ (chip % 2))
    else:
        held = [lax.all_gather(part, "aux", axis_index_groups=same_core, axis=0, tiled=True) for part in parts]
        chip_of_slot = slot_ids

    live = live_counts[0]
    tile_ids = jnp.arange(slots, dtype=jnp.int32)
    row_starts = jnp.where(tile_ids < live, block_pairs[:, 0] * BLK, total)
    groups = jnp.full((slots,), (live + UNROLL - 1) // UNROLL, jnp.int32)
    table = jnp.stack([row_starts, block_pairs[:, 1], groups])
    other_table = lax.ppermute(table, "aux", swap)
    block_values = after(block_values, parts[1])
    tiles = block_values.reshape(slots, BLK, BLK)
    other_values = lax.ppermute(block_values, "aux", swap)
    other_tiles = other_values.reshape(slots, BLK, BLK)

    rows = jnp.concatenate([table[0], other_table[0]])
    columns = jnp.concatenate([table[1], other_table[1]])
    first = columns[:, None] * BLK + jnp.arange(BLK // piece, dtype=jnp.int32) * piece
    owner = first // shard
    owner_chip = owner // 2
    slot_of = owner_chip
    if lined:
        level = chip // 2
        apart = (owner_chip // 2) ^ level
        in_middle = ((level == 1) | (level == 2)).astype(jnp.int32)
        slot_of = (apart ^ (apart // 2 * in_middle)) + LINE * ((owner_chip % 2) ^ (chip % 2))
    spots = ((((owner % 2) ^ core) * chips + slot_of) * shard + first % shard).reshape(-1)
    meta = jnp.stack([table[2, 0], other_table[2, 0], core]).astype(jnp.int32)

    smem = pl.BlockSpec(memory_space=pltpu.SMEM)
    hbm = pl.BlockSpec(memory_space=pl.ANY)
    sizes = (chips, chips // 2, chips - chips // 2)
    keep, send_far, send_near = pl.pallas_call(
        functools.partial(work_kernel, piece, shard),
        out_shape=(
            jax.ShapeDtypeStruct((chips, shard, WIN), jnp.float32),
            jax.ShapeDtypeStruct((sizes[1], shard, WIN), jnp.bfloat16),
            jax.ShapeDtypeStruct((sizes[2], shard, WIN), jnp.bfloat16),
        ),
        in_specs=[smem] * 4 + [hbm] * (len(held) + 2),
        out_specs=(hbm, hbm, hbm),
        scratch_shapes=[
            pltpu.VMEM((total, LANES), jnp.bfloat16),
            pltpu.VMEM((2, slots, BLK, BLK), jnp.bfloat16),
            pltpu.VMEM((2, total + BLK, LANES), jnp.float32),
            pltpu.VMEM((2 * LANES, WIN), jnp.bfloat16),
            pltpu.VMEM((sizes[0], shard, WIN), jnp.float32),
            pltpu.VMEM((sizes[1], shard, WIN), jnp.bfloat16),
            pltpu.VMEM((sizes[2], shard, WIN), jnp.bfloat16),
            pltpu.SemaphoreType.DMA((6,)),
        ],
        compiler_params=pltpu.CompilerParams(vmem_limit_bytes=VMEM_BYTES),
        cost_estimate=pl.CostEstimate(
            flops=2 * total * width * (WIN + BLK), bytes_accessed=25 << 20, transcendentals=0
        ),
    )(chip_of_slot, rows, spots, meta, *held, tiles, other_tiles)

    factor = 1.0 / math.sqrt(owners * width)
    if lined:
        return collect(keep, send_far, send_near, swap) * factor
    send = jnp.concatenate([send_near, send_far], axis=0)
    pair_sum = (keep + move(send, swap).astype(jnp.float32)).astype(jnp.bfloat16)
    block_sum = lax.psum_scatter(
        pair_sum.reshape(total // 2, WIN), "aux", axis_index_groups=same_core, scatter_dimension=0, tiled=True
    )
    return block_sum.astype(jnp.float32) * factor


def solution(mesh):
    placed = (
        P(("groups", "aux"), None),
        P(("groups", "aux"), None),
        P(("groups", "aux")),
        P(("groups", "aux"), None),
    )
    return jax.shard_map(
        local, mesh=mesh, in_specs=placed, out_specs=P(("groups", "aux"), None), check_vma=False
    )
```

```python
import functools
import math

import jax
import jax.numpy as jnp
from jax import lax
from jax.experimental import pallas as pl
from jax.experimental.pallas import tpu as pltpu
from jax.sharding import PartitionSpec as P

BLK = 64
WIN = 128
LANES = 128
UNROLL = 8
VMEM_BYTES = 60 * 1024 * 1024
LINE = 4


def place(z, x, core):
    return (z * 2 + x) * 2 + core


def pairs_of(step):
    return [
        (place(z, x, core), place(*step(z, x), core)) for z in range(LINE) for x in range(2) for core in range(2)
    ]


def tie(*arrays):
    return lax.optimization_barrier(arrays)


def move(array, pairs):
    return lax.ppermute(array, "aux", pairs)


ALONG = pairs_of(lambda z, x: ((z + 1) % LINE, x))
ACROSS = pairs_of(lambda z, x: (z, 1 - x))


def spread(parts):
    lines, others = [[part] for part in parts], [[] for _ in parts]
    for step in range(LINE):
        for line, other in zip(lines, others):
            if other:
                line[-1], other[-1] = tie(line[-1], other[-1])
            now = line[-1]
            if step + 1 < LINE:
                line.append(move(now, ALONG))
            other.append(move(now, ACROSS))
    return [array for line, other in zip(lines, others) for array in line + other]


def collect(keep, send, swap):
    order = [LINE + 3, LINE + 2, 3, LINE + 1, 2, LINE, 1, 0]
    paired = {}
    for slot in order:
        paired[slot] = keep[slot] + move(send[slot], swap).astype(jnp.float32)
    crossed = []
    for step in (3, 2, 1, 0):
        part = paired[LINE + step].astype(jnp.bfloat16)
        if len(crossed) > 1:
            part, crossed[-2] = tie(part, crossed[-2])
        crossed.append(move(part, ACROSS))
    total = paired[3] + crossed[0].astype(jnp.float32)
    for step in (2, 1, 0):
        arrived = move(total.astype(jnp.bfloat16), ALONG)
        total = paired[step] + crossed[3 - step].astype(jnp.float32) + arrived.astype(jnp.float32)
    return total


def work_kernel(counts, piece, shard, chips_ref, rows_ref, spots_ref, meta_ref, *refs):
    occ, tiles, half, weights, keep_buf, send_buf, sem = refs[-7:]
    count, outs = counts
    sources = refs[:count]
    values, other_values = refs[count : count + 2]
    keep, send = refs[count + 2 : count + 2 + outs], refs[count + 2 + outs : count + 2 + 2 * outs]
    core = meta_ref[2]
    slot_rows = occ.shape[0] // count
    for index in range(count):
        pltpu.make_async_copy(sources[index], occ.at[pl.ds(index * slot_rows, slot_rows)], sem.at[0]).start()
    loads = [
        pltpu.make_async_copy(values, tiles.at[0], sem.at[1]),
        pltpu.make_async_copy(other_values, tiles.at[1], sem.at[2]),
    ]
    for load in loads:
        load.start()

    @pl.loop(0, half.shape[1] // BLK)
    def _(index):
        span = pl.ds(pl.multiple_of(index * BLK, BLK), BLK)
        for side in range(2):
            half[side, span, :] = jnp.zeros((BLK, LANES), jnp.float32)

    pltpu.make_async_copy(occ, occ, sem.at[0]).wait()
    slots = tiles.shape[1]
    pieces = BLK // piece
    low = lax.broadcasted_iota(jnp.int32, tiles.shape[2:], 1) < BLK
    zero = jnp.zeros(tiles.shape[2:], jnp.bfloat16)

    for side in range(2):
        loads[side].wait()

        @pl.loop(0, meta_ref[side])
        def _(group):
            products = []
            for lane in range(UNROLL):
                slot = group * UNROLL + lane
                table = side * slots + slot
                parts = [
                    occ[pl.ds(pl.multiple_of(spots_ref[table * pieces + cut], piece), piece), :]
                    for cut in range(pieces)
                ]
                pair = tiles[side, slot]
                rows = jnp.concatenate([jnp.where(low, pair, zero), jnp.where(low, zero, pair)], axis=0)
                block = jnp.concatenate(parts * 2, axis=0)
                products.append(jnp.dot(rows, block, preferred_element_type=jnp.float32))
            for lane in range(UNROLL):
                start = pl.multiple_of(rows_ref[side * slots + group * UNROLL + lane], BLK)
                for odd in range(2):
                    span = pl.ds(start + odd, BLK // 2, stride=2)
                    half[side, span, :] += products[lane][odd * (BLK // 2) : (odd + 1) * (BLK // 2)]

        weights[pl.ds(side * LANES, LANES), :] = half[side, pl.ds(0, WIN), :].T.astype(jnp.bfloat16)

    def rows_of(owner):
        span = pl.ds(pl.multiple_of(owner * shard, 32), shard)
        both = jnp.concatenate([half[side, span, :].astype(jnp.bfloat16) for side in range(2)], axis=1)
        return jnp.dot(both, weights[...], preferred_element_type=jnp.float32)

    chips = keep_buf.shape[0]
    each = chips // outs

    def give(buf, outputs, copied, turn, block):
        slot = chips - 1 - turn
        buf[slot] = block(chips_ref[slot])
        for index, out in enumerate(outputs):

            @pl.when(slot // each == index)
            def _():
                pltpu.make_async_copy(buf.at[slot], out.at[slot % each], sem.at[copied]).start()

    @pl.loop(0, chips)
    def _(turn):
        give(send_buf, send, 3, turn, lambda chip: rows_of(2 * chip + 1 - core).astype(jnp.bfloat16))

    @pl.loop(0, chips)
    def _(turn):
        give(keep_buf, keep, 4, turn, lambda chip: rows_of(2 * chip + core))

    pltpu.make_async_copy(send_buf, send_buf, sem.at[3]).wait()
    pltpu.make_async_copy(keep_buf, keep_buf, sem.at[4]).wait()


def local(block_values, block_pairs, live_counts, occupied):
    owners = lax.axis_size("aux")
    me = lax.axis_index("aux")
    core, chip = me % 2, me // 2
    shard, width = occupied.shape
    total = owners * shard
    slots = block_values.shape[0]
    piece = math.gcd(BLK, shard)
    same_core = [[2 * i + k for i in range(owners // 2)] for k in range(2)]
    swap = [(i, i ^ 1) for i in range(owners)]

    mine = lax.dynamic_slice_in_dim(occupied, core * LANES, LANES, 1)
    given = lax.dynamic_slice_in_dim(occupied, (1 - core) * LANES, LANES, 1)
    parts = (mine, move(given, swap))

    tile_sets = [
        values.reshape(slots, BLK * BLK // LANES, LANES) for values in (block_values, move(block_values, swap))
    ]

    chips = owners // 2
    slot_ids = jnp.arange(chips, dtype=jnp.int32)
    lined = chips == 2 * LINE
    if lined:
        held = spread(parts)
        chip_of_slot = (slot_ids + chip // 2) % LINE * 2 + ((slot_ids // LINE) ^ (chip % 2))
    else:
        held = [lax.all_gather(part, "aux", axis_index_groups=same_core, axis=0, tiled=True) for part in parts]
        chip_of_slot = slot_ids

    live = live_counts[0]
    tile_ids = jnp.arange(slots, dtype=jnp.int32)
    row_starts = jnp.where(tile_ids < live, block_pairs[:, 0] * BLK, total)
    groups = jnp.full((slots,), (live + UNROLL - 1) // UNROLL, jnp.int32)
    table = jnp.stack([row_starts, block_pairs[:, 1], groups])
    other_table = lax.ppermute(table, "aux", swap)

    rows = jnp.concatenate([table[0], other_table[0]])
    columns = jnp.concatenate([table[1], other_table[1]])
    first = columns[:, None] * BLK + jnp.arange(BLK // piece, dtype=jnp.int32) * piece
    owner = first // shard
    owner_chip = owner // 2
    slot_of = owner_chip
    if lined:
        slot_of = (chip // 2 - owner_chip // 2) % LINE + LINE * ((owner_chip % 2) ^ (chip % 2))
    spots = ((((owner % 2) ^ core) * chips + slot_of) * shard + first % shard).reshape(-1)
    meta = jnp.stack([table[2, 0], other_table[2, 0], core]).astype(jnp.int32)

    smem = pl.BlockSpec(memory_space=pltpu.SMEM)
    hbm = pl.BlockSpec(memory_space=pl.ANY)
    outs = chips if lined else 1
    block = (chips // outs, shard, WIN)
    results = pl.pallas_call(
        functools.partial(work_kernel, (len(held), outs), piece, shard),
        out_shape=[jax.ShapeDtypeStruct(block, jnp.float32)] * outs
        + [jax.ShapeDtypeStruct(block, jnp.bfloat16)] * outs,
        in_specs=[smem] * 4 + [hbm] * (len(held) + 2),
        out_specs=[hbm] * (2 * outs),
        scratch_shapes=[
            pltpu.VMEM((total, LANES), jnp.bfloat16),
            pltpu.VMEM((2, slots, BLK * BLK // LANES, LANES), jnp.bfloat16),
            pltpu.VMEM((2, total + BLK, LANES), jnp.float32),
            pltpu.VMEM((2 * LANES, WIN), jnp.bfloat16),
            pltpu.VMEM((chips, shard, WIN), jnp.float32),
            pltpu.VMEM((chips, shard, WIN), jnp.bfloat16),
            pltpu.SemaphoreType.DMA((5,)),
        ],
        compiler_params=pltpu.CompilerParams(vmem_limit_bytes=VMEM_BYTES),
        cost_estimate=pl.CostEstimate(
            flops=2 * total * width * (WIN + BLK), bytes_accessed=25 << 20, transcendentals=0
        ),
    )(chip_of_slot, rows, spots, meta, *held, *tile_sets)
    keep, send = results[:outs], results[outs:]

    factor = 1.0 / math.sqrt(owners * width)
    if lined:
        return collect([part[0] for part in keep], [part[0] for part in send], swap) * factor
    pair_sum = (keep[0] + move(send[0], swap).astype(jnp.float32)).astype(jnp.bfloat16)
    block_sum = lax.psum_scatter(
        pair_sum.reshape(total // 2, WIN), "aux", axis_index_groups=same_core, scatter_dimension=0, tiled=True
    )
    return block_sum.astype(jnp.float32) * factor


def solution(mesh):
    placed = (
        P(("groups", "aux"), None),
        P(("groups", "aux"), None),
        P(("groups", "aux")),
        P(("groups", "aux"), None),
    )
    return jax.shard_map(
        local, mesh=mesh, in_specs=placed, out_specs=P(("groups", "aux"), None), check_vma=False
    )
```

```python
import functools
import math

import jax
import jax.numpy as jnp
from jax import lax
from jax.experimental import pallas as pl
from jax.experimental.pallas import tpu as pltpu
from jax.sharding import PartitionSpec as P

BLK = 64
WIN = 128
LANES = 128
UNROLL = 8
LINE = 4
SCOPED_BYTES = 16 * 1024 * 1024


def place(z, x, core):
    return (z * 2 + x) * 2 + core


def pairs_of(step):
    return [
        (place(z, x, core), place(*step(z, x), core)) for z in range(LINE) for x in range(2) for core in range(2)
    ]


def tie(*arrays):
    return lax.optimization_barrier(arrays)


def move(array, pairs):
    return lax.ppermute(array, "aux", pairs)


ALONG = pairs_of(lambda z, x: ((z + 1) % LINE, x))
ACROSS = pairs_of(lambda z, x: (z, 1 - x))
ADD_AT = {}
LAY_AT = {}


def spread(parts, meanwhile):
    lines, others = [[part] for part in parts], [[] for _ in parts]

    def arrived(stage):
        held = [line[stage] for line in lines] if stage < LINE else []
        return held + ([other[stage - 1] for other in others] if stage else [])

    for step in range(LINE):
        for index, (line, other) in enumerate(zip(lines, others)):
            if other:
                line[-1], other[-1] = tie(line[-1], other[-1])
            line[-1] = meanwhile(step, index, arrived, line[-1])
            now = line[-1]
            if step + 1 < LINE:
                line.append(move(now, ALONG))
            other.append(move(now, ACROSS))
    return [arrived(stage) for stage in range(LINE + 1)]


def collect(keep, send, swap):
    order = [LINE + 3, LINE + 2, 3, LINE + 1, 2, LINE, 1, 0]
    paired = {}
    for slot in order:
        paired[slot] = keep[slot] + move(send[slot], swap).astype(jnp.float32)
    crossed = []
    for step in (3, 2, 1, 0):
        part = paired[LINE + step].astype(jnp.bfloat16)
        if len(crossed) > 1:
            part, crossed[-2] = tie(part, crossed[-2])
        crossed.append(move(part, ACROSS))
    total = paired[3] + crossed[0].astype(jnp.float32)
    for step in (2, 1, 0):
        arrived = move(total.astype(jnp.bfloat16), ALONG)
        total = paired[step] + crossed[3 - step].astype(jnp.float32) + arrived.astype(jnp.float32)
    return total


def add_tiles(stage, pieces, table_ref, bounds_ref, sources, tile_sets, half, occ, sem):
    rows = sources[0].shape[0]
    for index, source in enumerate(sources):
        pltpu.make_async_copy(source, occ.at[pl.ds(index * rows, rows)], sem).start()
    pltpu.make_async_copy(occ, occ, sem).wait()
    begin, end = bounds_ref[stage], bounds_ref[stage + 1]
    slots, depth, lanes = tile_sets[0].shape
    low = lax.broadcasted_iota(jnp.int32, (depth, lanes), 1) < BLK
    zero = jnp.zeros((depth, lanes), jnp.bfloat16)
    spill = half.shape[0] - BLK
    columns = 2 + pieces
    piece = BLK // pieces

    @pl.loop(0, (end - begin + UNROLL - 1) // UNROLL)
    def _(group):
        products, starts = [], []
        for lane in range(UNROLL):
            entry = begin + group * UNROLL + lane
            tile = table_ref[entry * columns]
            starts.append(jnp.where(entry < end, table_ref[entry * columns + 1], spill))
            spots = [jnp.where(entry < end, table_ref[entry * columns + 2 + cut], 0) for cut in range(pieces)]
            parts = [occ[pl.ds(pl.multiple_of(spot, piece), piece), :] for spot in spots]
            slot = lax.rem(tile, slots)
            pair = jnp.where(tile < slots, tile_sets[0][slot], tile_sets[1][slot])
            left = jnp.concatenate([jnp.where(low, pair, zero), jnp.where(low, zero, pair)], axis=0)
            block = jnp.concatenate(parts * 2, axis=0)
            products.append(jnp.dot(left, block, preferred_element_type=jnp.float32))
        for product, start in zip(products, starts):
            start = pl.multiple_of(start, BLK)
            for odd in range(2):
                span = pl.ds(start + odd, BLK // 2, stride=2)
                half[span, :] += product[odd * (BLK // 2) : (odd + 1) * (BLK // 2)]


def fill_window(half, weights, shard, chips_ref, first, parity, out):
    side_rows = (half.shape[0] - BLK) // 2
    chunk = math.gcd(shard, 256)
    chunks = shard // chunk

    @pl.loop(0, out.shape[0] * chunks)
    def _(turn):
        index, part = turn // chunks, lax.rem(turn, chunks) * chunk
        start = pl.multiple_of((2 * chips_ref[first + index] + parity) * shard + part, 32)
        both = jnp.concatenate(
            [half[pl.ds(side * side_rows + start, chunk), :].astype(jnp.bfloat16) for side in range(2)], axis=1
        )
        product = jnp.dot(both, weights[...], preferred_element_type=jnp.float32)
        out[index, pl.ds(pl.multiple_of(part, 32), chunk), :] = product.astype(out.dtype)


def stage_kernel(stage, count, pieces, table_ref, bounds_ref, *refs):
    sources, tile_sets = refs[:count], refs[count : count + 2]
    half, occ, sem = refs[-3:]
    if stage == 0:

        @pl.loop(0, half.shape[0] // BLK)
        def _(index):
            half[pl.ds(pl.multiple_of(index * BLK, BLK), BLK), :] = jnp.zeros((BLK, LANES), jnp.float32)

    add_tiles(stage, pieces, table_ref, bounds_ref, sources, tile_sets, half, occ, sem)


def window_kernel(stage, count, pieces, shard, first, table_ref, bounds_ref, chips_ref, core_ref, *refs):
    sources, tile_sets = refs[:count], refs[count : count + 2]
    half, weights = refs[count + 3 : count + 5]
    outs = refs[count + 5 : -2]
    occ, sem = refs[-2:]
    add_tiles(stage, pieces, table_ref, bounds_ref, sources, tile_sets, half, occ, sem)
    side_rows = (half.shape[0] - BLK) // 2
    for side in range(2):
        weights[pl.ds(side * LANES, LANES), :] = half[pl.ds(side * side_rows, WIN), :].T.astype(jnp.bfloat16)
    for index, out in enumerate(outs):
        fill_window(half, weights, shard, chips_ref, first + index * out.shape[0], 1 - core_ref[0], out)


def rest_kernel(shard, plan, chips_ref, core_ref, half, weights, *outs):
    for (first, keeps), out in zip(plan, outs):
        parity = core_ref[0] if keeps else 1 - core_ref[0]
        fill_window(half, weights, shard, chips_ref, first, parity, out)


SMEM = pl.BlockSpec(memory_space=pltpu.SMEM)
HBM = pl.BlockSpec(memory_space=pl.ANY)
VMEM = pl.BlockSpec(memory_space=pltpu.VMEM)


def pinned(array):
    return pltpu.with_memory_space_constraint(array, pltpu.VMEM)


def call(kernel, ins, in_specs, outs, scratch, aliases, flops):
    return pl.pallas_call(
        kernel,
        out_shape=outs,
        in_specs=in_specs,
        out_specs=[VMEM] * len(outs),
        scratch_shapes=scratch,
        input_output_aliases=aliases,
        compiler_params=pltpu.CompilerParams(vmem_limit_bytes=SCOPED_BYTES),
        cost_estimate=pl.CostEstimate(flops=flops, bytes_accessed=4 << 20, transcendentals=0),
    )(*ins)


def local(block_values, block_pairs, live_counts, occupied):
    owners = lax.axis_size("aux")
    me = lax.axis_index("aux")
    core, chip = me % 2, me // 2
    shard, width = occupied.shape
    total = owners * shard
    slots = block_values.shape[0]
    piece = math.gcd(BLK, shard)
    pieces = BLK // piece
    chips = owners // 2
    lined = chips == 2 * LINE
    same_core = [[2 * i + k for i in range(chips)] for k in range(2)]
    swap = [(i, i ^ 1) for i in range(owners)]

    mine = lax.dynamic_slice_in_dim(occupied, core * LANES, LANES, 1)
    given = lax.dynamic_slice_in_dim(occupied, (1 - core) * LANES, LANES, 1)
    parts = (mine, move(given, swap))
    tile_sets = [
        values.reshape(slots, BLK * BLK // LANES, LANES) for values in (block_values, move(block_values, swap))
    ]

    slot_ids = jnp.arange(chips, dtype=jnp.int32)
    chip_of_slot = slot_ids
    stage_count = 1
    if lined:
        chip_of_slot = (slot_ids + chip // 2) % LINE * 2 + ((slot_ids // LINE) ^ (chip % 2))
        stage_count = LINE + 1

    tile_ids = jnp.arange(2 * slots, dtype=jnp.int32)
    row_starts = jnp.where(tile_ids[:slots] < live_counts[0], block_pairs[:, 0] * BLK, -1)
    table = jnp.stack([row_starts, block_pairs[:, 1]])
    both = jnp.concatenate([table, move(table, swap)], axis=1)
    first = both[1][:, None] * BLK + jnp.arange(pieces, dtype=jnp.int32) * piece
    owner = first // shard
    part = (owner % 2) ^ core
    owner_chip = owner // 2
    if lined:
        back = (chip // 2 - owner_chip // 2) % LINE
        side = (owner_chip % 2) ^ (chip % 2)
        stage = (back + side)[:, 0]
        slot_of = part + 2 * jnp.where(back + side < LINE, side, 0)
    else:
        stage = jnp.zeros_like(tile_ids)
        slot_of = part * chips + owner_chip
    spots = slot_of * shard + first % shard
    stage = jnp.where(both[0] >= 0, stage, stage_count)
    rows = both[0] + tile_ids // slots * total
    ahead = (stage[None, :] < stage[:, None]) | (
        (stage[None, :] == stage[:, None]) & (tile_ids[None, :] < tile_ids[:, None])
    )
    rank = jnp.sum(ahead.astype(jnp.int32), axis=1)
    entries = jnp.arange(2 * slots + UNROLL, dtype=jnp.int32)
    chosen = rank[None, :] == entries[:, None]
    columns = [tile_ids, rows] + [spots[:, cut] for cut in range(pieces)]
    ordered = jnp.stack(
        [jnp.sum(jnp.where(chosen, column[None, :], 0), axis=1) for column in columns], axis=1
    ).reshape(-1)
    bounds = jnp.sum((stage[None, :] < jnp.arange(stage_count + 1)[:, None]).astype(jnp.int32), axis=1)
    cores = core.astype(jnp.int32).reshape(1)

    half_type = pltpu.VMEM((2 * total + BLK, LANES), jnp.float32)
    work = 4 * slots * BLK * BLK * LANES // stage_count
    halves = []

    def stage_ins(sources):
        scratch = [
            pltpu.VMEM((len(sources) * sources[0].shape[0], LANES), jnp.bfloat16),
            pltpu.SemaphoreType.DMA,
        ]
        return [*sources, *map(pinned, tile_sets)], [HBM] * len(sources) + [VMEM] * 2, scratch

    def add_stage(stage, sources):
        ins, specs, scratch = stage_ins(sources)
        ins, specs = [ordered, bounds] + ins, [SMEM] * 2 + specs
        aliases = {}
        if halves:
            aliases = {len(ins): 0}
            ins, specs = ins + [pinned(halves[-1])], specs + [VMEM]
        halves.extend(
            call(
                functools.partial(stage_kernel, stage, len(sources), pieces),
                ins, specs, [half_type], scratch, aliases, work,
            )
        )

    def meanwhile(step, index, arrived, moved):
        if (step, index) in LAY_AT:
            which = LAY_AT[step, index]
            moved, tile_sets[which] = tie(moved, tile_sets[which])
        if (step, index) in ADD_AT:
            stage = ADD_AT[step, index]
            add_stage(stage, arrived(stage))
            moved, halves[-1] = tie(moved, halves[-1])
        return moved

    if lined:
        stages = spread(parts, meanwhile)
        for stage in range(len(ADD_AT), LINE):
            add_stage(stage, stages[stage])
    else:
        stages = [[lax.all_gather(part, "aux", axis_index_groups=same_core, axis=0, tiled=True) for part in parts]]
        halves.extend(call(clear_kernel, [], [], [half_type], [], {}, 0))

    group = 1 if lined else chips // 2
    far = [group] * (chips // 2 // group)
    ins, specs, scratch = stage_ins(stages[-1])
    ins = [ordered, bounds, chip_of_slot, cores] + ins + [pinned(halves[-1])]
    half, weights, *far_send = call(
        functools.partial(window_kernel, stage_count - 1, len(stages[-1]), pieces, shard, chips // 2),
        ins,
        [SMEM] * 4 + specs + [VMEM],
        [half_type, pltpu.VMEM((2 * LANES, WIN), jnp.bfloat16)]
        + [pltpu.VMEM((size, shard, WIN), jnp.bfloat16) for size in far],
        scratch,
        {len(ins) - 1: 0},
        work + total // 4 * width * WIN * 2,
    )

    def rest(plan):
        return call(
            functools.partial(rest_kernel, shard, plan),
            [chip_of_slot, cores, pinned(half), pinned(weights)],
            [SMEM] * 2 + [VMEM] * 2,
            [pltpu.VMEM((group, shard, WIN), jnp.float32 if keeps else jnp.bfloat16) for _, keeps in plan],
            [],
            {},
            total // 4 * width * WIN * 2,
        )

    far_keep = rest([(chips // 2 + index * group, True) for index in range(len(far))])
    near = rest([(index * group, keeps) for keeps in (False, True) for index in range(len(far))])
    near_send, near_keep = near[: len(far)], near[len(far) :]

    factor = 1.0 / math.sqrt(owners * width)
    keep, send = [*near_keep, *far_keep], [*near_send, *far_send]
    if lined:
        return collect([block[0] for block in keep], [block[0] for block in send], swap) * factor
    keep, send = jnp.concatenate(keep), jnp.concatenate(send)
    pair_sum = (keep + move(send, swap).astype(jnp.float32)).astype(jnp.bfloat16)
    block_sum = lax.psum_scatter(
        pair_sum.reshape(total // 2, WIN), "aux", axis_index_groups=same_core, scatter_dimension=0, tiled=True
    )
    return block_sum.astype(jnp.float32) * factor


def clear_kernel(half):
    @pl.loop(0, half.shape[0] // BLK)
    def _(index):
        half[pl.ds(pl.multiple_of(index * BLK, BLK), BLK), :] = jnp.zeros((BLK, LANES), jnp.float32)


def solution(mesh):
    placed = (
        P(("groups", "aux"), None),
        P(("groups", "aux"), None),
        P(("groups", "aux")),
        P(("groups", "aux"), None),
    )
    return jax.shard_map(
        local, mesh=mesh, in_specs=placed, out_specs=P(("groups", "aux"), None), check_vma=False
    )
```

```python
import functools
import math

import jax
import jax.numpy as jnp
from jax import lax
from jax.experimental import pallas as pl
from jax.experimental.pallas import tpu as pltpu
from jax.sharding import PartitionSpec as P

BLK = 64
WIN = 128
LANES = 128
UNROLL = 8
LINE = 4
SCOPED_BYTES = 16 * 1024 * 1024


def place(z, x, core):
    return (z * 2 + x) * 2 + core


def pairs_of(step):
    return [
        (place(z, x, core), place(*step(z, x), core)) for z in range(LINE) for x in range(2) for core in range(2)
    ]


def tie(*arrays):
    return lax.optimization_barrier(arrays)


def move(array, pairs):
    return lax.ppermute(array, "aux", pairs)


ALONG = pairs_of(lambda z, x: ((z + 1) % LINE, x))
ACROSS = pairs_of(lambda z, x: (z, 1 - x))
ADD_AT = {(2, 1): 0, (3, 1): 1}
CLEAR_AT = (1, 1)


def spread(parts, meanwhile):
    lines, others = [[part] for part in parts], [[] for _ in parts]

    def arrived(stage):
        held = [line[stage] for line in lines] if stage < LINE else []
        return held + ([other[stage - 1] for other in others] if stage else [])

    for step in range(LINE):
        for index, (line, other) in enumerate(zip(lines, others)):
            if other:
                line[-1], other[-1] = tie(line[-1], other[-1])
            line[-1] = meanwhile(step, index, arrived, line[-1])
            now = line[-1]
            if step + 1 < LINE:
                line.append(move(now, ALONG))
            other.append(move(now, ACROSS))
    return [arrived(stage) for stage in range(LINE + 1)]


def collect(far_keep, far_send, near_of, half, swap):
    def paired(keep, send):
        return keep + move(send, swap).astype(jnp.float32)

    steps = range(LINE - 1, -1, -1)
    parts = {step: paired(far_keep[step], far_send[step]).astype(jnp.bfloat16) for step in steps}
    half, parts[3], parts[2] = tie(half, parts[3], parts[2])
    crossed = []
    for step in steps:
        part = parts[step]
        if len(crossed) > 1:
            part, crossed[-2] = tie(part, crossed[-2])
        crossed.append(move(part, ACROSS))
    near_keep, near_send = near_of(half)
    total = paired(near_keep[3], near_send[3]) + crossed[0].astype(jnp.float32)
    for step in (2, 1, 0):
        arrived = move(total.astype(jnp.bfloat16), ALONG)
        total = paired(near_keep[step], near_send[step]) + crossed[3 - step].astype(jnp.float32)
        total = total + arrived.astype(jnp.float32)
    return total


def add_tiles(stage, pieces, table_ref, bounds_ref, sources, tile_sets, half, occ, sem):
    rows = sources[0].shape[0]
    for index, source in enumerate(sources):
        pltpu.make_async_copy(source, occ.at[pl.ds(index * rows, rows)], sem).start()
    pltpu.make_async_copy(occ, occ, sem).wait()
    begin, end = bounds_ref[stage], bounds_ref[stage + 1]
    slots, depth, lanes = tile_sets[0].shape
    low = lax.broadcasted_iota(jnp.int32, (depth, lanes), 1) < BLK
    zero = jnp.zeros((depth, lanes), jnp.bfloat16)
    spill = half.shape[0] - BLK
    columns = 2 + pieces
    piece = BLK // pieces

    @pl.loop(0, (end - begin + UNROLL - 1) // UNROLL)
    def _(group):
        products, starts = [], []
        for lane in range(UNROLL):
            entry = begin + group * UNROLL + lane
            tile = table_ref[entry * columns]
            starts.append(jnp.where(entry < end, table_ref[entry * columns + 1], spill))
            spots = [jnp.where(entry < end, table_ref[entry * columns + 2 + cut], 0) for cut in range(pieces)]
            parts = [occ[pl.ds(pl.multiple_of(spot, piece), piece), :] for spot in spots]
            slot = lax.rem(tile, slots)
            pair = jnp.where(tile < slots, tile_sets[0][slot], tile_sets[1][slot])
            left = jnp.concatenate([jnp.where(low, pair, zero), jnp.where(low, zero, pair)], axis=0)
            block = jnp.concatenate(parts * 2, axis=0)
            products.append(jnp.dot(left, block, preferred_element_type=jnp.float32))
        for product, start in zip(products, starts):
            start = pl.multiple_of(start, BLK)
            for odd in range(2):
                span = pl.ds(start + odd, BLK // 2, stride=2)
                half[span, :] += product[odd * (BLK // 2) : (odd + 1) * (BLK // 2)]


def fill_window(half, weights, shard, chips_ref, first, parity, out):
    side_rows = (half.shape[0] - BLK) // 2

    @pl.loop(0, out.shape[0])
    def _(index):
        start = pl.multiple_of((2 * chips_ref[first + index] + parity) * shard, 32)
        both = jnp.concatenate(
            [half[pl.ds(side * side_rows + start, shard), :].astype(jnp.bfloat16) for side in range(2)], axis=1
        )
        out[index] = jnp.dot(both, weights[...], preferred_element_type=jnp.float32).astype(out.dtype)


def stage_kernel(stage, count, pieces, table_ref, bounds_ref, *refs):
    sources, tile_sets = refs[:count], refs[count : count + 2]
    half, occ, sem = refs[-3:]
    add_tiles(stage, pieces, table_ref, bounds_ref, sources, tile_sets, half, occ, sem)


def window_kernel(stage, count, pieces, shard, first, table_ref, bounds_ref, chips_ref, core_ref, *refs):
    sources, tile_sets = refs[:count], refs[count : count + 2]
    half, weights = refs[count + 3 : count + 5]
    outs = refs[count + 5 : -2]
    occ, sem = refs[-2:]
    add_tiles(stage, pieces, table_ref, bounds_ref, sources, tile_sets, half, occ, sem)
    side_rows = (half.shape[0] - BLK) // 2
    for side in range(2):
        weights[pl.ds(side * LANES, LANES), :] = half[pl.ds(side * side_rows, WIN), :].T.astype(jnp.bfloat16)
    for index, out in enumerate(outs):
        fill_window(half, weights, shard, chips_ref, first + index * out.shape[0], 1 - core_ref[0], out)


def rest_kernel(shard, plan, chips_ref, core_ref, half, weights, *outs):
    for (first, keeps), out in zip(plan, outs):
        parity = core_ref[0] if keeps else 1 - core_ref[0]
        fill_window(half, weights, shard, chips_ref, first, parity, out)


SMEM = pl.BlockSpec(memory_space=pltpu.SMEM)
HBM = pl.BlockSpec(memory_space=pl.ANY)
VMEM = pl.BlockSpec(memory_space=pltpu.VMEM)


def pinned(array):
    return pltpu.with_memory_space_constraint(array, pltpu.VMEM)


def call(kernel, ins, in_specs, outs, scratch, aliases, flops):
    return pl.pallas_call(
        kernel,
        out_shape=outs,
        in_specs=in_specs,
        out_specs=[VMEM] * len(outs),
        scratch_shapes=scratch,
        input_output_aliases=aliases,
        compiler_params=pltpu.CompilerParams(vmem_limit_bytes=SCOPED_BYTES),
        cost_estimate=pl.CostEstimate(flops=flops, bytes_accessed=4 << 20, transcendentals=0),
    )(*ins)


def local(block_values, block_pairs, live_counts, occupied):
    owners = lax.axis_size("aux")
    me = lax.axis_index("aux")
    core, chip = me % 2, me // 2
    shard, width = occupied.shape
    total = owners * shard
    slots = block_values.shape[0]
    piece = math.gcd(BLK, shard)
    pieces = BLK // piece
    chips = owners // 2
    lined = chips == 2 * LINE
    same_core = [[2 * i + k for i in range(chips)] for k in range(2)]
    swap = [(i, i ^ 1) for i in range(owners)]

    mine = lax.dynamic_slice_in_dim(occupied, core * LANES, LANES, 1)
    given = lax.dynamic_slice_in_dim(occupied, (1 - core) * LANES, LANES, 1)
    parts = (mine, move(given, swap))
    tile_sets = [
        values.reshape(slots, BLK * BLK // LANES, LANES) for values in (block_values, move(block_values, swap))
    ]

    slot_ids = jnp.arange(chips, dtype=jnp.int32)
    chip_of_slot = slot_ids
    stage_count = 1
    if lined:
        chip_of_slot = (slot_ids + chip // 2) % LINE * 2 + ((slot_ids // LINE) ^ (chip % 2))
        stage_count = LINE + 1

    tile_ids = jnp.arange(2 * slots, dtype=jnp.int32)
    row_starts = jnp.where(tile_ids[:slots] < live_counts[0], block_pairs[:, 0] * BLK, -1)
    table = jnp.stack([row_starts, block_pairs[:, 1]])
    both = jnp.concatenate([table, move(table, swap)], axis=1)
    first = both[1][:, None] * BLK + jnp.arange(pieces, dtype=jnp.int32) * piece
    owner = first // shard
    part = (owner % 2) ^ core
    owner_chip = owner // 2
    if lined:
        back = (chip // 2 - owner_chip // 2) % LINE
        side = (owner_chip % 2) ^ (chip % 2)
        stage = (back + side)[:, 0]
        slot_of = part + 2 * jnp.where(back + side < LINE, side, 0)
    else:
        stage = jnp.zeros_like(tile_ids)
        slot_of = part * chips + owner_chip
    spots = slot_of * shard + first % shard
    stage = jnp.where(both[0] >= 0, stage, stage_count)
    rows = both[0] + tile_ids // slots * total
    ahead = (stage[None, :] < stage[:, None]) | (
        (stage[None, :] == stage[:, None]) & (tile_ids[None, :] < tile_ids[:, None])
    )
    rank = jnp.sum(ahead.astype(jnp.int32), axis=1)
    entries = jnp.arange(2 * slots + UNROLL, dtype=jnp.int32)
    chosen = rank[None, :] == entries[:, None]
    columns = [tile_ids, rows] + [spots[:, cut] for cut in range(pieces)]
    ordered = jnp.stack(
        [jnp.sum(jnp.where(chosen, column[None, :], 0), axis=1) for column in columns], axis=1
    ).reshape(-1)
    bounds = jnp.sum((stage[None, :] < jnp.arange(stage_count + 1)[:, None]).astype(jnp.int32), axis=1)
    cores = core.astype(jnp.int32).reshape(1)

    half_type = pltpu.VMEM((2 * total + BLK, LANES), jnp.float32)
    work = 4 * slots * BLK * BLK * LANES // stage_count
    halves = list(call(clear_kernel, [], [], [half_type], [], {}, 0))

    def stage_ins(sources):
        scratch = [
            pltpu.VMEM((len(sources) * sources[0].shape[0], LANES), jnp.bfloat16),
            pltpu.SemaphoreType.DMA,
        ]
        return [*sources, *map(pinned, tile_sets)], [HBM] * len(sources) + [VMEM] * 2, scratch

    def add_stage(stage, sources):
        ins, specs, scratch = stage_ins(sources)
        ins = [ordered, bounds] + ins + [pinned(halves[-1])]
        halves.extend(
            call(
                functools.partial(stage_kernel, stage, len(sources), pieces),
                ins, [SMEM] * 2 + specs + [VMEM], [half_type], scratch, {len(ins) - 1: 0}, work,
            )
        )

    def meanwhile(step, index, arrived, moved):
        if (step, index) == CLEAR_AT:
            moved, halves[-1] = tie(moved, halves[-1])
        if (step, index) in ADD_AT:
            stage = ADD_AT[step, index]
            add_stage(stage, arrived(stage))
            moved, halves[-1] = tie(moved, halves[-1])
        return moved

    if lined:
        stages = spread(parts, meanwhile)
        for stage in range(len(ADD_AT), LINE):
            add_stage(stage, stages[stage])
    else:
        stages = [[lax.all_gather(part, "aux", axis_index_groups=same_core, axis=0, tiled=True) for part in parts]]

    group = 1 if lined else chips // 2
    far = [group] * (chips // 2 // group)
    ins, specs, scratch = stage_ins(stages[-1])
    ins = [ordered, bounds, chip_of_slot, cores] + ins + [pinned(halves[-1])]
    half, weights, *far_send = call(
        functools.partial(window_kernel, stage_count - 1, len(stages[-1]), pieces, shard, chips // 2),
        ins,
        [SMEM] * 4 + specs + [VMEM],
        [half_type, pltpu.VMEM((2 * LANES, WIN), jnp.bfloat16)]
        + [pltpu.VMEM((size, shard, WIN), jnp.bfloat16) for size in far],
        scratch,
        {len(ins) - 1: 0},
        work + total // 4 * width * WIN * 2,
    )

    def rest(plan, half):
        return call(
            functools.partial(rest_kernel, shard, plan),
            [chip_of_slot, cores, pinned(half), pinned(weights)],
            [SMEM] * 2 + [VMEM] * 2,
            [pltpu.VMEM((group, shard, WIN), jnp.float32 if keeps else jnp.bfloat16) for _, keeps in plan],
            [],
            {},
            total // 4 * width * WIN * 2,
        )

    def near_of(half):
        blocks = rest([(index * group, keeps) for keeps in (True, False) for index in range(len(far))], half)
        if lined:
            blocks = [block[0] for block in blocks]
        return blocks[: len(far)], blocks[len(far) :]

    far_keep = rest([(chips // 2 + index * group, True) for index in range(len(far))], half)

    factor = 1.0 / math.sqrt(owners * width)
    if lined:
        far_keep, far_send = [block[0] for block in far_keep], [block[0] for block in far_send]
        return collect(far_keep, far_send, near_of, half, swap) * factor
    near_keep, near_send = near_of(half)
    keep, send = [*near_keep, *far_keep], [*near_send, *far_send]
    keep, send = jnp.concatenate(keep), jnp.concatenate(send)
    pair_sum = (keep + move(send, swap).astype(jnp.float32)).astype(jnp.bfloat16)
    block_sum = lax.psum_scatter(
        pair_sum.reshape(total // 2, WIN), "aux", axis_index_groups=same_core, scatter_dimension=0, tiled=True
    )
    return block_sum.astype(jnp.float32) * factor


def clear_kernel(half):
    @pl.loop(0, half.shape[0] // BLK)
    def _(index):
        half[pl.ds(pl.multiple_of(index * BLK, BLK), BLK), :] = jnp.zeros((BLK, LANES), jnp.float32)


def solution(mesh):
    placed = (
        P(("groups", "aux"), None),
        P(("groups", "aux"), None),
        P(("groups", "aux")),
        P(("groups", "aux"), None),
    )
    return jax.shard_map(
        local, mesh=mesh, in_specs=placed, out_specs=P(("groups", "aux"), None), check_vma=False
    )
```

```python
import functools
import math

import jax
import jax.numpy as jnp
from jax import lax
from jax.experimental import pallas as pl
from jax.experimental.pallas import tpu as pltpu
from jax.sharding import PartitionSpec as P

BLK = 64
WIN = 128
LANES = 128
UNROLL = 8
LINE = 4
SCOPED_BYTES = 16 * 1024 * 1024


def place(z, x, core):
    return (z * 2 + x) * 2 + core


def pairs_of(step):
    return [
        (place(z, x, core), place(*step(z, x), core)) for z in range(LINE) for x in range(2) for core in range(2)
    ]


def tie(*arrays):
    return lax.optimization_barrier(arrays)


def move(array, pairs):
    return lax.ppermute(array, "aux", pairs)


ALONG = pairs_of(lambda z, x: ((z + 1) % LINE, x))
BACK = pairs_of(lambda z, x: ((z - 1) % LINE, x))
ACROSS = pairs_of(lambda z, x: (z, 1 - x))
ADD_AT = {(3, 1): 0}
LAY_AT = (2, 1)


def spread(parts, meanwhile):
    lines, others = [[part] for part in parts], [[] for _ in parts]

    def arrived(stage):
        held = [line[stage] for line in lines] if stage < LINE else []
        return held + ([other[stage - 1] for other in others] if stage else [])

    for step in range(LINE):
        for index, (line, other) in enumerate(zip(lines, others)):
            if other:
                line[-1], other[-1] = tie(line[-1], other[-1])
            line[-1] = meanwhile(step, index, arrived, line[-1])
            now = line[-1]
            if step + 1 < LINE:
                line.append(move(now, ALONG))
            other.append(move(now, ACROSS))
    return [arrived(stage) for stage in range(LINE + 1)]


def collect(far_keep, far_send, near_of, half, swap):
    def paired(keep, send):
        return keep + move(send, swap).astype(jnp.float32)

    order = (2, 1, 3, 0)
    parts = {step: paired(far_keep[step], far_send[step]).astype(jnp.bfloat16) for step in order}
    half, parts[2] = tie(half, parts[2])
    crossed = {2: move(parts[2], ACROSS)}
    near_keep, near_send = near_of(half)
    total = {step: paired(near_keep[step], near_send[step]) for step in order}
    parts[1], total[2] = tie(parts[1], total[2])
    crossed[1] = move(parts[1], ACROSS)
    parts[3], crossed[2] = tie(parts[3], crossed[2])
    crossed[3] = move(parts[3], ACROSS)
    parts[0], crossed[1] = tie(parts[0], crossed[1])
    crossed[0] = move(parts[0], ACROSS)

    total = {step: total[step] + crossed[step].astype(jnp.float32) for step in order}
    two_on = move(total[2].astype(jnp.bfloat16), ALONG)
    one_on = move((total[1] + two_on.astype(jnp.float32)).astype(jnp.bfloat16), ALONG)
    one_back = move(total[3].astype(jnp.bfloat16), BACK)
    return total[0] + one_on.astype(jnp.float32) + one_back.astype(jnp.float32)


def clear(half):
    whole = half.shape[0] // (4 * BLK) * (4 * BLK)

    @pl.loop(0, whole // (4 * BLK))
    def _(index):
        half[pl.ds(pl.multiple_of(index * 4 * BLK, BLK), 4 * BLK), :] = jnp.zeros((4 * BLK, LANES), jnp.float32)

    half[pl.ds(whole, half.shape[0] - whole), :] = jnp.zeros((half.shape[0] - whole, LANES), jnp.float32)


def add_tiles(stage, pieces, table_ref, bounds_ref, sources, tile_sets, half, occ, sem):
    rows = sources[0].shape[0]
    for index, source in enumerate(sources):
        pltpu.make_async_copy(source, occ.at[pl.ds(index * rows, rows)], sem).start()
    pltpu.make_async_copy(occ, occ, sem).wait()
    begin, end = bounds_ref[stage], bounds_ref[stage + 1]
    slots, depth, lanes = tile_sets[0].shape
    low = lax.broadcasted_iota(jnp.int32, (depth, lanes), 1) < BLK
    zero = jnp.zeros((depth, lanes), jnp.bfloat16)
    spill = half.shape[0] - BLK
    columns = 2 + pieces
    piece = BLK // pieces

    @pl.loop(0, (end - begin + UNROLL - 1) // UNROLL)
    def _(group):
        products, starts = [], []
        for lane in range(UNROLL):
            entry = begin + group * UNROLL + lane
            tile = table_ref[entry * columns]
            starts.append(jnp.where(entry < end, table_ref[entry * columns + 1], spill))
            spots = [jnp.where(entry < end, table_ref[entry * columns + 2 + cut], 0) for cut in range(pieces)]
            parts = [occ[pl.ds(pl.multiple_of(spot, piece), piece), :] for spot in spots]
            slot = lax.rem(tile, slots)
            pair = jnp.where(tile < slots, tile_sets[0][slot], tile_sets[1][slot])
            left = jnp.concatenate([jnp.where(low, pair, zero), jnp.where(low, zero, pair)], axis=0)
            block = jnp.concatenate(parts * 2, axis=0)
            products.append(jnp.dot(left, block, preferred_element_type=jnp.float32))
        for product, start in zip(products, starts):
            start = pl.multiple_of(start, BLK)
            for odd in range(2):
                span = pl.ds(start + odd, BLK // 2, stride=2)
                half[span, :] += product[odd * (BLK // 2) : (odd + 1) * (BLK // 2)]


def fill_window(half, weights, shard, chips_ref, first, parity, out):
    side_rows = (half.shape[0] - BLK) // 2

    @pl.loop(0, out.shape[0])
    def _(index):
        start = pl.multiple_of((2 * chips_ref[first + index] + parity) * shard, 32)
        both = jnp.concatenate(
            [half[pl.ds(side * side_rows + start, shard), :].astype(jnp.bfloat16) for side in range(2)], axis=1
        )
        out[index] = jnp.dot(both, weights[...], preferred_element_type=jnp.float32).astype(out.dtype)


def stage_kernel(stage, count, pieces, table_ref, bounds_ref, *refs):
    sources, tile_sets = refs[:count], refs[count : count + 2]
    half, occ, sem = refs[-3:]
    if stage == 0:
        clear(half)
    add_tiles(stage, pieces, table_ref, bounds_ref, sources, tile_sets, half, occ, sem)


def window_kernel(stage, count, pieces, shard, first, table_ref, bounds_ref, chips_ref, core_ref, *refs):
    sources, tile_sets = refs[:count], refs[count : count + 2]
    before = 1 if stage else 0
    half, weights = refs[count + 2 + before : count + 4 + before]
    outs = refs[count + 4 + before : -2]
    occ, sem = refs[-2:]
    if stage == 0:
        clear(half)
    add_tiles(stage, pieces, table_ref, bounds_ref, sources, tile_sets, half, occ, sem)
    side_rows = (half.shape[0] - BLK) // 2
    for side in range(2):
        weights[pl.ds(side * LANES, LANES), :] = half[pl.ds(side * side_rows, WIN), :].T.astype(jnp.bfloat16)
    for index, out in enumerate(outs):
        fill_window(half, weights, shard, chips_ref, first + index * out.shape[0], 1 - core_ref[0], out)


def rest_kernel(shard, plan, chips_ref, core_ref, half, weights, *outs):
    for (first, keeps), out in zip(plan, outs):
        parity = core_ref[0] if keeps else 1 - core_ref[0]
        fill_window(half, weights, shard, chips_ref, first, parity, out)


SMEM = pl.BlockSpec(memory_space=pltpu.SMEM)
HBM = pl.BlockSpec(memory_space=pl.ANY)
VMEM = pl.BlockSpec(memory_space=pltpu.VMEM)


def pinned(array):
    return pltpu.with_memory_space_constraint(array, pltpu.VMEM)


def call(kernel, ins, in_specs, outs, scratch, aliases, flops):
    return pl.pallas_call(
        kernel,
        out_shape=outs,
        in_specs=in_specs,
        out_specs=[VMEM] * len(outs),
        scratch_shapes=scratch,
        input_output_aliases=aliases,
        compiler_params=pltpu.CompilerParams(vmem_limit_bytes=SCOPED_BYTES),
        cost_estimate=pl.CostEstimate(flops=flops, bytes_accessed=4 << 20, transcendentals=0),
    )(*ins)


def local(block_values, block_pairs, live_counts, occupied):
    owners = lax.axis_size("aux")
    me = lax.axis_index("aux")
    core, chip = me % 2, me // 2
    shard, width = occupied.shape
    total = owners * shard
    slots = block_values.shape[0]
    piece = math.gcd(BLK, shard)
    pieces = BLK // piece
    chips = owners // 2
    lined = chips == 2 * LINE
    same_core = [[2 * i + k for i in range(chips)] for k in range(2)]
    swap = [(i, i ^ 1) for i in range(owners)]

    mine = lax.dynamic_slice_in_dim(occupied, core * LANES, LANES, 1)
    given = lax.dynamic_slice_in_dim(occupied, (1 - core) * LANES, LANES, 1)
    parts = (mine, move(given, swap))
    tile_sets = [
        values.reshape(slots, BLK * BLK // LANES, LANES) for values in (block_values, move(block_values, swap))
    ]

    slot_ids = jnp.arange(chips, dtype=jnp.int32)
    chip_of_slot = slot_ids
    stage_count = 1
    if lined:
        chip_of_slot = (slot_ids + chip // 2) % LINE * 2 + ((slot_ids // LINE) ^ (chip % 2))
        stage_count = LINE + 1

    tile_ids = jnp.arange(2 * slots, dtype=jnp.int32)
    row_starts = jnp.where(tile_ids[:slots] < live_counts[0], block_pairs[:, 0] * BLK, -1)
    table = jnp.stack([row_starts, block_pairs[:, 1]])
    both = jnp.concatenate([table, move(table, swap)], axis=1)
    first = both[1][:, None] * BLK + jnp.arange(pieces, dtype=jnp.int32) * piece
    owner = first // shard
    part = (owner % 2) ^ core
    owner_chip = owner // 2
    if lined:
        back = (chip // 2 - owner_chip // 2) % LINE
        side = (owner_chip % 2) ^ (chip % 2)
        stage = (back + side)[:, 0]
        slot_of = part + 2 * jnp.where(back + side < LINE, side, 0)
    else:
        stage = jnp.zeros_like(tile_ids)
        slot_of = part * chips + owner_chip
    spots = slot_of * shard + first % shard
    stage = jnp.where(both[0] >= 0, stage, stage_count)
    rows = both[0] + tile_ids // slots * total
    ahead = (stage[None, :] < stage[:, None]) | (
        (stage[None, :] == stage[:, None]) & (tile_ids[None, :] < tile_ids[:, None])
    )
    rank = jnp.sum(ahead.astype(jnp.int32), axis=1)
    entries = jnp.arange(2 * slots + UNROLL, dtype=jnp.int32)
    chosen = rank[None, :] == entries[:, None]
    columns = [tile_ids, rows] + [spots[:, cut] for cut in range(pieces)]
    ordered = jnp.stack(
        [jnp.sum(jnp.where(chosen, column[None, :], 0), axis=1) for column in columns], axis=1
    ).reshape(-1)
    bounds = jnp.sum((stage[None, :] < jnp.arange(stage_count + 1)[:, None]).astype(jnp.int32), axis=1)
    cores = core.astype(jnp.int32).reshape(1)

    half_type = pltpu.VMEM((2 * total + BLK, LANES), jnp.float32)
    work = 4 * slots * BLK * BLK * LANES // stage_count
    halves = []

    def stage_ins(sources):
        scratch = [
            pltpu.VMEM((len(sources) * sources[0].shape[0], LANES), jnp.bfloat16),
            pltpu.SemaphoreType.DMA,
        ]
        earlier = [pinned(halves[-1])] if halves else []
        ins = [*sources, *map(pinned, tile_sets), *earlier]
        return ins, [HBM] * len(sources) + [VMEM] * (2 + len(earlier)), scratch

    def aliases(ahead, ins):
        return {ahead + len(ins) - 1: 0} if halves else {}

    def add_stage(stage, sources):
        ins, specs, scratch = stage_ins(sources)
        halves.extend(
            call(
                functools.partial(stage_kernel, stage, len(sources), pieces),
                [ordered, bounds] + ins, [SMEM] * 2 + specs, [half_type], scratch, aliases(2, ins), work,
            )
        )

    def meanwhile(step, index, arrived, moved):
        if (step, index) == LAY_AT:
            moved, *tile_sets[:] = tie(moved, *tile_sets)
        if (step, index) in ADD_AT:
            stage = ADD_AT[step, index]
            add_stage(stage, arrived(stage))
            moved, halves[-1] = tie(moved, halves[-1])
        return moved

    if lined:
        stages = spread(parts, meanwhile)
        for stage in range(len(ADD_AT), LINE):
            add_stage(stage, stages[stage])
    else:
        stages = [[lax.all_gather(part, "aux", axis_index_groups=same_core, axis=0, tiled=True) for part in parts]]

    group = 1 if lined else chips // 2
    far = [group] * (chips // 2 // group)
    ins, specs, scratch = stage_ins(stages[-1])
    half, weights, *far_send = call(
        functools.partial(window_kernel, stage_count - 1, len(stages[-1]), pieces, shard, chips // 2),
        [ordered, bounds, chip_of_slot, cores] + ins,
        [SMEM] * 4 + specs,
        [half_type, pltpu.VMEM((2 * LANES, WIN), jnp.bfloat16)]
        + [pltpu.VMEM((size, shard, WIN), jnp.bfloat16) for size in far],
        scratch,
        aliases(4, ins),
        work + total // 4 * width * WIN * 2,
    )

    def rest(plan, half):
        return call(
            functools.partial(rest_kernel, shard, plan),
            [chip_of_slot, cores, pinned(half), pinned(weights)],
            [SMEM] * 2 + [VMEM] * 2,
            [pltpu.VMEM((group, shard, WIN), jnp.float32 if keeps else jnp.bfloat16) for _, keeps in plan],
            [],
            {},
            total // 4 * width * WIN * 2,
        )

    def near_of(half):
        blocks = rest([(index * group, keeps) for keeps in (True, False) for index in range(len(far))], half)
        if lined:
            blocks = [block[0] for block in blocks]
        return blocks[: len(far)], blocks[len(far) :]

    far_keep = rest([(chips // 2 + index * group, True) for index in range(len(far))], half)

    factor = 1.0 / math.sqrt(owners * width)
    if lined:
        far_keep, far_send = [block[0] for block in far_keep], [block[0] for block in far_send]
        return collect(far_keep, far_send, near_of, half, swap) * factor
    near_keep, near_send = near_of(half)
    keep, send = [*near_keep, *far_keep], [*near_send, *far_send]
    keep, send = jnp.concatenate(keep), jnp.concatenate(send)
    pair_sum = (keep + move(send, swap).astype(jnp.float32)).astype(jnp.bfloat16)
    block_sum = lax.psum_scatter(
        pair_sum.reshape(total // 2, WIN), "aux", axis_index_groups=same_core, scatter_dimension=0, tiled=True
    )
    return block_sum.astype(jnp.float32) * factor


def solution(mesh):
    placed = (
        P(("groups", "aux"), None),
        P(("groups", "aux"), None),
        P(("groups", "aux")),
        P(("groups", "aux"), None),
    )
    return jax.shard_map(
        local, mesh=mesh, in_specs=placed, out_specs=P(("groups", "aux"), None), check_vma=False
    )
```

```python
import functools
import math

import jax
import jax.numpy as jnp
from jax import lax
from jax.experimental import pallas as pl
from jax.experimental.pallas import tpu as pltpu
from jax.sharding import PartitionSpec as P

BLK = 64
WIN = 128
LANES = 128
UNROLL = 8
LINE = 4
SCOPED_BYTES = 6 * 1024 * 1024


def place(z, x, core):
    return (z * 2 + x) * 2 + core


def pairs_of(step):
    return [
        (place(z, x, core), place(*step(z, x), core)) for z in range(LINE) for x in range(2) for core in range(2)
    ]


def tie(*arrays):
    return lax.optimization_barrier(arrays)


def move(array, pairs):
    return lax.ppermute(array, "aux", pairs)


ALONG = pairs_of(lambda z, x: ((z + 1) % LINE, x))
BACK = pairs_of(lambda z, x: ((z - 1) % LINE, x))
ACROSS = pairs_of(lambda z, x: (z, 1 - x))
ADD_AT = {(2, 1): 0, (3, 0): 1, (3, 1): 2}
LAY_AT = (1, 1)


def spread(parts, meanwhile):
    lines, others = [[part] for part in parts], [[] for _ in parts]

    def arrived(stage):
        held = [line[stage] for line in lines] if stage < LINE else []
        return held + ([other[stage - 1] for other in others] if stage else [])

    for step in range(LINE):
        for index, (line, other) in enumerate(zip(lines, others)):
            if other:
                line[-1], other[-1] = tie(line[-1], other[-1])
            turn = step == LINE - 1 and index == 0
            source = other if turn else line
            source[-1] = meanwhile(step, index, arrived, source[-1])
            now = source[-1]
            if step + 1 < LINE:
                line.append(move(now, ALONG))
            other.append(move(now, ALONG if turn else ACROSS))
    return [arrived(stage) for stage in range(LINE + 1)]


def collect(far_keep, far_send, near_of, half, swap):
    def paired(keep, send):
        return keep + move(send, swap).astype(jnp.float32)

    order = (1, 2, 3, 0)
    far = {step: paired(far_keep[step], far_send[step]) for step in order}
    aside, crossing = far[1].astype(jnp.bfloat16), far[2].astype(jnp.bfloat16)
    half, aside, crossing = tie(half, aside, crossing)
    crossed = {2: move(crossing, ACROSS)}
    joining = move(aside, ALONG)
    near_keep, near_send = near_of(half)
    near = {step: paired(near_keep[step], near_send[step]) for step in (2, 1, 3, 0)}
    crossing, crossed[2] = tie(far[3].astype(jnp.bfloat16), crossed[2])
    crossed[3] = move(crossing, ACROSS)
    crossed[0] = move((far[0] + joining.astype(jnp.float32)).astype(jnp.bfloat16), ACROSS)

    two_on = move((near[2] + crossed[2].astype(jnp.float32)).astype(jnp.bfloat16), ALONG)
    one_on = move((near[1] + two_on.astype(jnp.float32)).astype(jnp.bfloat16), ALONG)
    one_back = move((near[3] + crossed[3].astype(jnp.float32)).astype(jnp.bfloat16), BACK)
    return near[0] + crossed[0].astype(jnp.float32) + one_on.astype(jnp.float32) + one_back.astype(jnp.float32)


def clear(half):
    whole = half.shape[0] // (4 * BLK) * (4 * BLK)

    @pl.loop(0, whole // (4 * BLK))
    def _(index):
        half[pl.ds(pl.multiple_of(index * 4 * BLK, BLK), 4 * BLK), :] = jnp.zeros((4 * BLK, LANES), jnp.float32)

    half[pl.ds(whole, half.shape[0] - whole), :] = jnp.zeros((half.shape[0] - whole, LANES), jnp.float32)


def add_tiles(stage, pieces, table_ref, bounds_ref, sources, tiles, half, occ, sem):
    rows = sources[0].shape[0]
    for index, source in enumerate(sources):
        pltpu.make_async_copy(source, occ.at[pl.ds(index * rows, rows)], sem).start()
    pltpu.make_async_copy(occ, occ, sem).wait()
    begin, end = bounds_ref[stage], bounds_ref[stage + 1]
    spill = half.shape[0] - BLK
    columns = 2 + pieces
    piece = BLK // pieces

    @pl.loop(0, (end - begin + UNROLL - 1) // UNROLL)
    def _(group):
        products, starts = [], []
        for lane in range(UNROLL):
            entry = begin + group * UNROLL + lane
            tile = table_ref[entry * columns]
            starts.append(jnp.where(entry < end, table_ref[entry * columns + 1], spill))
            spots = [jnp.where(entry < end, table_ref[entry * columns + 2 + cut], 0) for cut in range(pieces)]
            parts = [occ[pl.ds(pl.multiple_of(spot, piece), piece), :] for spot in spots]
            pair = tiles[tile]
            left = jnp.concatenate([pair[:, :BLK], pair[:, BLK:]], axis=0)
            block = parts[0] if pieces == 1 else jnp.concatenate(parts, axis=0)
            products.append(jnp.dot(left, block, preferred_element_type=jnp.float32))
        for product, start in zip(products, starts):
            start = pl.multiple_of(start, BLK)
            for odd in range(2):
                span = pl.ds(start + odd, BLK // 2, stride=2)
                half[span, :] += product[odd * (BLK // 2) : (odd + 1) * (BLK // 2)]


def fill_window(half, weights, shard, chips_ref, first, parity, out):
    side_rows = (half.shape[0] - BLK) // 2

    @pl.loop(0, out.shape[0])
    def _(index):
        start = pl.multiple_of((2 * chips_ref[first + index] + parity) * shard, 32)
        both = jnp.concatenate(
            [half[pl.ds(side * side_rows + start, shard), :].astype(jnp.bfloat16) for side in range(2)], axis=1
        )
        out[index] = jnp.dot(both, weights[...], preferred_element_type=jnp.float32).astype(out.dtype)


def load_tiles(tile_sets, tiles, sems):
    slots = tile_sets[0].shape[0]
    copies = [
        pltpu.make_async_copy(source, tiles.at[pl.ds(index * slots, slots)], sems.at[index])
        for index, source in enumerate(tile_sets)
    ]
    for copy in copies:
        copy.start()
    return copies


def add_stage(stage, count, pieces, table_ref, bounds_ref, refs):
    sources = refs[:count]
    if stage:
        tiles, _, half, *outs, occ, sems = refs[count:]
        copies = []
    else:
        *tile_sets, half, tiles = refs[count : count + 4]
        *outs, occ, sems = refs[count + 4 :]
        copies = load_tiles(tile_sets, tiles, sems)
        clear(half)
    for copy in copies:
        copy.wait()
    add_tiles(stage, pieces, table_ref, bounds_ref, sources, tiles, half, occ, sems.at[2])
    return half, outs


def stage_kernel(stage, count, pieces, table_ref, bounds_ref, *refs):
    add_stage(stage, count, pieces, table_ref, bounds_ref, refs)


def window_kernel(stage, count, pieces, shard, first, table_ref, bounds_ref, chips_ref, core_ref, *refs):
    half, (weights, *outs) = add_stage(stage, count, pieces, table_ref, bounds_ref, refs)
    side_rows = (half.shape[0] - BLK) // 2
    for side in range(2):
        weights[pl.ds(side * LANES, LANES), :] = half[pl.ds(side * side_rows, WIN), :].T.astype(jnp.bfloat16)
    for index, out in enumerate(outs):
        fill_window(half, weights, shard, chips_ref, first + index * out.shape[0], 1 - core_ref[0], out)


def rest_kernel(shard, plan, chips_ref, core_ref, half, weights, *outs):
    for (first, keeps), out in zip(plan, outs):
        parity = core_ref[0] if keeps else 1 - core_ref[0]
        fill_window(half, weights, shard, chips_ref, first, parity, out)


SMEM = pl.BlockSpec(memory_space=pltpu.SMEM)
HBM = pl.BlockSpec(memory_space=pl.ANY)
VMEM = pl.BlockSpec(memory_space=pltpu.VMEM)


def pinned(array):
    return pltpu.with_memory_space_constraint(array, pltpu.VMEM)


def call(kernel, ins, in_specs, outs, scratch, aliases, flops, scoped=0):
    return pl.pallas_call(
        kernel,
        out_shape=outs,
        in_specs=in_specs,
        out_specs=[VMEM] * len(outs),
        scratch_shapes=scratch,
        input_output_aliases=aliases,
        compiler_params=pltpu.CompilerParams(vmem_limit_bytes=SCOPED_BYTES + scoped),
        cost_estimate=pl.CostEstimate(flops=flops, bytes_accessed=4 << 20, transcendentals=0),
    )(*ins)


def local(block_values, block_pairs, live_counts, occupied):
    owners = lax.axis_size("aux")
    me = lax.axis_index("aux")
    core, chip = me % 2, me // 2
    shard, width = occupied.shape
    total = owners * shard
    slots = block_values.shape[0]
    piece = math.gcd(BLK, shard)
    pieces = BLK // piece
    chips = owners // 2
    lined = chips == 2 * LINE
    same_core = [[2 * i + k for i in range(chips)] for k in range(2)]
    swap = [(i, i ^ 1) for i in range(owners)]

    mine = lax.dynamic_slice_in_dim(occupied, core * LANES, LANES, 1)
    given = lax.dynamic_slice_in_dim(occupied, (1 - core) * LANES, LANES, 1)
    parts = (mine, move(given, swap))
    tile_sets = [
        values.reshape(slots, BLK * BLK // LANES, LANES) for values in (block_values, move(block_values, swap))
    ]

    slot_ids = jnp.arange(chips, dtype=jnp.int32)
    chip_of_slot = slot_ids
    stage_count = 1
    if lined:
        chip_of_slot = (slot_ids + chip // 2) % LINE * 2 + ((slot_ids // LINE) ^ (chip % 2))
        stage_count = LINE + 1

    tile_ids = jnp.arange(2 * slots, dtype=jnp.int32)
    row_starts = jnp.where(tile_ids[:slots] < live_counts[0], block_pairs[:, 0] * BLK, -1)
    table = jnp.stack([row_starts, block_pairs[:, 1]])
    both = jnp.concatenate([table, move(table, swap)], axis=1)
    first = both[1][:, None] * BLK + jnp.arange(pieces, dtype=jnp.int32) * piece
    owner = first // shard
    part = (owner % 2) ^ core
    owner_chip = owner // 2
    if lined:
        back = (chip // 2 - owner_chip // 2) % LINE
        side = (owner_chip % 2) ^ (chip % 2)
        stage = (back + side)[:, 0]
        slot_of = part + 2 * jnp.where(back + side < LINE, side, 0)
    else:
        stage = jnp.zeros_like(tile_ids)
        slot_of = part * chips + owner_chip
    spots = slot_of * shard + first % shard
    stage = jnp.where(both[0] >= 0, stage, stage_count)
    rows = both[0] + tile_ids // slots * total
    ahead = (stage[None, :] < stage[:, None]) | (
        (stage[None, :] == stage[:, None]) & (tile_ids[None, :] < tile_ids[:, None])
    )
    rank = jnp.sum(ahead.astype(jnp.int32), axis=1)
    entries = jnp.arange(2 * slots + UNROLL, dtype=jnp.int32)
    chosen = rank[None, :] == entries[:, None]
    columns = [tile_ids, rows] + [spots[:, cut] for cut in range(pieces)]
    ordered = jnp.stack(
        [jnp.sum(jnp.where(chosen, column[None, :], 0), axis=1) for column in columns], axis=1
    ).reshape(-1)
    bounds = jnp.sum((stage[None, :] < jnp.arange(stage_count + 1)[:, None]).astype(jnp.int32), axis=1)
    cores = core.astype(jnp.int32).reshape(1)

    half_type = pltpu.VMEM((2 * total + BLK, LANES), jnp.float32)
    tiles_type = pltpu.VMEM((2 * slots, BLK * BLK // LANES, LANES), jnp.bfloat16)
    work = 4 * slots * BLK * BLK * LANES // stage_count
    state = []

    def run_stage(kernel, sources, tables, outs, flops):
        rows = len(sources) * sources[0].shape[0]
        scratch = [pltpu.VMEM((rows, LANES), jnp.bfloat16), pltpu.SemaphoreType.DMA((3,))]
        ins, specs = [*tables, *sources], [SMEM] * len(tables) + [HBM] * len(sources)
        made, aliases = [half_type], {}
        if state:
            aliases = {len(ins) + 1: 0}
            ins, specs = ins + [pinned(state[1]), pinned(state[0])], specs + [VMEM] * 2
        else:
            ins, specs, made = ins + tile_sets, specs + [HBM] * 2, [half_type, tiles_type]
        results = call(kernel, ins, specs, made + outs, scratch, aliases, flops, 2 * rows * LANES)
        state[:] = [results[0], state[1] if state else results[1]]
        return results[len(made) :]

    def add(stage, sources):
        kernel = functools.partial(stage_kernel, stage, len(sources), pieces)
        run_stage(kernel, sources, [ordered, bounds], [], work)

    def meanwhile(step, index, arrived, moved):
        if (step, index) == LAY_AT:
            moved, *tile_sets[:] = tie(moved, *tile_sets)
        if (step, index) in ADD_AT:
            stage = ADD_AT[step, index]
            add(stage, arrived(stage))
            moved, state[0] = tie(moved, state[0])
        return moved

    if lined:
        stages = spread(parts, meanwhile)
        for stage in range(len(ADD_AT), LINE):
            add(stage, stages[stage])
    else:
        stages = [[lax.all_gather(part, "aux", axis_index_groups=same_core, axis=0, tiled=True) for part in parts]]

    group = 1 if lined else chips // 2
    far = [group] * (chips // 2 // group)
    weights, *far_send = run_stage(
        functools.partial(window_kernel, stage_count - 1, len(stages[-1]), pieces, shard, chips // 2),
        stages[-1],
        [ordered, bounds, chip_of_slot, cores],
        [pltpu.VMEM((2 * LANES, WIN), jnp.bfloat16)]
        + [pltpu.VMEM((size, shard, WIN), jnp.bfloat16) for size in far],
        work + total // 4 * width * WIN * 2,
    )
    half = state[0]

    def rest(plan, half):
        return call(
            functools.partial(rest_kernel, shard, plan),
            [chip_of_slot, cores, pinned(half), pinned(weights)],
            [SMEM] * 2 + [VMEM] * 2,
            [pltpu.VMEM((group, shard, WIN), jnp.float32 if keeps else jnp.bfloat16) for _, keeps in plan],
            [],
            {},
            total // 4 * width * WIN * 2,
        )

    def near_of(half):
        blocks = rest([(index * group, keeps) for keeps in (True, False) for index in range(len(far))], half)
        if lined:
            blocks = [block[0] for block in blocks]
        return blocks[: len(far)], blocks[len(far) :]

    far_keep = rest([(chips // 2 + index * group, True) for index in range(len(far))], half)

    factor = 1.0 / math.sqrt(owners * width)
    if lined:
        far_keep, far_send = [block[0] for block in far_keep], [block[0] for block in far_send]
        return collect(far_keep, far_send, near_of, half, swap) * factor
    near_keep, near_send = near_of(half)
    keep, send = [*near_keep, *far_keep], [*near_send, *far_send]
    keep, send = jnp.concatenate(keep), jnp.concatenate(send)
    pair_sum = (keep + move(send, swap).astype(jnp.float32)).astype(jnp.bfloat16)
    block_sum = lax.psum_scatter(
        pair_sum.reshape(total // 2, WIN), "aux", axis_index_groups=same_core, scatter_dimension=0, tiled=True
    )
    return block_sum.astype(jnp.float32) * factor


def solution(mesh):
    placed = (
        P(("groups", "aux"), None),
        P(("groups", "aux"), None),
        P(("groups", "aux")),
        P(("groups", "aux"), None),
    )
    return jax.shard_map(
        local, mesh=mesh, in_specs=placed, out_specs=P(("groups", "aux"), None), check_vma=False
    )
```

```python
import functools
import math

import jax
import jax.numpy as jnp
from jax import lax
from jax.experimental import pallas as pl
from jax.experimental.pallas import tpu as pltpu
from jax.sharding import PartitionSpec as P

BLK = 64
WIN = 128
LANES = 128
UNROLL = 16
LINE = 4
SCOPED_BYTES = 6 * 1024 * 1024


def place(z, x, core):
    return (z * 2 + x) * 2 + core


def pairs_of(step):
    return [
        (place(z, x, core), place(*step(z, x), core)) for z in range(LINE) for x in range(2) for core in range(2)
    ]


def tie(*arrays):
    return lax.optimization_barrier(arrays)


def move(array, pairs):
    return lax.ppermute(array, "aux", pairs)


ALONG = pairs_of(lambda z, x: ((z + 1) % LINE, x))
BACK = pairs_of(lambda z, x: ((z - 1) % LINE, x))
ACROSS = pairs_of(lambda z, x: (z, 1 - x))
ADD_AT = {2: (0,), 3: (1, 2)}
LAY_AT = 1


def spread(own, meanwhile):
    stages = [[own]]
    line, other = own, None
    for step in range(LINE):
        line = meanwhile(step, stages, line)
        if other is not None:
            line, other = tie(line, other)
            stages[-1][:] = [line, other]
        if step + 1 < LINE:
            line, other = move(line, ALONG), move(line, ACROSS)
            stages.append([line, other])
    half = own.shape[0] // 2
    stages.append([move(other[:half], ALONG), move(line[half:], ACROSS)])
    return stages


def collect(far_keep, far_send, near_of, half, swap):
    def paired(keep, send):
        return keep + move(send, swap).astype(jnp.float32)

    order = (1, 2, 3, 0)
    far = {step: paired(far_keep[step], far_send[step]) for step in order}
    aside, crossing = far[1].astype(jnp.bfloat16), far[2].astype(jnp.bfloat16)
    half, aside, crossing = tie(half, aside, crossing)
    crossed = {2: move(crossing, ACROSS)}
    joining = move(aside, ALONG)
    near_keep, near_send = near_of(half)
    near = {step: paired(near_keep[step], near_send[step]) for step in (2, 1, 3, 0)}
    crossing, crossed[2] = tie(far[3].astype(jnp.bfloat16), crossed[2])
    crossed[3] = move(crossing, ACROSS)
    crossing, crossed[3] = tie((far[0] + joining.astype(jnp.float32)).astype(jnp.bfloat16), crossed[3])
    crossed[0] = move(crossing, ACROSS)

    two_on = move((near[2] + crossed[2].astype(jnp.float32)).astype(jnp.bfloat16), ALONG)
    one_on = move((near[1] + two_on.astype(jnp.float32)).astype(jnp.bfloat16), ALONG)
    one_back = move((near[3] + crossed[3].astype(jnp.float32)).astype(jnp.bfloat16), BACK)
    return near[0] + crossed[0].astype(jnp.float32) + one_on.astype(jnp.float32) + one_back.astype(jnp.float32)


def clear(half):
    whole = half.shape[0] // (4 * BLK) * (4 * BLK)

    @pl.loop(0, whole // (4 * BLK))
    def _(index):
        half[pl.ds(pl.multiple_of(index * 4 * BLK, BLK), 4 * BLK), :] = jnp.zeros((4 * BLK, LANES), jnp.float32)

    half[pl.ds(whole, half.shape[0] - whole), :] = jnp.zeros((half.shape[0] - whole, LANES), jnp.float32)


def add_tiles(stage, pieces, table_ref, bounds_ref, sources, tiles, half, occ, sem):
    rows = sources[0].shape[0]
    for index, source in enumerate(sources):
        pltpu.make_async_copy(source, occ.at[pl.ds(index * rows, rows)], sem).start()
    pltpu.make_async_copy(occ, occ, sem).wait()
    begin, end = bounds_ref[stage], bounds_ref[stage + 1]
    low = lax.broadcasted_iota(jnp.int32, tiles.shape[1:], 1) < BLK
    zero = jnp.zeros(tiles.shape[1:], jnp.bfloat16)
    spill = half.shape[0] - BLK
    entries = table_ref.shape[0] // (2 + pieces)
    piece = BLK // pieces

    @pl.loop(0, (end - begin + UNROLL - 1) // UNROLL)
    def _(group):
        products, starts = [], []
        for lane in range(UNROLL):
            entry = begin + group * UNROLL + lane
            tile = table_ref[entry]
            starts.append(jnp.where(entry < end, table_ref[entries + entry], spill))
            spots = [jnp.where(entry < end, table_ref[(2 + cut) * entries + entry], 0) for cut in range(pieces)]
            parts = [occ[pl.ds(pl.multiple_of(spot, piece), piece), :] for spot in spots]
            pair = tiles[tile]
            left = jnp.concatenate([jnp.where(low, pair, zero), jnp.where(low, zero, pair)], axis=0)
            block = jnp.concatenate(parts * 2, axis=0)
            products.append(jnp.dot(left, block, preferred_element_type=jnp.float32))
        for product, start in zip(products, starts):
            start = pl.multiple_of(start, BLK)
            for odd in range(2):
                span = pl.ds(start + odd, BLK // 2, stride=2)
                half[span, :] += product[odd * (BLK // 2) : (odd + 1) * (BLK // 2)]


def fill_window(half, weights, shard, chips_ref, first, parity, out):
    side_rows = (half.shape[0] - BLK) // 2

    @pl.loop(0, out.shape[0])
    def _(index):
        start = pl.multiple_of((2 * chips_ref[first + index] + parity) * shard, 32)
        both = jnp.concatenate(
            [half[pl.ds(side * side_rows + start, shard), :].astype(jnp.bfloat16) for side in range(2)], axis=1
        )
        out[index] = jnp.dot(both, weights[...], preferred_element_type=jnp.float32).astype(out.dtype)


def load_tiles(tile_sets, tiles, sems):
    slots = tile_sets[0].shape[0]
    copies = [
        pltpu.make_async_copy(source, tiles.at[pl.ds(index * slots, slots)], sems.at[index])
        for index, source in enumerate(tile_sets)
    ]
    for copy in copies:
        copy.start()
    return copies


def add_stage(stage, count, pieces, table_ref, bounds_ref, refs):
    sources = refs[:count]
    if stage:
        tiles, _, half, *outs, occ, sems = refs[count:]
        copies = []
    else:
        *tile_sets, half, tiles = refs[count : count + 4]
        *outs, occ, sems = refs[count + 4 :]
        copies = load_tiles(tile_sets, tiles, sems)
        clear(half)
    for copy in copies:
        copy.wait()
    add_tiles(stage, pieces, table_ref, bounds_ref, sources, tiles, half, occ, sems.at[2])
    return half, outs


def stage_kernel(stage, count, pieces, table_ref, bounds_ref, *refs):
    add_stage(stage, count, pieces, table_ref, bounds_ref, refs)


def window_kernel(stage, count, pieces, shard, first, table_ref, bounds_ref, chips_ref, core_ref, *refs):
    half, (weights, *outs) = add_stage(stage, count, pieces, table_ref, bounds_ref, refs)
    side_rows = (half.shape[0] - BLK) // 2
    for side in range(2):
        weights[pl.ds(side * LANES, LANES), :] = half[pl.ds(side * side_rows, WIN), :].T.astype(jnp.bfloat16)
    for index, out in enumerate(outs):
        fill_window(half, weights, shard, chips_ref, first + index * out.shape[0], 1 - core_ref[0], out)


def rest_kernel(shard, plan, chips_ref, core_ref, half, weights, *outs):
    for (first, keeps), out in zip(plan, outs):
        parity = core_ref[0] if keeps else 1 - core_ref[0]
        fill_window(half, weights, shard, chips_ref, first, parity, out)


SMEM = pl.BlockSpec(memory_space=pltpu.SMEM)
HBM = pl.BlockSpec(memory_space=pl.ANY)
VMEM = pl.BlockSpec(memory_space=pltpu.VMEM)


def pinned(array):
    return pltpu.with_memory_space_constraint(array, pltpu.VMEM)


def call(kernel, ins, in_specs, outs, scratch, aliases, flops, scoped=0):
    return pl.pallas_call(
        kernel,
        out_shape=outs,
        in_specs=in_specs,
        out_specs=[VMEM] * len(outs),
        scratch_shapes=scratch,
        input_output_aliases=aliases,
        compiler_params=pltpu.CompilerParams(vmem_limit_bytes=SCOPED_BYTES + scoped),
        cost_estimate=pl.CostEstimate(flops=flops, bytes_accessed=4 << 20, transcendentals=0),
    )(*ins)


def local(block_values, block_pairs, live_counts, occupied):
    owners = lax.axis_size("aux")
    me = lax.axis_index("aux")
    core, chip = me % 2, me // 2
    shard, width = occupied.shape
    total = owners * shard
    slots = block_values.shape[0]
    piece = math.gcd(BLK, shard)
    pieces = BLK // piece
    chips = owners // 2
    lined = chips == 2 * LINE
    same_core = [[2 * i + k for i in range(chips)] for k in range(2)]
    swap = [(i, i ^ 1) for i in range(owners)]

    mine = lax.dynamic_slice_in_dim(occupied, core * LANES, LANES, 1)
    given = lax.dynamic_slice_in_dim(occupied, (1 - core) * LANES, LANES, 1)
    parts = (mine, move(given, swap))
    others = [move(array, swap) for array in (block_values, block_pairs, live_counts)]
    own, block_values, block_pairs, live_counts = tie(
        jnp.concatenate(parts, axis=0), block_values, block_pairs, live_counts
    )
    tile_sets = [values.reshape(slots, BLK * BLK // LANES, LANES) for values in (block_values, others[0])]

    slot_ids = jnp.arange(chips, dtype=jnp.int32)
    chip_of_slot = slot_ids
    stage_count = 1
    if lined:
        chip_of_slot = (slot_ids + chip // 2) % LINE * 2 + ((slot_ids // LINE) ^ (chip % 2))
        stage_count = LINE + 1

    tile_ids = jnp.arange(2 * slots, dtype=jnp.int32)
    pairs = jnp.concatenate([block_pairs, others[1]])
    live = tile_ids % slots < jnp.where(tile_ids < slots, live_counts[0], others[2][0])
    first = pairs[:, 1][:, None] * BLK + jnp.arange(pieces, dtype=jnp.int32) * piece
    owner = first // shard
    part = (owner % 2) ^ core
    owner_chip = owner // 2
    if lined:
        back = (chip // 2 - owner_chip // 2) % LINE
        side = (owner_chip % 2) ^ (chip % 2)
        stage = (back + side)[:, 0]
        slot_of = part + 2 * jnp.where(back + side < LINE, side, 0)
    else:
        stage = jnp.zeros_like(tile_ids)
        slot_of = 2 * owner_chip + part
    spots = slot_of * shard + first % shard
    stage = jnp.where(live, stage, stage_count)
    rows = pairs[:, 0] * BLK + tile_ids // slots * total
    ahead = (stage[None, :] < stage[:, None]) | (
        (stage[None, :] == stage[:, None]) & (tile_ids[None, :] < tile_ids[:, None])
    )
    rank = jnp.sum(ahead.astype(jnp.int32), axis=1)
    entries = jnp.arange(2 * slots + UNROLL, dtype=jnp.int32)
    chosen = rank[None, :] == entries[:, None]
    columns = [tile_ids, rows] + [spots[:, cut] for cut in range(pieces)]
    ordered = jnp.concatenate([jnp.sum(jnp.where(chosen, column[None, :], 0), axis=1) for column in columns])
    bounds = jnp.sum((stage[None, :] < jnp.arange(stage_count + 1)[:, None]).astype(jnp.int32), axis=1)
    cores = core.astype(jnp.int32).reshape(1)

    half_type = pltpu.VMEM((2 * total + BLK, LANES), jnp.float32)
    tiles_type = pltpu.VMEM((2 * slots, BLK * BLK // LANES, LANES), jnp.bfloat16)
    work = 4 * slots * BLK * BLK * LANES // stage_count
    state = []

    def run_stage(kernel, sources, tables, outs, flops):
        rows = len(sources) * sources[0].shape[0]
        scratch = [pltpu.VMEM((rows, LANES), jnp.bfloat16), pltpu.SemaphoreType.DMA((3,))]
        ins, specs = [*tables, *sources], [SMEM] * len(tables) + [HBM] * len(sources)
        made, aliases = [half_type], {}
        if state:
            aliases = {len(ins) + 1: 0}
            ins, specs = ins + [pinned(state[1]), pinned(state[0])], specs + [VMEM] * 2
        else:
            ins, specs, made = ins + tile_sets, specs + [HBM] * 2, [half_type, tiles_type]
        results = call(kernel, ins, specs, made + outs, scratch, aliases, flops, 2 * rows * LANES)
        state[:] = [results[0], state[1] if state else results[1]]
        return results[len(made) :]

    def add(stage, sources):
        kernel = functools.partial(stage_kernel, stage, len(sources), pieces)
        run_stage(kernel, sources, [ordered, bounds], [], work)

    def meanwhile(step, stages, moved):
        if step == LAY_AT:
            moved, *tile_sets[:] = tie(moved, *tile_sets)
        for stage in ADD_AT.get(step, ()):
            add(stage, stages[stage])
            moved, state[0] = tie(moved, state[0])
        return moved

    if lined:
        stages = spread(own, meanwhile)
        for stage in range(sum(map(len, ADD_AT.values())), LINE):
            add(stage, stages[stage])
    else:
        stages = [[lax.all_gather(own, "aux", axis_index_groups=same_core, axis=0, tiled=True)]]

    group = 1 if lined else chips // 2
    far = [group] * (chips // 2 // group)
    weights, *far_send = run_stage(
        functools.partial(window_kernel, stage_count - 1, len(stages[-1]), pieces, shard, chips // 2),
        stages[-1],
        [ordered, bounds, chip_of_slot, cores],
        [pltpu.VMEM((2 * LANES, WIN), jnp.bfloat16)]
        + [pltpu.VMEM((size, shard, WIN), jnp.bfloat16) for size in far],
        work + total // 4 * width * WIN * 2,
    )
    half = state[0]

    def rest(plan, half):
        return call(
            functools.partial(rest_kernel, shard, plan),
            [chip_of_slot, cores, pinned(half), pinned(weights)],
            [SMEM] * 2 + [VMEM] * 2,
            [pltpu.VMEM((group, shard, WIN), jnp.float32 if keeps else jnp.bfloat16) for _, keeps in plan],
            [],
            {},
            total // 4 * width * WIN * 2,
        )

    def near_of(half):
        blocks = rest([(index * group, keeps) for keeps in (True, False) for index in range(len(far))], half)
        if lined:
            blocks = [block[0] for block in blocks]
        return blocks[: len(far)], blocks[len(far) :]

    far_keep = rest([(chips // 2 + index * group, True) for index in range(len(far))], half)

    factor = 1.0 / math.sqrt(owners * width)
    if lined:
        far_keep, far_send = [block[0] for block in far_keep], [block[0] for block in far_send]
        return collect(far_keep, far_send, near_of, half, swap) * factor
    near_keep, near_send = near_of(half)
    keep, send = [*near_keep, *far_keep], [*near_send, *far_send]
    keep, send = jnp.concatenate(keep), jnp.concatenate(send)
    pair_sum = (keep + move(send, swap).astype(jnp.float32)).astype(jnp.bfloat16)
    block_sum = lax.psum_scatter(
        pair_sum.reshape(total // 2, WIN), "aux", axis_index_groups=same_core, scatter_dimension=0, tiled=True
    )
    return block_sum.astype(jnp.float32) * factor


def solution(mesh):
    placed = (
        P(("groups", "aux"), None),
        P(("groups", "aux"), None),
        P(("groups", "aux")),
        P(("groups", "aux"), None),
    )
    return jax.shard_map(
        local, mesh=mesh, in_specs=placed, out_specs=P(("groups", "aux"), None), check_vma=False
    )
```

```python
import functools
import math

import jax
import jax.numpy as jnp
from jax import lax
from jax.experimental import pallas as pl
from jax.experimental.pallas import tpu as pltpu
from jax.sharding import PartitionSpec as P

BLK = 64
WIN = 128
LANES = 128
UNROLL = 16
LINE = 4
SCOPED_BYTES = 6 * 1024 * 1024


def place(z, x, core):
    return (z * 2 + x) * 2 + core


def pairs_of(step):
    return [
        (place(z, x, core), place(*step(z, x), core)) for z in range(LINE) for x in range(2) for core in range(2)
    ]


def tie(*arrays):
    return lax.optimization_barrier(arrays)


def move(array, pairs):
    return lax.ppermute(array, "aux", pairs)


ALONG = pairs_of(lambda z, x: ((z + 1) % LINE, x))
BACK = pairs_of(lambda z, x: ((z - 1) % LINE, x))
ACROSS = pairs_of(lambda z, x: (z, 1 - x))
ADD_AT = {(2, 1): 0, (3, 0): 1, (3, 1): 2}
LAY_AT = (1, 1)


def spread(parts, meanwhile):
    lines, others = [[part] for part in parts], [[] for _ in parts]

    def arrived(stage):
        held = [line[stage] for line in lines] if stage < LINE else []
        return held + ([other[stage - 1] for other in others] if stage else [])

    for step in range(LINE):
        for index, (line, other) in enumerate(zip(lines, others)):
            if other:
                line[-1], other[-1] = tie(line[-1], other[-1])
            turn = step == LINE - 1 and index == 0
            source = other if turn else line
            source[-1] = meanwhile(step, index, arrived, source[-1])
            now = source[-1]
            if step + 1 < LINE:
                line.append(move(now, ALONG))
            other.append(move(now, ALONG if turn else ACROSS))
    return [arrived(stage) for stage in range(LINE + 1)]


def collect(far_keep, far_send, near_of, half, swap):
    def paired(keep, send):
        return keep + move(send, swap).astype(jnp.float32)

    order = (1, 2, 3, 0)
    far = {step: paired(far_keep[step], far_send[step]) for step in order}
    aside, crossing = far[1].astype(jnp.bfloat16), far[2].astype(jnp.bfloat16)
    half, aside, crossing = tie(half, aside, crossing)
    crossed = {2: move(crossing, ACROSS)}
    joining = move(aside, ALONG)
    near_keep, near_send = near_of(half)
    near = {step: paired(near_keep[step], near_send[step]) for step in (2, 1, 3, 0)}
    crossing, crossed[2] = tie(far[3].astype(jnp.bfloat16), crossed[2])
    crossed[3] = move(crossing, ACROSS)
    crossing, crossed[3] = tie((far[0] + joining.astype(jnp.float32)).astype(jnp.bfloat16), crossed[3])
    crossed[0] = move(crossing, ACROSS)

    two_on = move((near[2] + crossed[2].astype(jnp.float32)).astype(jnp.bfloat16), ALONG)
    one_on = move((near[1] + two_on.astype(jnp.float32)).astype(jnp.bfloat16), ALONG)
    one_back = move((near[3] + crossed[3].astype(jnp.float32)).astype(jnp.bfloat16), BACK)
    return near[0] + crossed[0].astype(jnp.float32) + one_on.astype(jnp.float32) + one_back.astype(jnp.float32)


def clear(half):
    whole = half.shape[0] // (4 * BLK) * (4 * BLK)

    @pl.loop(0, whole // (4 * BLK))
    def _(index):
        half[pl.ds(pl.multiple_of(index * 4 * BLK, BLK), 4 * BLK), :] = jnp.zeros((4 * BLK, LANES), jnp.float32)

    half[pl.ds(whole, half.shape[0] - whole), :] = jnp.zeros((half.shape[0] - whole, LANES), jnp.float32)


def add_tiles(stage, pieces, table_ref, bounds_ref, sources, tiles, half, occ, sem):
    rows = sources[0].shape[0]
    for index, source in enumerate(sources):
        pltpu.make_async_copy(source, occ.at[pl.ds(index * rows, rows)], sem).start()
    pltpu.make_async_copy(occ, occ, sem).wait()
    begin, end = bounds_ref[stage], bounds_ref[stage + 1]
    low = lax.broadcasted_iota(jnp.int32, tiles.shape[1:], 1) < BLK
    zero = jnp.zeros(tiles.shape[1:], jnp.bfloat16)
    spill = half.shape[0] - BLK
    entries = table_ref.shape[0] // (2 + pieces)
    piece = BLK // pieces

    @pl.loop(0, (end - begin + UNROLL - 1) // UNROLL)
    def _(group):
        products, starts = [], []
        for lane in range(UNROLL):
            entry = begin + group * UNROLL + lane
            tile = table_ref[entry]
            starts.append(jnp.where(entry < end, table_ref[entries + entry], spill))
            spots = [jnp.where(entry < end, table_ref[(2 + cut) * entries + entry], 0) for cut in range(pieces)]
            parts = [occ[pl.ds(pl.multiple_of(spot, piece), piece), :] for spot in spots]
            pair = tiles[tile]
            left = jnp.concatenate([jnp.where(low, pair, zero), jnp.where(low, zero, pair)], axis=0)
            block = jnp.concatenate(parts * 2, axis=0)
            products.append(jnp.dot(left, block, preferred_element_type=jnp.float32))
        for product, start in zip(products, starts):
            start = pl.multiple_of(start, BLK)
            for odd in range(2):
                span = pl.ds(start + odd, BLK // 2, stride=2)
                half[span, :] += product[odd * (BLK // 2) : (odd + 1) * (BLK // 2)]


def fill_window(half, weights, shard, chips_ref, first, parity, out):
    side_rows = (half.shape[0] - BLK) // 2

    @pl.loop(0, out.shape[0])
    def _(index):
        start = pl.multiple_of((2 * chips_ref[first + index] + parity) * shard, 32)
        both = jnp.concatenate(
            [half[pl.ds(side * side_rows + start, shard), :].astype(jnp.bfloat16) for side in range(2)], axis=1
        )
        out[index] = jnp.dot(both, weights[...], preferred_element_type=jnp.float32).astype(out.dtype)


def load_tiles(tile_sets, tiles, sems):
    slots = tile_sets[0].shape[0]
    copies = [
        pltpu.make_async_copy(source, tiles.at[pl.ds(index * slots, slots)], sems.at[index])
        for index, source in enumerate(tile_sets)
    ]
    for copy in copies:
        copy.start()
    return copies


def add_stage(stage, count, pieces, table_ref, bounds_ref, refs):
    sources = refs[:count]
    if stage:
        tiles, _, half, *outs, occ, sems = refs[count:]
        copies = []
    else:
        *tile_sets, half, tiles = refs[count : count + 4]
        *outs, occ, sems = refs[count + 4 :]
        copies = load_tiles(tile_sets, tiles, sems)
        clear(half)
    for copy in copies:
        copy.wait()
    add_tiles(stage, pieces, table_ref, bounds_ref, sources, tiles, half, occ, sems.at[2])
    return half, outs


def stage_kernel(stage, count, pieces, table_ref, bounds_ref, *refs):
    add_stage(stage, count, pieces, table_ref, bounds_ref, refs)


def window_kernel(stage, count, pieces, shard, first, table_ref, bounds_ref, chips_ref, core_ref, *refs):
    half, (weights, *outs) = add_stage(stage, count, pieces, table_ref, bounds_ref, refs)
    side_rows = (half.shape[0] - BLK) // 2
    for side in range(2):
        weights[pl.ds(side * LANES, LANES), :] = half[pl.ds(side * side_rows, WIN), :].T.astype(jnp.bfloat16)
    for index, out in enumerate(outs):
        fill_window(half, weights, shard, chips_ref, first + index * out.shape[0], 1 - core_ref[0], out)


def rest_kernel(shard, plan, chips_ref, core_ref, half, weights, *outs):
    for (first, keeps), out in zip(plan, outs):
        parity = core_ref[0] if keeps else 1 - core_ref[0]
        fill_window(half, weights, shard, chips_ref, first, parity, out)


SMEM = pl.BlockSpec(memory_space=pltpu.SMEM)
HBM = pl.BlockSpec(memory_space=pl.ANY)
VMEM = pl.BlockSpec(memory_space=pltpu.VMEM)


def pinned(array):
    return pltpu.with_memory_space_constraint(array, pltpu.VMEM)


def call(kernel, ins, in_specs, outs, scratch, aliases, flops, scoped=0):
    return pl.pallas_call(
        kernel,
        out_shape=outs,
        in_specs=in_specs,
        out_specs=[VMEM] * len(outs),
        scratch_shapes=scratch,
        input_output_aliases=aliases,
        compiler_params=pltpu.CompilerParams(vmem_limit_bytes=SCOPED_BYTES + scoped),
        cost_estimate=pl.CostEstimate(flops=flops, bytes_accessed=4 << 20, transcendentals=0),
    )(*ins)


def local(block_values, block_pairs, live_counts, occupied):
    owners = lax.axis_size("aux")
    me = lax.axis_index("aux")
    core, chip = me % 2, me // 2
    shard, width = occupied.shape
    total = owners * shard
    slots = block_values.shape[0]
    piece = math.gcd(BLK, shard)
    pieces = BLK // piece
    chips = owners // 2
    lined = chips == 2 * LINE
    same_core = [[2 * i + k for i in range(chips)] for k in range(2)]
    swap = [(i, i ^ 1) for i in range(owners)]

    mine = lax.dynamic_slice_in_dim(occupied, core * LANES, LANES, 1)
    given = lax.dynamic_slice_in_dim(occupied, (1 - core) * LANES, LANES, 1)
    parts = [mine, move(given, swap)]
    others = [move(array, swap) for array in (block_values, block_pairs, live_counts)]
    *parts, block_values, block_pairs, live_counts = tie(*parts, block_values, block_pairs, live_counts)
    tile_sets = [values.reshape(slots, BLK * BLK // LANES, LANES) for values in (block_values, others[0])]

    slot_ids = jnp.arange(chips, dtype=jnp.int32)
    chip_of_slot = slot_ids
    stage_count = 1
    if lined:
        chip_of_slot = (slot_ids + chip // 2) % LINE * 2 + ((slot_ids // LINE) ^ (chip % 2))
        stage_count = LINE + 1

    tile_ids = jnp.arange(2 * slots, dtype=jnp.int32)
    pairs = jnp.concatenate([block_pairs, others[1]])
    live = tile_ids % slots < jnp.where(tile_ids < slots, live_counts[0], others[2][0])
    first = pairs[:, 1][:, None] * BLK + jnp.arange(pieces, dtype=jnp.int32) * piece
    owner = first // shard
    part = (owner % 2) ^ core
    owner_chip = owner // 2
    if lined:
        back = (chip // 2 - owner_chip // 2) % LINE
        side = (owner_chip % 2) ^ (chip % 2)
        stage = (back + side)[:, 0]
        slot_of = part + 2 * jnp.where(back + side < LINE, side, 0)
    else:
        stage = jnp.zeros_like(tile_ids)
        slot_of = part * chips + owner_chip
    spots = slot_of * shard + first % shard
    stage = jnp.where(live, stage, stage_count)
    rows = pairs[:, 0] * BLK + tile_ids // slots * total
    ahead = (stage[None, :] < stage[:, None]) | (
        (stage[None, :] == stage[:, None]) & (tile_ids[None, :] < tile_ids[:, None])
    )
    rank = jnp.sum(ahead.astype(jnp.int32), axis=1)
    entries = jnp.arange(2 * slots + UNROLL, dtype=jnp.int32)
    chosen = rank[None, :] == entries[:, None]
    columns = [tile_ids, rows] + [spots[:, cut] for cut in range(pieces)]
    ordered = jnp.concatenate([jnp.sum(jnp.where(chosen, column[None, :], 0), axis=1) for column in columns])
    bounds = jnp.sum((stage[None, :] < jnp.arange(stage_count + 1)[:, None]).astype(jnp.int32), axis=1)
    cores = core.astype(jnp.int32).reshape(1)

    half_type = pltpu.VMEM((2 * total + BLK, LANES), jnp.float32)
    tiles_type = pltpu.VMEM((2 * slots, BLK * BLK // LANES, LANES), jnp.bfloat16)
    work = 4 * slots * BLK * BLK * LANES // stage_count
    state = []

    def run_stage(kernel, sources, tables, outs, flops):
        rows = len(sources) * sources[0].shape[0]
        scratch = [pltpu.VMEM((rows, LANES), jnp.bfloat16), pltpu.SemaphoreType.DMA((3,))]
        ins, specs = [*tables, *sources], [SMEM] * len(tables) + [HBM] * len(sources)
        made, aliases = [half_type], {}
        if state:
            aliases = {len(ins) + 1: 0}
            ins, specs = ins + [pinned(state[1]), pinned(state[0])], specs + [VMEM] * 2
        else:
            ins, specs, made = ins + tile_sets, specs + [HBM] * 2, [half_type, tiles_type]
        results = call(kernel, ins, specs, made + outs, scratch, aliases, flops, 2 * rows * LANES)
        state[:] = [results[0], state[1] if state else results[1]]
        return results[len(made) :]

    def add(stage, sources):
        kernel = functools.partial(stage_kernel, stage, len(sources), pieces)
        run_stage(kernel, sources, [ordered, bounds], [], work)

    def meanwhile(step, index, arrived, moved):
        if (step, index) == LAY_AT:
            moved, *tile_sets[:] = tie(moved, *tile_sets)
        if (step, index) in ADD_AT:
            stage = ADD_AT[step, index]
            add(stage, arrived(stage))
            moved, state[0] = tie(moved, state[0])
        return moved

    if lined:
        stages = spread(parts, meanwhile)
        for stage in range(len(ADD_AT), LINE):
            add(stage, stages[stage])
    else:
        stages = [[lax.all_gather(part, "aux", axis_index_groups=same_core, axis=0, tiled=True) for part in parts]]

    group = 1 if lined else chips // 2
    far = [group] * (chips // 2 // group)
    weights, *far_send = run_stage(
        functools.partial(window_kernel, stage_count - 1, len(stages[-1]), pieces, shard, chips // 2),
        stages[-1],
        [ordered, bounds, chip_of_slot, cores],
        [pltpu.VMEM((2 * LANES, WIN), jnp.bfloat16)]
        + [pltpu.VMEM((size, shard, WIN), jnp.bfloat16) for size in far],
        work + total // 4 * width * WIN * 2,
    )
    half = state[0]

    def rest(plan, half):
        return call(
            functools.partial(rest_kernel, shard, plan),
            [chip_of_slot, cores, pinned(half), pinned(weights)],
            [SMEM] * 2 + [VMEM] * 2,
            [pltpu.VMEM((group, shard, WIN), jnp.float32 if keeps else jnp.bfloat16) for _, keeps in plan],
            [],
            {},
            total // 4 * width * WIN * 2,
        )

    def near_of(half):
        blocks = rest([(index * group, keeps) for keeps in (True, False) for index in range(len(far))], half)
        if lined:
            blocks = [block[0] for block in blocks]
        return blocks[: len(far)], blocks[len(far) :]

    far_keep = rest([(chips // 2 + index * group, True) for index in range(len(far))], half)

    factor = 1.0 / math.sqrt(owners * width)
    if lined:
        far_keep, far_send = [block[0] for block in far_keep], [block[0] for block in far_send]
        return collect(far_keep, far_send, near_of, half, swap) * factor
    near_keep, near_send = near_of(half)
    keep, send = [*near_keep, *far_keep], [*near_send, *far_send]
    keep, send = jnp.concatenate(keep), jnp.concatenate(send)
    pair_sum = (keep + move(send, swap).astype(jnp.float32)).astype(jnp.bfloat16)
    block_sum = lax.psum_scatter(
        pair_sum.reshape(total // 2, WIN), "aux", axis_index_groups=same_core, scatter_dimension=0, tiled=True
    )
    return block_sum.astype(jnp.float32) * factor


def solution(mesh):
    placed = (
        P(("groups", "aux"), None),
        P(("groups", "aux"), None),
        P(("groups", "aux")),
        P(("groups", "aux"), None),
    )
    return jax.shard_map(
        local, mesh=mesh, in_specs=placed, out_specs=P(("groups", "aux"), None), check_vma=False
    )
```

```python
import functools
import math

import jax
import jax.numpy as jnp
from jax import lax
from jax.experimental import pallas as pl
from jax.experimental.pallas import tpu as pltpu
from jax.sharding import PartitionSpec as P

BLK = 64
WIN = 128
LANES = 128
UNROLL = 16
LINE = 4
SCOPED_BYTES = 6 * 1024 * 1024


def place(z, x, core):
    return (z * 2 + x) * 2 + core


def pairs_of(step):
    return [
        (place(z, x, core), place(*step(z, x), core)) for z in range(LINE) for x in range(2) for core in range(2)
    ]


def tie(*arrays):
    return lax.optimization_barrier(arrays)


def move(array, pairs):
    return lax.ppermute(array, "aux", pairs)


ALONG = pairs_of(lambda z, x: ((z + 1) % LINE, x))
BACK = pairs_of(lambda z, x: ((z - 1) % LINE, x))
ACROSS = pairs_of(lambda z, x: (z, 1 - x))
ADD_AT = {(2, 1): 0, (3, 0): 1, (3, 1): 2}
LAY_AT = (1, 1)


def spread(parts, meanwhile):
    lines, others = [[part] for part in parts], [[] for _ in parts]

    def arrived(stage):
        held = [line[stage] for line in lines] if stage < LINE else []
        return held + ([other[stage - 1] for other in others] if stage else [])

    for step in range(LINE):
        for index, (line, other) in enumerate(zip(lines, others)):
            if other:
                line[-1], other[-1] = tie(line[-1], other[-1])
            turn = step == LINE - 1 and index == 0
            source = other if turn else line
            source[-1] = meanwhile(step, index, arrived, source[-1])
            now = source[-1]
            if step + 1 < LINE:
                line.append(move(now, ALONG))
            other.append(move(now, ALONG if turn else ACROSS))
    return [arrived(stage) for stage in range(LINE + 1)]


def collect(far_keep, far_send, near_of, half, swap):
    def paired(keep, send):
        return keep + move(send, swap).astype(jnp.float32)

    def halves(array):
        return array[: array.shape[0] // 2], array[array.shape[0] // 2 :]

    def narrow(array):
        return array.astype(jnp.bfloat16)

    def wide(array):
        return array.astype(jnp.float32)

    far = {step: paired(far_keep[step], far_send[step]) for step in (2, 1, 3, 0)}
    half, far[3], far[0], aside, *crossing = tie(half, far[3], far[0], narrow(far[1]), *map(narrow, halves(far[2])))
    crossed = {2: [move(part, ACROSS) for part in crossing]}
    joining = move(aside, ALONG)
    near_keep, near_send = near_of(half)
    near = {step: paired(near_keep[step], near_send[step]) for step in (2, 1, 3, 0)}
    crossing, crossed[2][1] = tie(narrow(far[3]), crossed[2][1])
    crossed[3] = move(crossing, ACROSS)
    crossing, crossed[3] = tie(narrow(far[0] + wide(joining)), crossed[3])
    crossed[0] = move(crossing, ACROSS)

    two_on = [move(narrow(own + wide(part)), ALONG) for own, part in zip(halves(near[2]), crossed[2])]
    later, two_on[0] = tie(near[1], two_on[0])
    one_on = [
        move(narrow(halves(own)[index] + wide(two_on[index])), ALONG) for index, own in enumerate((near[1], later))
    ]
    one_back = move(narrow(near[3] + wide(crossed[3])), BACK)
    return near[0] + wide(crossed[0]) + wide(one_back) + wide(jnp.concatenate(one_on))


def clear(half):
    whole = half.shape[0] // (4 * BLK) * (4 * BLK)

    @pl.loop(0, whole // (4 * BLK))
    def _(index):
        half[pl.ds(pl.multiple_of(index * 4 * BLK, BLK), 4 * BLK), :] = jnp.zeros((4 * BLK, LANES), jnp.float32)

    half[pl.ds(whole, half.shape[0] - whole), :] = jnp.zeros((half.shape[0] - whole, LANES), jnp.float32)


def add_tiles(stage, pieces, table_ref, bounds_ref, sources, tiles, half, occ, sem):
    rows = sources[0].shape[0]
    for index, source in enumerate(sources):
        pltpu.make_async_copy(source, occ.at[pl.ds(index * rows, rows)], sem).start()
    pltpu.make_async_copy(occ, occ, sem).wait()
    begin, end = bounds_ref[stage], bounds_ref[stage + 1]
    low = lax.broadcasted_iota(jnp.int32, tiles.shape[1:], 1) < BLK
    zero = jnp.zeros(tiles.shape[1:], jnp.bfloat16)
    spill = half.shape[0] - BLK
    entries = table_ref.shape[0] // (2 + pieces)
    piece = BLK // pieces

    @pl.loop(0, (end - begin + UNROLL - 1) // UNROLL)
    def _(group):
        products, starts = [], []
        for lane in range(UNROLL):
            entry = begin + group * UNROLL + lane
            tile = table_ref[entry]
            starts.append(jnp.where(entry < end, table_ref[entries + entry], spill))
            spots = [jnp.where(entry < end, table_ref[(2 + cut) * entries + entry], 0) for cut in range(pieces)]
            parts = [occ[pl.ds(pl.multiple_of(spot, piece), piece), :] for spot in spots]
            pair = tiles[tile]
            left = jnp.concatenate([jnp.where(low, pair, zero), jnp.where(low, zero, pair)], axis=0)
            block = jnp.concatenate(parts * 2, axis=0)
            products.append(jnp.dot(left, block, preferred_element_type=jnp.float32))
        for product, start in zip(products, starts):
            start = pl.multiple_of(start, BLK)
            for odd in range(2):
                span = pl.ds(start + odd, BLK // 2, stride=2)
                half[span, :] += product[odd * (BLK // 2) : (odd + 1) * (BLK // 2)]


def fill_window(half, weights, shard, chips_ref, first, parity, out):
    side_rows = (half.shape[0] - BLK) // 2

    @pl.loop(0, out.shape[0])
    def _(index):
        start = pl.multiple_of((2 * chips_ref[first + index] + parity) * shard, 32)
        both = jnp.concatenate(
            [half[pl.ds(side * side_rows + start, shard), :].astype(jnp.bfloat16) for side in range(2)], axis=1
        )
        out[index] = jnp.dot(both, weights[...], preferred_element_type=jnp.float32).astype(out.dtype)


def load_tiles(tile_sets, tiles, sems):
    slots = tile_sets[0].shape[0]
    copies = [
        pltpu.make_async_copy(source, tiles.at[pl.ds(index * slots, slots)], sems.at[index])
        for index, source in enumerate(tile_sets)
    ]
    for copy in copies:
        copy.start()
    return copies


def add_stage(stage, count, pieces, table_ref, bounds_ref, refs):
    sources = refs[:count]
    if stage:
        tiles, _, half, *outs, occ, sems = refs[count:]
        copies = []
    else:
        *tile_sets, half, tiles = refs[count : count + 4]
        *outs, occ, sems = refs[count + 4 :]
        copies = load_tiles(tile_sets, tiles, sems)
        clear(half)
    for copy in copies:
        copy.wait()
    add_tiles(stage, pieces, table_ref, bounds_ref, sources, tiles, half, occ, sems.at[2])
    return half, outs


def stage_kernel(stage, count, pieces, table_ref, bounds_ref, *refs):
    add_stage(stage, count, pieces, table_ref, bounds_ref, refs)


def window_kernel(stage, count, pieces, shard, first, table_ref, bounds_ref, chips_ref, core_ref, *refs):
    half, (weights, *outs) = add_stage(stage, count, pieces, table_ref, bounds_ref, refs)
    side_rows = (half.shape[0] - BLK) // 2
    for side in range(2):
        weights[pl.ds(side * LANES, LANES), :] = half[pl.ds(side * side_rows, WIN), :].T.astype(jnp.bfloat16)
    for index, out in enumerate(outs):
        fill_window(half, weights, shard, chips_ref, first + index * out.shape[0], 1 - core_ref[0], out)


def rest_kernel(shard, plan, chips_ref, core_ref, half, weights, *outs):
    for (first, keeps), out in zip(plan, outs):
        parity = core_ref[0] if keeps else 1 - core_ref[0]
        fill_window(half, weights, shard, chips_ref, first, parity, out)


SMEM = pl.BlockSpec(memory_space=pltpu.SMEM)
HBM = pl.BlockSpec(memory_space=pl.ANY)
VMEM = pl.BlockSpec(memory_space=pltpu.VMEM)


def pinned(array):
    return pltpu.with_memory_space_constraint(array, pltpu.VMEM)


def call(kernel, ins, in_specs, outs, scratch, aliases, flops, scoped=0):
    return pl.pallas_call(
        kernel,
        out_shape=outs,
        in_specs=in_specs,
        out_specs=[VMEM] * len(outs),
        scratch_shapes=scratch,
        input_output_aliases=aliases,
        compiler_params=pltpu.CompilerParams(vmem_limit_bytes=SCOPED_BYTES + scoped),
        cost_estimate=pl.CostEstimate(flops=flops, bytes_accessed=4 << 20, transcendentals=0),
    )(*ins)


def local(block_values, block_pairs, live_counts, occupied):
    owners = lax.axis_size("aux")
    me = lax.axis_index("aux")
    core, chip = me % 2, me // 2
    shard, width = occupied.shape
    total = owners * shard
    slots = block_values.shape[0]
    piece = math.gcd(BLK, shard)
    pieces = BLK // piece
    chips = owners // 2
    lined = chips == 2 * LINE
    same_core = [[2 * i + k for i in range(chips)] for k in range(2)]
    swap = [(i, i ^ 1) for i in range(owners)]

    mine = lax.dynamic_slice_in_dim(occupied, core * LANES, LANES, 1)
    given = lax.dynamic_slice_in_dim(occupied, (1 - core) * LANES, LANES, 1)
    parts = [mine, move(given, swap)]
    others = [move(array, swap) for array in (block_values, block_pairs, live_counts)]
    tile_sets = [values.reshape(slots, BLK * BLK // LANES, LANES) for values in (block_values, others[0])]

    slot_ids = jnp.arange(chips, dtype=jnp.int32)
    chip_of_slot = slot_ids
    stage_count = 1
    if lined:
        chip_of_slot = (slot_ids + chip // 2) % LINE * 2 + ((slot_ids // LINE) ^ (chip % 2))
        stage_count = LINE + 1

    tile_ids = jnp.arange(2 * slots, dtype=jnp.int32)
    pairs = jnp.concatenate([block_pairs, others[1]])
    live = tile_ids % slots < jnp.where(tile_ids < slots, live_counts[0], others[2][0])
    first = pairs[:, 1][:, None] * BLK + jnp.arange(pieces, dtype=jnp.int32) * piece
    owner = first // shard
    part = (owner % 2) ^ core
    owner_chip = owner // 2
    if lined:
        back = (chip // 2 - owner_chip // 2) % LINE
        side = (owner_chip % 2) ^ (chip % 2)
        stage = (back + side)[:, 0]
        slot_of = part + 2 * jnp.where(back + side < LINE, side, 0)
    else:
        stage = jnp.zeros_like(tile_ids)
        slot_of = part * chips + owner_chip
    spots = slot_of * shard + first % shard
    stage = jnp.where(live, stage, stage_count)
    rows = pairs[:, 0] * BLK + tile_ids // slots * total
    ahead = (stage[None, :] < stage[:, None]) | (
        (stage[None, :] == stage[:, None]) & (tile_ids[None, :] < tile_ids[:, None])
    )
    rank = jnp.sum(ahead.astype(jnp.int32), axis=1)
    entries = jnp.arange(2 * slots + UNROLL, dtype=jnp.int32)
    chosen = rank[None, :] == entries[:, None]
    columns = [tile_ids, rows] + [spots[:, cut] for cut in range(pieces)]
    ordered = jnp.concatenate([jnp.sum(jnp.where(chosen, column[None, :], 0), axis=1) for column in columns])
    bounds = jnp.sum((stage[None, :] < jnp.arange(stage_count + 1)[:, None]).astype(jnp.int32), axis=1)
    cores = core.astype(jnp.int32).reshape(1)

    half_type = pltpu.VMEM((2 * total + BLK, LANES), jnp.float32)
    tiles_type = pltpu.VMEM((2 * slots, BLK * BLK // LANES, LANES), jnp.bfloat16)
    work = 4 * slots * BLK * BLK * LANES // stage_count
    state = []

    def run_stage(kernel, sources, tables, outs, flops):
        rows = len(sources) * sources[0].shape[0]
        scratch = [pltpu.VMEM((rows, LANES), jnp.bfloat16), pltpu.SemaphoreType.DMA((3,))]
        ins, specs = [*tables, *sources], [SMEM] * len(tables) + [HBM] * len(sources)
        made, aliases = [half_type], {}
        if state:
            aliases = {len(ins) + 1: 0}
            ins, specs = ins + [pinned(state[1]), pinned(state[0])], specs + [VMEM] * 2
        else:
            ins, specs, made = ins + tile_sets, specs + [HBM] * 2, [half_type, tiles_type]
        results = call(kernel, ins, specs, made + outs, scratch, aliases, flops, 2 * rows * LANES)
        state[:] = [results[0], state[1] if state else results[1]]
        return results[len(made) :]

    def add(stage, sources):
        kernel = functools.partial(stage_kernel, stage, len(sources), pieces)
        run_stage(kernel, sources, [ordered, bounds], [], work)

    def meanwhile(step, index, arrived, moved):
        if (step, index) == LAY_AT:
            moved, *tile_sets[:] = tie(moved, *tile_sets)
        if (step, index) in ADD_AT:
            stage = ADD_AT[step, index]
            add(stage, arrived(stage))
            moved, state[0] = tie(moved, state[0])
        return moved

    if lined:
        stages = spread(parts, meanwhile)
        for stage in range(len(ADD_AT), LINE):
            add(stage, stages[stage])
    else:
        stages = [[lax.all_gather(part, "aux", axis_index_groups=same_core, axis=0, tiled=True) for part in parts]]

    group = 1 if lined else chips // 2
    far = [group] * (chips // 2 // group)
    weights, *far_send = run_stage(
        functools.partial(window_kernel, stage_count - 1, len(stages[-1]), pieces, shard, chips // 2),
        stages[-1],
        [ordered, bounds, chip_of_slot, cores],
        [pltpu.VMEM((2 * LANES, WIN), jnp.bfloat16)]
        + [pltpu.VMEM((size, shard, WIN), jnp.bfloat16) for size in far],
        work + total // 4 * width * WIN * 2,
    )
    half = state[0]

    def rest(plan, half):
        return call(
            functools.partial(rest_kernel, shard, plan),
            [chip_of_slot, cores, pinned(half), pinned(weights)],
            [SMEM] * 2 + [VMEM] * 2,
            [pltpu.VMEM((group, shard, WIN), jnp.float32 if keeps else jnp.bfloat16) for _, keeps in plan],
            [],
            {},
            total // 4 * width * WIN * 2,
        )

    def near_of(half):
        blocks = rest([(index * group, keeps) for keeps in (True, False) for index in range(len(far))], half)
        if lined:
            blocks = [block[0] for block in blocks]
        return blocks[: len(far)], blocks[len(far) :]

    far_keep = rest([(chips // 2 + index * group, True) for index in range(len(far))], half)

    factor = 1.0 / math.sqrt(owners * width)
    if lined:
        far_keep, far_send = [block[0] for block in far_keep], [block[0] for block in far_send]
        return collect(far_keep, far_send, near_of, half, swap) * factor
    near_keep, near_send = near_of(half)
    keep, send = [*near_keep, *far_keep], [*near_send, *far_send]
    keep, send = jnp.concatenate(keep), jnp.concatenate(send)
    pair_sum = (keep + move(send, swap).astype(jnp.float32)).astype(jnp.bfloat16)
    block_sum = lax.psum_scatter(
        pair_sum.reshape(total // 2, WIN), "aux", axis_index_groups=same_core, scatter_dimension=0, tiled=True
    )
    return block_sum.astype(jnp.float32) * factor


def solution(mesh):
    placed = (
        P(("groups", "aux"), None),
        P(("groups", "aux"), None),
        P(("groups", "aux")),
        P(("groups", "aux"), None),
    )
    return jax.shard_map(
        local, mesh=mesh, in_specs=placed, out_specs=P(("groups", "aux"), None), check_vma=False
    )
```

```python
import functools
import math

import jax
import jax.numpy as jnp
from jax import lax
from jax.experimental import pallas as pl
from jax.experimental.pallas import tpu as pltpu
from jax.sharding import PartitionSpec as P

BLK = 64
WIN = 128
LANES = 128
UNROLL = 16
LINE = 4
SCOPED_BYTES = 6 * 1024 * 1024


def place(z, x, core):
    return (z * 2 + x) * 2 + core


def pairs_of(step):
    return [
        (place(z, x, core), place(*step(z, x), core)) for z in range(LINE) for x in range(2) for core in range(2)
    ]


def tie(*arrays):
    return lax.optimization_barrier(arrays)


def move(array, pairs):
    return lax.ppermute(array, "aux", pairs)


ALONG = pairs_of(lambda z, x: ((z + 1) % LINE, x))
BACK = pairs_of(lambda z, x: ((z - 1) % LINE, x))
ACROSS = pairs_of(lambda z, x: (z, 1 - x))
NEAR0, NEAR1, NEAR2, NEAR3, FAR0, FAR1, FAR2, FAR3 = range(2 * LINE)
ADD_AT = {(2, 1): 0, (3, 0): 1, (3, 1): 2}
LAY_AT = (1, 1)


def spread(parts, meanwhile):
    lines, others = [[part] for part in parts], [[] for _ in parts]

    def arrived(stage):
        held = [line[stage] for line in lines] if stage < LINE else []
        return held + ([other[stage - 1] for other in others] if stage else [])

    for step in range(LINE):
        for index, (line, other) in enumerate(zip(lines, others)):
            if other:
                line[-1], other[-1] = tie(line[-1], other[-1])
            turn = step == LINE - 1 and index == 0
            source = other if turn else line
            source[-1] = meanwhile(step, index, arrived, source[-1])
            now = source[-1]
            if step + 1 < LINE:
                line.append(move(now, ALONG))
            other.append(move(now, ALONG if turn else ACROSS))
    return [arrived(stage) for stage in range(LINE + 1)]


def collect(blocks_of, swap):
    def halves(array):
        return array[: array.shape[0] // 2], array[array.shape[0] // 2 :]

    def narrow(array):
        return array.astype(jnp.bfloat16)

    def wide(array):
        return array.astype(jnp.float32)

    def paired(send, keep):
        return keep + wide(move(send, swap))

    first = [FAR2, FAR1, NEAR2]
    rest = [FAR3, NEAR1, FAR0, NEAR3, NEAR0]
    sends = blocks_of(first, False)
    total = {name: paired(*pair) for name, *pair in zip(first, sends, blocks_of(first, True))}
    crossing, aside = list(map(narrow, halves(total[FAR2]))), narrow(total[FAR1])
    *crossing, aside = blocks_of.hold(*crossing, aside)
    two_on = [move(part, ACROSS) for part in crossing]
    joining = move(aside, ALONG)
    total.update({name: paired(*pair) for name, *pair in zip(rest, blocks_of(rest, False), blocks_of(rest, True))})

    crossing, two_on[1] = tie(narrow(total[FAR3]), two_on[1])
    three_on = move(crossing, ACROSS)
    crossing, three_on = tie(narrow(total[FAR0] + wide(joining)), three_on)
    straight = move(crossing, ACROSS)
    two_on = [move(narrow(own + wide(part)), ALONG) for own, part in zip(halves(total[NEAR2]), two_on)]
    later, two_on[0] = tie(total[NEAR1], two_on[0])
    one_on = [
        move(narrow(halves(own)[index] + wide(two_on[index])), ALONG)
        for index, own in enumerate((total[NEAR1], later))
    ]
    one_back = move(narrow(total[NEAR3] + wide(three_on)), BACK)
    return total[NEAR0] + wide(straight) + wide(one_back) + wide(jnp.concatenate(one_on))


def clear(half):
    whole = half.shape[0] // (4 * BLK) * (4 * BLK)

    @pl.loop(0, whole // (4 * BLK))
    def _(index):
        half[pl.ds(pl.multiple_of(index * 4 * BLK, BLK), 4 * BLK), :] = jnp.zeros((4 * BLK, LANES), jnp.float32)

    half[pl.ds(whole, half.shape[0] - whole), :] = jnp.zeros((half.shape[0] - whole, LANES), jnp.float32)


def add_tiles(stage, pieces, table_ref, bounds_ref, sources, tiles, half, occ, sem):
    rows = sources[0].shape[0]
    for index, source in enumerate(sources):
        pltpu.make_async_copy(source, occ.at[pl.ds(index * rows, rows)], sem).start()
    pltpu.make_async_copy(occ, occ, sem).wait()
    begin, end = bounds_ref[stage], bounds_ref[stage + 1]
    low = lax.broadcasted_iota(jnp.int32, tiles.shape[1:], 1) < BLK
    zero = jnp.zeros(tiles.shape[1:], jnp.bfloat16)
    spill = half.shape[0] - BLK
    entries = table_ref.shape[0] // (2 + pieces)
    piece = BLK // pieces

    @pl.loop(0, (end - begin + UNROLL - 1) // UNROLL)
    def _(group):
        products, starts = [], []
        for lane in range(UNROLL):
            entry = begin + group * UNROLL + lane
            tile = table_ref[entry]
            starts.append(jnp.where(entry < end, table_ref[entries + entry], spill))
            spots = [jnp.where(entry < end, table_ref[(2 + cut) * entries + entry], 0) for cut in range(pieces)]
            parts = [occ[pl.ds(pl.multiple_of(spot, piece), piece), :] for spot in spots]
            pair = tiles[tile]
            left = jnp.concatenate([jnp.where(low, pair, zero), jnp.where(low, zero, pair)], axis=0)
            block = jnp.concatenate(parts * 2, axis=0)
            products.append(jnp.dot(left, block, preferred_element_type=jnp.float32))
        for product, start in zip(products, starts):
            start = pl.multiple_of(start, BLK)
            for odd in range(2):
                span = pl.ds(start + odd, BLK // 2, stride=2)
                half[span, :] += product[odd * (BLK // 2) : (odd + 1) * (BLK // 2)]


def fill_window(half, weights, shard, chips_ref, first, parity, out):
    side_rows = (half.shape[0] - BLK) // 2

    @pl.loop(0, out.shape[0])
    def _(index):
        start = pl.multiple_of((2 * chips_ref[first + index] + parity) * shard, 32)
        both = jnp.concatenate(
            [half[pl.ds(side * side_rows + start, shard), :].astype(jnp.bfloat16) for side in range(2)], axis=1
        )
        out[index] = jnp.dot(both, weights[...], preferred_element_type=jnp.float32).astype(out.dtype)


def load_tiles(tile_sets, tiles, sems):
    slots = tile_sets[0].shape[0]
    copies = [
        pltpu.make_async_copy(source, tiles.at[pl.ds(index * slots, slots)], sems.at[index])
        for index, source in enumerate(tile_sets)
    ]
    for copy in copies:
        copy.start()
    return copies


def add_stage(stage, count, pieces, table_ref, bounds_ref, refs):
    sources = refs[:count]
    if stage:
        tiles, _, half, *outs, occ, sems = refs[count:]
        copies = []
    else:
        *tile_sets, half, tiles = refs[count : count + 4]
        *outs, occ, sems = refs[count + 4 :]
        copies = load_tiles(tile_sets, tiles, sems)
        clear(half)
    for copy in copies:
        copy.wait()
    add_tiles(stage, pieces, table_ref, bounds_ref, sources, tiles, half, occ, sems.at[2])
    return half, outs


def stage_kernel(stage, count, pieces, table_ref, bounds_ref, *refs):
    add_stage(stage, count, pieces, table_ref, bounds_ref, refs)


def window_kernel(stage, count, pieces, shard, plan, table_ref, bounds_ref, chips_ref, core_ref, *refs):
    half, (weights, *outs) = add_stage(stage, count, pieces, table_ref, bounds_ref, refs)
    side_rows = (half.shape[0] - BLK) // 2
    for side in range(2):
        weights[pl.ds(side * LANES, LANES), :] = half[pl.ds(side * side_rows, WIN), :].T.astype(jnp.bfloat16)
    rest_kernel(shard, plan, False, chips_ref, core_ref, half, weights, *outs)


def rest_kernel(shard, plan, keeps, chips_ref, core_ref, half, weights, *outs):
    for first, out in zip(plan, outs):
        fill_window(half, weights, shard, chips_ref, first, core_ref[0] if keeps else 1 - core_ref[0], out)


SMEM = pl.BlockSpec(memory_space=pltpu.SMEM)
HBM = pl.BlockSpec(memory_space=pl.ANY)
VMEM = pl.BlockSpec(memory_space=pltpu.VMEM)


def pinned(array):
    return pltpu.with_memory_space_constraint(array, pltpu.VMEM)


def held(array):
    return pltpu.with_memory_space_constraint(array, pltpu.HBM)


def call(kernel, ins, in_specs, outs, scratch, aliases, flops, scoped=0):
    return pl.pallas_call(
        kernel,
        out_shape=outs,
        in_specs=in_specs,
        out_specs=[VMEM] * len(outs),
        scratch_shapes=scratch,
        input_output_aliases=aliases,
        compiler_params=pltpu.CompilerParams(vmem_limit_bytes=SCOPED_BYTES + scoped),
        cost_estimate=pl.CostEstimate(flops=flops, bytes_accessed=4 << 20, transcendentals=0),
    )(*ins)


def local(block_values, block_pairs, live_counts, occupied):
    owners = lax.axis_size("aux")
    me = lax.axis_index("aux")
    core, chip = me % 2, me // 2
    shard, width = occupied.shape
    total = owners * shard
    slots = block_values.shape[0]
    piece = math.gcd(BLK, shard)
    pieces = BLK // piece
    chips = owners // 2
    lined = chips == 2 * LINE
    same_core = [[2 * i + k for i in range(chips)] for k in range(2)]
    swap = [(i, i ^ 1) for i in range(owners)]

    mine = lax.dynamic_slice_in_dim(occupied, core * LANES, LANES, 1)
    given = lax.dynamic_slice_in_dim(occupied, (1 - core) * LANES, LANES, 1)
    parts = [mine, move(given, swap)]
    others = [move(array, swap) for array in (block_values, block_pairs, live_counts)]
    tile_sets = [values.reshape(slots, BLK * BLK // LANES, LANES) for values in (block_values, others[0])]

    slot_ids = jnp.arange(chips, dtype=jnp.int32)
    chip_of_slot = slot_ids
    stage_count = 1
    if lined:
        chip_of_slot = (slot_ids + chip // 2) % LINE * 2 + ((slot_ids // LINE) ^ (chip % 2))
        stage_count = LINE + 1

    tile_ids = jnp.arange(2 * slots, dtype=jnp.int32)
    pairs = jnp.concatenate([block_pairs, others[1]])
    live = tile_ids % slots < jnp.where(tile_ids < slots, live_counts[0], others[2][0])
    first = pairs[:, 1][:, None] * BLK + jnp.arange(pieces, dtype=jnp.int32) * piece
    owner = first // shard
    part = (owner % 2) ^ core
    owner_chip = owner // 2
    if lined:
        back = (chip // 2 - owner_chip // 2) % LINE
        side = (owner_chip % 2) ^ (chip % 2)
        stage = (back + side)[:, 0]
        slot_of = part + 2 * jnp.where(back + side < LINE, side, 0)
    else:
        stage = jnp.zeros_like(tile_ids)
        slot_of = part * chips + owner_chip
    spots = slot_of * shard + first % shard
    stage = jnp.where(live, stage, stage_count)
    rows = pairs[:, 0] * BLK + tile_ids // slots * total
    ahead = (stage[None, :] < stage[:, None]) | (
        (stage[None, :] == stage[:, None]) & (tile_ids[None, :] < tile_ids[:, None])
    )
    rank = jnp.sum(ahead.astype(jnp.int32), axis=1)
    entries = jnp.arange(2 * slots + UNROLL, dtype=jnp.int32)
    chosen = rank[None, :] == entries[:, None]
    columns = [tile_ids, rows] + [spots[:, cut] for cut in range(pieces)]
    ordered = jnp.concatenate([jnp.sum(jnp.where(chosen, column[None, :], 0), axis=1) for column in columns])
    bounds = jnp.sum((stage[None, :] < jnp.arange(stage_count + 1)[:, None]).astype(jnp.int32), axis=1)
    cores = core.astype(jnp.int32).reshape(1)

    half_type = pltpu.VMEM((2 * total + BLK, LANES), jnp.float32)
    tiles_type = pltpu.VMEM((2 * slots, BLK * BLK // LANES, LANES), jnp.bfloat16)
    work = 4 * slots * BLK * BLK * LANES // stage_count
    state = []

    def run_stage(kernel, sources, tables, outs, flops):
        rows = len(sources) * sources[0].shape[0]
        scratch = [pltpu.VMEM((rows, LANES), jnp.bfloat16), pltpu.SemaphoreType.DMA((3,))]
        ins, specs = [*tables, *sources], [SMEM] * len(tables) + [HBM] * len(sources)
        made, aliases = [half_type], {}
        if state:
            aliases = {len(ins) + 1: 0}
            ins, specs = ins + [pinned(state[1]), pinned(state[0])], specs + [VMEM] * 2
        else:
            ins, specs = [*tables, *map(held, sources), *map(held, tile_sets)], specs + [HBM] * 2
            made = [half_type, tiles_type]
        results = call(kernel, ins, specs, made + outs, scratch, aliases, flops, 2 * rows * LANES)
        state[:] = [results[0], state[1] if state else results[1]]
        return results[len(made) :]

    def add(stage, sources):
        kernel = functools.partial(stage_kernel, stage, len(sources), pieces)
        run_stage(kernel, sources, [ordered, bounds], [], work)

    def meanwhile(step, index, arrived, moved):
        if (step, index) == LAY_AT:
            moved, *tile_sets[:] = tie(moved, *tile_sets)
        if (step, index) in ADD_AT:
            stage = ADD_AT[step, index]
            add(stage, arrived(stage))
            moved, state[0] = tie(moved, state[0])
        return moved

    if lined:
        stages = spread(parts, meanwhile)
        for stage in range(len(ADD_AT), LINE):
            add(stage, stages[stage])
    else:
        stages = [[lax.all_gather(part, "aux", axis_index_groups=same_core, axis=0, tiled=True) for part in parts]]

    group = 1 if lined else chips

    def window_types(plan, keeps):
        return [pltpu.VMEM((group, shard, WIN), jnp.float32 if keeps else jnp.bfloat16) for _ in plan]

    def first_sends(plan):
        weights, *blocks = run_stage(
            functools.partial(window_kernel, stage_count - 1, len(stages[-1]), pieces, shard, plan),
            stages[-1],
            [ordered, bounds, chip_of_slot, cores],
            [pltpu.VMEM((2 * LANES, WIN), jnp.bfloat16)] + window_types(plan, False),
            work + len(plan) * group * shard * width * WIN * 2,
        )
        state.append(weights)
        return blocks

    def blocks_of(plan, keeps):
        if len(state) < 3:
            blocks = first_sends(plan)
        else:
            blocks = call(
                functools.partial(rest_kernel, shard, plan, keeps),
                [chip_of_slot, cores, pinned(state[0]), pinned(state[2])],
                [SMEM] * 2 + [VMEM] * 2,
                window_types(plan, keeps),
                [],
                {},
                len(plan) * group * shard * width * WIN * 2,
            )
        return [block[0] for block in blocks] if lined else blocks

    def hold(*arrays):
        state[0], *arrays = tie(state[0], *arrays)
        return arrays

    blocks_of.hold = hold
    factor = 1.0 / math.sqrt(owners * width)
    if lined:
        return collect(blocks_of, swap) * factor
    (send,), (keep,) = blocks_of([0], False), blocks_of([0], True)
    pair_sum = (keep + move(send, swap).astype(jnp.float32)).astype(jnp.bfloat16)
    block_sum = lax.psum_scatter(
        pair_sum.reshape(total // 2, WIN), "aux", axis_index_groups=same_core, scatter_dimension=0, tiled=True
    )
    return block_sum.astype(jnp.float32) * factor


def solution(mesh):
    placed = (
        P(("groups", "aux"), None),
        P(("groups", "aux"), None),
        P(("groups", "aux")),
        P(("groups", "aux"), None),
    )
    return jax.shard_map(
        local, mesh=mesh, in_specs=placed, out_specs=P(("groups", "aux"), None), check_vma=False
    )
```

```python
import functools
import math

import jax
import jax.numpy as jnp
from jax import lax
from jax.experimental import pallas as pl
from jax.experimental.pallas import tpu as pltpu
from jax.sharding import PartitionSpec as P

BLK = 64
WIN = 128
LANES = 128
UNROLL = 16
LINE = 4
SCOPED_BYTES = 6 * 1024 * 1024


def place(z, x, core):
    return (z * 2 + x) * 2 + core


def pairs_of(step):
    return [
        (place(z, x, core), place(*step(z, x), core)) for z in range(LINE) for x in range(2) for core in range(2)
    ]


def tie(*arrays):
    return lax.optimization_barrier(arrays)


def move(array, pairs):
    return lax.ppermute(array, "aux", pairs)


ALONG = pairs_of(lambda z, x: ((z + 1) % LINE, x))
BACK = pairs_of(lambda z, x: ((z - 1) % LINE, x))
ACROSS = pairs_of(lambda z, x: (z, 1 - x))
NEAR0, NEAR1, NEAR2, NEAR3, FAR0, FAR1, FAR2, FAR3 = range(2 * LINE)
ADD_AT = {(2, 1): 0, (3, 0): 1, (3, 1): 2}
LAY_AT = (1, 1)


def spread(parts, meanwhile):
    lines, others = [[part] for part in parts], [[] for _ in parts]

    def arrived(stage):
        held = [line[stage] for line in lines] if stage < LINE else []
        return held + ([other[stage - 1] for other in others] if stage else [])

    for step in range(LINE):
        for index, (line, other) in enumerate(zip(lines, others)):
            if other:
                line[-1], other[-1] = tie(line[-1], other[-1])
            turn = step == LINE - 1 and index == 0
            source = other if turn else line
            source[-1] = meanwhile(step, index, arrived, source[-1])
            now = source[-1]
            if step + 1 < LINE:
                line.append(move(now, ALONG))
            other.append(move(now, ALONG if turn else ACROSS))
    return [arrived(stage) for stage in range(LINE + 1)]


def collect(blocks_of, swap):
    def halves(array):
        return array[: array.shape[0] // 2], array[array.shape[0] // 2 :]

    def narrow(array):
        return array.astype(jnp.bfloat16)

    def wide(array):
        return array.astype(jnp.float32)

    def paired(send, keep):
        return keep + wide(move(send, swap))

    first = [FAR2, FAR1, NEAR2]
    rest = [FAR3, NEAR1, FAR0, NEAR3, NEAR0]
    sends = blocks_of(first, False)
    total = {name: paired(*pair) for name, *pair in zip(first, sends, blocks_of(first, True))}
    crossing, aside = list(map(narrow, halves(total[FAR2]))), narrow(total[FAR1])
    *crossing, aside = blocks_of.hold(*crossing, aside)
    two_on = [move(part, ACROSS) for part in crossing]
    joining = move(aside, ALONG)
    total.update({name: paired(*pair) for name, *pair in zip(rest, blocks_of(rest, False), blocks_of(rest, True))})

    two_on[0], joining = tie(two_on[0], joining)
    two_on = [move(narrow(own + wide(part)), ALONG) for own, part in zip(halves(total[NEAR2]), two_on)]
    crossing, two_on[0] = tie(narrow(total[FAR3]), two_on[0])
    three_on = move(crossing, ACROSS)
    later, two_on[0] = tie(total[NEAR1], two_on[0])
    one_on = [
        move(narrow(halves(own)[index] + wide(two_on[index])), ALONG)
        for index, own in enumerate((total[NEAR1], later))
    ]
    crossing, three_on = tie(narrow(total[FAR0] + wide(joining)), three_on)
    straight = move(crossing, ACROSS)
    one_back = move(narrow(total[NEAR3] + wide(three_on)), BACK)
    (result,) = tie(total[NEAR0] + wide(jnp.concatenate(one_on)))
    return result + wide(straight) + wide(one_back)


def clear(half):
    whole = half.shape[0] // (4 * BLK) * (4 * BLK)

    @pl.loop(0, whole // (4 * BLK))
    def _(index):
        half[pl.ds(pl.multiple_of(index * 4 * BLK, BLK), 4 * BLK), :] = jnp.zeros((4 * BLK, LANES), jnp.float32)

    half[pl.ds(whole, half.shape[0] - whole), :] = jnp.zeros((half.shape[0] - whole, LANES), jnp.float32)


def add_tiles(stage, pieces, table_ref, bounds_ref, sources, tiles, half, occ, sem):
    rows = sources[0].shape[0]
    for index, source in enumerate(sources):
        pltpu.make_async_copy(source, occ.at[pl.ds(index * rows, rows)], sem).start()
    pltpu.make_async_copy(occ, occ, sem).wait()
    begin, end = bounds_ref[stage], bounds_ref[stage + 1]
    low = lax.broadcasted_iota(jnp.int32, tiles.shape[1:], 1) < BLK
    zero = jnp.zeros(tiles.shape[1:], jnp.bfloat16)
    spill = half.shape[0] - BLK
    entries = table_ref.shape[0] // (2 + pieces)
    piece = BLK // pieces

    @pl.loop(0, (end - begin + UNROLL - 1) // UNROLL)
    def _(group):
        products, starts = [], []
        for lane in range(UNROLL):
            entry = begin + group * UNROLL + lane
            tile = table_ref[entry]
            starts.append(jnp.where(entry < end, table_ref[entries + entry], spill))
            spots = [jnp.where(entry < end, table_ref[(2 + cut) * entries + entry], 0) for cut in range(pieces)]
            parts = [occ[pl.ds(pl.multiple_of(spot, piece), piece), :] for spot in spots]
            pair = tiles[tile]
            left = jnp.concatenate([jnp.where(low, pair, zero), jnp.where(low, zero, pair)], axis=0)
            block = jnp.concatenate(parts * 2, axis=0)
            products.append(jnp.dot(left, block, preferred_element_type=jnp.float32))
        for product, start in zip(products, starts):
            start = pl.multiple_of(start, BLK)
            for odd in range(2):
                span = pl.ds(start + odd, BLK // 2, stride=2)
                half[span, :] += product[odd * (BLK // 2) : (odd + 1) * (BLK // 2)]


def fill_window(half, weights, shard, chips_ref, first, parity, out):
    side_rows = (half.shape[0] - BLK) // 2

    @pl.loop(0, out.shape[0])
    def _(index):
        start = pl.multiple_of((2 * chips_ref[first + index] + parity) * shard, 32)
        both = jnp.concatenate(
            [half[pl.ds(side * side_rows + start, shard), :].astype(jnp.bfloat16) for side in range(2)], axis=1
        )
        out[index] = jnp.dot(both, weights[...], preferred_element_type=jnp.float32).astype(out.dtype)


def load_tiles(tile_sets, tiles, sems):
    slots = tile_sets[0].shape[0]
    copies = [
        pltpu.make_async_copy(source, tiles.at[pl.ds(index * slots, slots)], sems.at[index])
        for index, source in enumerate(tile_sets)
    ]
    for copy in copies:
        copy.start()
    return copies


def add_stage(stage, count, pieces, table_ref, bounds_ref, refs):
    sources = refs[:count]
    if stage:
        tiles, _, half, *outs, occ, sems = refs[count:]
        copies = []
    else:
        *tile_sets, half, tiles = refs[count : count + 4]
        *outs, occ, sems = refs[count + 4 :]
        copies = load_tiles(tile_sets, tiles, sems)
        clear(half)
    for copy in copies:
        copy.wait()
    add_tiles(stage, pieces, table_ref, bounds_ref, sources, tiles, half, occ, sems.at[2])
    return half, outs


def stage_kernel(stage, count, pieces, table_ref, bounds_ref, *refs):
    add_stage(stage, count, pieces, table_ref, bounds_ref, refs)


def window_kernel(stage, count, pieces, shard, plan, table_ref, bounds_ref, chips_ref, core_ref, *refs):
    half, (weights, *outs) = add_stage(stage, count, pieces, table_ref, bounds_ref, refs)
    side_rows = (half.shape[0] - BLK) // 2
    for side in range(2):
        weights[pl.ds(side * LANES, LANES), :] = half[pl.ds(side * side_rows, WIN), :].T.astype(jnp.bfloat16)
    rest_kernel(shard, plan, False, chips_ref, core_ref, half, weights, *outs)


def rest_kernel(shard, plan, keeps, chips_ref, core_ref, half, weights, *outs):
    for first, out in zip(plan, outs):
        fill_window(half, weights, shard, chips_ref, first, core_ref[0] if keeps else 1 - core_ref[0], out)


SMEM = pl.BlockSpec(memory_space=pltpu.SMEM)
HBM = pl.BlockSpec(memory_space=pl.ANY)
VMEM = pl.BlockSpec(memory_space=pltpu.VMEM)


def pinned(array):
    return pltpu.with_memory_space_constraint(array, pltpu.VMEM)


def held(array):
    return pltpu.with_memory_space_constraint(array, pltpu.HBM)


def call(kernel, ins, in_specs, outs, scratch, aliases, flops, scoped=0):
    return pl.pallas_call(
        kernel,
        out_shape=outs,
        in_specs=in_specs,
        out_specs=[VMEM] * len(outs),
        scratch_shapes=scratch,
        input_output_aliases=aliases,
        compiler_params=pltpu.CompilerParams(vmem_limit_bytes=SCOPED_BYTES + scoped),
        cost_estimate=pl.CostEstimate(flops=flops, bytes_accessed=4 << 20, transcendentals=0),
    )(*ins)


def local(block_values, block_pairs, live_counts, occupied):
    owners = lax.axis_size("aux")
    me = lax.axis_index("aux")
    core, chip = me % 2, me // 2
    shard, width = occupied.shape
    total = owners * shard
    slots = block_values.shape[0]
    piece = math.gcd(BLK, shard)
    pieces = BLK // piece
    chips = owners // 2
    lined = chips == 2 * LINE
    same_core = [[2 * i + k for i in range(chips)] for k in range(2)]
    swap = [(i, i ^ 1) for i in range(owners)]

    mine = lax.dynamic_slice_in_dim(occupied, core * LANES, LANES, 1)
    given = lax.dynamic_slice_in_dim(occupied, (1 - core) * LANES, LANES, 1)
    parts = [mine, move(given, swap)]
    others = [move(array, swap) for array in (block_values, block_pairs, live_counts)]
    tile_sets = [values.reshape(slots, BLK * BLK // LANES, LANES) for values in (block_values, others[0])]

    slot_ids = jnp.arange(chips, dtype=jnp.int32)
    chip_of_slot = slot_ids
    stage_count = 1
    if lined:
        chip_of_slot = (slot_ids + chip // 2) % LINE * 2 + ((slot_ids // LINE) ^ (chip % 2))
        stage_count = LINE + 1

    tile_ids = jnp.arange(2 * slots, dtype=jnp.int32)
    pairs = jnp.concatenate([block_pairs, others[1]])
    live = tile_ids % slots < jnp.where(tile_ids < slots, live_counts[0], others[2][0])
    first = pairs[:, 1][:, None] * BLK + jnp.arange(pieces, dtype=jnp.int32) * piece
    owner = first // shard
    part = (owner % 2) ^ core
    owner_chip = owner // 2
    if lined:
        back = (chip // 2 - owner_chip // 2) % LINE
        side = (owner_chip % 2) ^ (chip % 2)
        stage = (back + side)[:, 0]
        slot_of = part + 2 * jnp.where(back + side < LINE, side, 0)
    else:
        stage = jnp.zeros_like(tile_ids)
        slot_of = part * chips + owner_chip
    spots = slot_of * shard + first % shard
    stage = jnp.where(live, stage, stage_count)
    rows = pairs[:, 0] * BLK + tile_ids // slots * total
    ahead = (stage[None, :] < stage[:, None]) | (
        (stage[None, :] == stage[:, None]) & (tile_ids[None, :] < tile_ids[:, None])
    )
    rank = jnp.sum(ahead.astype(jnp.int32), axis=1)
    entries = jnp.arange(2 * slots + UNROLL, dtype=jnp.int32)
    chosen = rank[None, :] == entries[:, None]
    columns = [tile_ids, rows] + [spots[:, cut] for cut in range(pieces)]
    ordered = jnp.concatenate([jnp.sum(jnp.where(chosen, column[None, :], 0), axis=1) for column in columns])
    bounds = jnp.sum((stage[None, :] < jnp.arange(stage_count + 1)[:, None]).astype(jnp.int32), axis=1)
    cores = core.astype(jnp.int32).reshape(1)

    half_type = pltpu.VMEM((2 * total + BLK, LANES), jnp.float32)
    tiles_type = pltpu.VMEM((2 * slots, BLK * BLK // LANES, LANES), jnp.bfloat16)
    work = 4 * slots * BLK * BLK * LANES // stage_count
    state = []

    def run_stage(kernel, sources, tables, outs, flops):
        rows = len(sources) * sources[0].shape[0]
        scratch = [pltpu.VMEM((rows, LANES), jnp.bfloat16), pltpu.SemaphoreType.DMA((3,))]
        ins, specs = [*tables, *sources], [SMEM] * len(tables) + [HBM] * len(sources)
        made, aliases = [half_type], {}
        if state:
            aliases = {len(ins) + 1: 0}
            ins, specs = ins + [pinned(state[1]), pinned(state[0])], specs + [VMEM] * 2
        else:
            ins, specs = [*tables, *map(held, sources), *map(held, tile_sets)], specs + [HBM] * 2
            made = [half_type, tiles_type]
        results = call(kernel, ins, specs, made + outs, scratch, aliases, flops, 2 * rows * LANES)
        state[:] = [results[0], state[1] if state else results[1]]
        return results[len(made) :]

    def add(stage, sources):
        kernel = functools.partial(stage_kernel, stage, len(sources), pieces)
        run_stage(kernel, sources, [ordered, bounds], [], work)

    def meanwhile(step, index, arrived, moved):
        if (step, index) == LAY_AT:
            moved, *tile_sets[:] = tie(moved, *tile_sets)
        if (step, index) in ADD_AT:
            stage = ADD_AT[step, index]
            add(stage, arrived(stage))
            moved, state[0] = tie(moved, state[0])
        return moved

    if lined:
        stages = spread(parts, meanwhile)
        for stage in range(len(ADD_AT), LINE):
            add(stage, stages[stage])
    else:
        stages = [[lax.all_gather(part, "aux", axis_index_groups=same_core, axis=0, tiled=True) for part in parts]]

    group = 1 if lined else chips

    def window_types(plan, keeps):
        return [pltpu.VMEM((group, shard, WIN), jnp.float32 if keeps else jnp.bfloat16) for _ in plan]

    def first_sends(plan):
        weights, *blocks = run_stage(
            functools.partial(window_kernel, stage_count - 1, len(stages[-1]), pieces, shard, plan),
            stages[-1],
            [ordered, bounds, chip_of_slot, cores],
            [pltpu.VMEM((2 * LANES, WIN), jnp.bfloat16)] + window_types(plan, False),
            work + len(plan) * group * shard * width * WIN * 2,
        )
        state.append(weights)
        return blocks

    def blocks_of(plan, keeps):
        if len(state) < 3:
            blocks = first_sends(plan)
        else:
            blocks = call(
                functools.partial(rest_kernel, shard, plan, keeps),
                [chip_of_slot, cores, pinned(state[0]), pinned(state[2])],
                [SMEM] * 2 + [VMEM] * 2,
                window_types(plan, keeps),
                [],
                {},
                len(plan) * group * shard * width * WIN * 2,
            )
        return [block[0] for block in blocks] if lined else blocks

    def hold(*arrays):
        state[0], *arrays = tie(state[0], *arrays)
        return arrays

    blocks_of.hold = hold
    factor = 1.0 / math.sqrt(owners * width)
    if lined:
        return collect(blocks_of, swap) * factor
    (send,), (keep,) = blocks_of([0], False), blocks_of([0], True)
    pair_sum = (keep + move(send, swap).astype(jnp.float32)).astype(jnp.bfloat16)
    block_sum = lax.psum_scatter(
        pair_sum.reshape(total // 2, WIN), "aux", axis_index_groups=same_core, scatter_dimension=0, tiled=True
    )
    return block_sum.astype(jnp.float32) * factor


def solution(mesh):
    placed = (
        P(("groups", "aux"), None),
        P(("groups", "aux"), None),
        P(("groups", "aux")),
        P(("groups", "aux"), None),
    )
    return jax.shard_map(
        local, mesh=mesh, in_specs=placed, out_specs=P(("groups", "aux"), None), check_vma=False
    )
```

```python
import functools
import math

import jax
import jax.numpy as jnp
from jax import lax
from jax.experimental import pallas as pl
from jax.experimental.pallas import tpu as pltpu
from jax.sharding import PartitionSpec as P

BLK = 64
WIN = 128
LANES = 128
UNROLL = 16
LINE = 4
SCOPED_BYTES = 6 * 1024 * 1024


def place(z, x, core):
    return (z * 2 + x) * 2 + core


def pairs_of(step):
    return [
        (place(z, x, core), place(*step(z, x), core)) for z in range(LINE) for x in range(2) for core in range(2)
    ]


def tie(*arrays):
    return lax.optimization_barrier(arrays)


def move(array, pairs):
    return lax.ppermute(array, "aux", pairs)


ALONG = pairs_of(lambda z, x: ((z + 1) % LINE, x))
BACK = pairs_of(lambda z, x: ((z - 1) % LINE, x))
ACROSS = pairs_of(lambda z, x: (z, 1 - x))
NEAR0, NEAR1, NEAR2, NEAR3, FAR0, FAR1, FAR2, FAR3 = range(2 * LINE)
ADD_AT = {(2, 1): 0, (3, 0): 1, (3, 1): 2}
RAW_AT, LAY_AT = (0, 1), (1, 1)


def spread(parts, meanwhile):
    lines, others = [[part] for part in parts], [[] for _ in parts]

    def arrived(stage):
        held = [line[stage] for line in lines] if stage < LINE else []
        return held + ([other[stage - 1] for other in others] if stage else [])

    for step in range(LINE):
        for index, (line, other) in enumerate(zip(lines, others)):
            if other:
                line[-1], other[-1] = tie(line[-1], other[-1])
            turn = step == LINE - 1 and index == 0
            source = other if turn else line
            source[-1] = meanwhile(step, index, arrived, source[-1])
            now = source[-1]
            if step + 1 < LINE:
                line.append(move(now, ALONG))
            other.append(move(now, ALONG if turn else ACROSS))
    return [arrived(stage) for stage in range(LINE + 1)]


def collect(blocks_of, swap):
    def halves(array):
        return array[: array.shape[0] // 2], array[array.shape[0] // 2 :]

    def narrow(array):
        return array.astype(jnp.bfloat16)

    def wide(array):
        return array.astype(jnp.float32)

    def paired(send, keep):
        return keep + wide(move(send, swap))

    first = [FAR2, FAR1, NEAR2]
    rest = [FAR3, NEAR1, FAR0, NEAR3, NEAR0]
    sends = blocks_of(first, False)
    total = {name: paired(*pair) for name, *pair in zip(first, sends, blocks_of(first, True))}
    crossing, aside = list(map(narrow, halves(total[FAR2]))), narrow(total[FAR1])
    *crossing, aside = blocks_of.hold(*crossing, aside)
    two_on = [move(part, ACROSS) for part in crossing]
    joining = move(aside, ALONG)
    total.update({name: paired(*pair) for name, *pair in zip(rest, blocks_of(rest, False), blocks_of(rest, True))})

    crossing, two_on[1] = tie(narrow(total[FAR3]), two_on[1])
    three_on = move(crossing, ACROSS)
    crossing, three_on = tie(narrow(total[FAR0] + wide(joining)), three_on)
    straight = move(crossing, ACROSS)
    two_on = [move(narrow(own + wide(part)), ALONG) for own, part in zip(halves(total[NEAR2]), two_on)]
    later, two_on[0] = tie(total[NEAR1], two_on[0])
    one_on = [
        move(narrow(halves(own)[index] + wide(two_on[index])), ALONG)
        for index, own in enumerate((total[NEAR1], later))
    ]
    one_back = move(narrow(total[NEAR3] + wide(three_on)), BACK)
    (result,) = tie(total[NEAR0] + wide(jnp.concatenate(one_on)))
    return result + wide(straight) + wide(one_back)


def clear(half):
    whole = half.shape[0] // (4 * BLK) * (4 * BLK)

    @pl.loop(0, whole // (4 * BLK))
    def _(index):
        half[pl.ds(pl.multiple_of(index * 4 * BLK, BLK), 4 * BLK), :] = jnp.zeros((4 * BLK, LANES), jnp.float32)

    half[pl.ds(whole, half.shape[0] - whole), :] = jnp.zeros((half.shape[0] - whole, LANES), jnp.float32)


def add_tiles(stage, pieces, table_ref, bounds_ref, sources, tiles, half, occ, sem):
    rows = sources[0].shape[0]
    for index, source in enumerate(sources):
        pltpu.make_async_copy(source, occ.at[pl.ds(index * rows, rows)], sem).start()
    pltpu.make_async_copy(occ, occ, sem).wait()
    begin, end = bounds_ref[stage], bounds_ref[stage + 1]
    low = lax.broadcasted_iota(jnp.int32, tiles.shape[1:], 1) < BLK
    zero = jnp.zeros(tiles.shape[1:], jnp.bfloat16)
    spill = half.shape[0] - BLK
    entries = table_ref.shape[0] // (2 + pieces)
    piece = BLK // pieces

    @pl.loop(0, (end - begin + UNROLL - 1) // UNROLL)
    def _(group):
        products, starts = [], []
        for lane in range(UNROLL):
            entry = begin + group * UNROLL + lane
            tile = table_ref[entry]
            starts.append(jnp.where(entry < end, table_ref[entries + entry], spill))
            spots = [jnp.where(entry < end, table_ref[(2 + cut) * entries + entry], 0) for cut in range(pieces)]
            parts = [occ[pl.ds(pl.multiple_of(spot, piece), piece), :] for spot in spots]
            pair = tiles[tile]
            left = jnp.concatenate([jnp.where(low, pair, zero), jnp.where(low, zero, pair)], axis=0)
            block = jnp.concatenate(parts * 2, axis=0)
            products.append(jnp.dot(left, block, preferred_element_type=jnp.float32))
        for product, start in zip(products, starts):
            start = pl.multiple_of(start, BLK)
            for odd in range(2):
                span = pl.ds(start + odd, BLK // 2, stride=2)
                half[span, :] += product[odd * (BLK // 2) : (odd + 1) * (BLK // 2)]


def fill_window(half, weights, shard, chips_ref, first, parity, out):
    side_rows = (half.shape[0] - BLK) // 2

    @pl.loop(0, out.shape[0])
    def _(index):
        start = pl.multiple_of((2 * chips_ref[first + index] + parity) * shard, 32)
        both = jnp.concatenate(
            [half[pl.ds(side * side_rows + start, shard), :].astype(jnp.bfloat16) for side in range(2)], axis=1
        )
        out[index] = jnp.dot(both, weights[...], preferred_element_type=jnp.float32).astype(out.dtype)


def load_tiles(tile_sets, tiles, sems):
    slots = tile_sets[0].shape[0]
    copies = [
        pltpu.make_async_copy(source, tiles.at[pl.ds(index * slots, slots)], sems.at[index])
        for index, source in enumerate(tile_sets)
    ]
    for copy in copies:
        copy.start()
    return copies


def add_stage(stage, count, pieces, table_ref, bounds_ref, refs):
    sources = refs[:count]
    if stage:
        tiles, _, half, *outs, occ, sems = refs[count:]
        copies = []
    else:
        *tile_sets, half, tiles = refs[count : count + 4]
        *outs, occ, sems = refs[count + 4 :]
        copies = load_tiles(tile_sets, tiles, sems)
        clear(half)
    for copy in copies:
        copy.wait()
    add_tiles(stage, pieces, table_ref, bounds_ref, sources, tiles, half, occ, sems.at[2])
    return half, outs


def stage_kernel(stage, count, pieces, table_ref, bounds_ref, *refs):
    add_stage(stage, count, pieces, table_ref, bounds_ref, refs)


def window_kernel(stage, count, pieces, shard, plan, table_ref, bounds_ref, chips_ref, core_ref, *refs):
    half, (weights, *outs) = add_stage(stage, count, pieces, table_ref, bounds_ref, refs)
    side_rows = (half.shape[0] - BLK) // 2
    for side in range(2):
        weights[pl.ds(side * LANES, LANES), :] = half[pl.ds(side * side_rows, WIN), :].T.astype(jnp.bfloat16)
    rest_kernel(shard, plan, False, chips_ref, core_ref, half, weights, *outs)


def rest_kernel(shard, plan, keeps, chips_ref, core_ref, half, weights, *outs):
    for first, out in zip(plan, outs):
        fill_window(half, weights, shard, chips_ref, first, core_ref[0] if keeps else 1 - core_ref[0], out)


SMEM = pl.BlockSpec(memory_space=pltpu.SMEM)
HBM = pl.BlockSpec(memory_space=pl.ANY)
VMEM = pl.BlockSpec(memory_space=pltpu.VMEM)


def pinned(array):
    return pltpu.with_memory_space_constraint(array, pltpu.VMEM)


def call(kernel, ins, in_specs, outs, scratch, aliases, flops, scoped=0):
    return pl.pallas_call(
        kernel,
        out_shape=outs,
        in_specs=in_specs,
        out_specs=[VMEM] * len(outs),
        scratch_shapes=scratch,
        input_output_aliases=aliases,
        compiler_params=pltpu.CompilerParams(vmem_limit_bytes=SCOPED_BYTES + scoped),
        cost_estimate=pl.CostEstimate(flops=flops, bytes_accessed=4 << 20, transcendentals=0),
    )(*ins)


def local(block_values, block_pairs, live_counts, occupied):
    owners = lax.axis_size("aux")
    me = lax.axis_index("aux")
    core, chip = me % 2, me // 2
    shard, width = occupied.shape
    total = owners * shard
    slots = block_values.shape[0]
    piece = math.gcd(BLK, shard)
    pieces = BLK // piece
    chips = owners // 2
    lined = chips == 2 * LINE
    same_core = [[2 * i + k for i in range(chips)] for k in range(2)]
    swap = [(i, i ^ 1) for i in range(owners)]

    mine = lax.dynamic_slice_in_dim(occupied, core * LANES, LANES, 1)
    given = lax.dynamic_slice_in_dim(occupied, (1 - core) * LANES, LANES, 1)
    parts = [mine, move(given, swap)]
    others = [move(array, swap) for array in (block_values, block_pairs, live_counts)]
    raw_sets = [block_values, others[0]]
    tile_sets = []

    def lay_tiles():
        tile_sets[:] = [values.reshape(slots, BLK * BLK // LANES, LANES) for values in raw_sets]

    slot_ids = jnp.arange(chips, dtype=jnp.int32)
    chip_of_slot = slot_ids
    stage_count = 1
    if lined:
        chip_of_slot = (slot_ids + chip // 2) % LINE * 2 + ((slot_ids // LINE) ^ (chip % 2))
        stage_count = LINE + 1

    tile_ids = jnp.arange(2 * slots, dtype=jnp.int32)
    pairs = jnp.concatenate([block_pairs, others[1]])
    live = tile_ids % slots < jnp.where(tile_ids < slots, live_counts[0], others[2][0])
    first = pairs[:, 1][:, None] * BLK + jnp.arange(pieces, dtype=jnp.int32) * piece
    owner = first // shard
    part = (owner % 2) ^ core
    owner_chip = owner // 2
    if lined:
        back = (chip // 2 - owner_chip // 2) % LINE
        side = (owner_chip % 2) ^ (chip % 2)
        stage = (back + side)[:, 0]
        slot_of = part + 2 * jnp.where(back + side < LINE, side, 0)
    else:
        stage = jnp.zeros_like(tile_ids)
        slot_of = part * chips + owner_chip
    spots = slot_of * shard + first % shard
    stage = jnp.where(live, stage, stage_count)
    rows = pairs[:, 0] * BLK + tile_ids // slots * total
    ahead = (stage[None, :] < stage[:, None]) | (
        (stage[None, :] == stage[:, None]) & (tile_ids[None, :] < tile_ids[:, None])
    )
    rank = jnp.sum(ahead.astype(jnp.int32), axis=1)
    entries = jnp.arange(2 * slots + UNROLL, dtype=jnp.int32)
    chosen = rank[None, :] == entries[:, None]
    columns = [tile_ids, rows] + [spots[:, cut] for cut in range(pieces)]
    ordered = jnp.concatenate([jnp.sum(jnp.where(chosen, column[None, :], 0), axis=1) for column in columns])
    bounds = jnp.sum((stage[None, :] < jnp.arange(stage_count + 1)[:, None]).astype(jnp.int32), axis=1)
    cores = core.astype(jnp.int32).reshape(1)

    half_type = pltpu.VMEM((2 * total + BLK, LANES), jnp.float32)
    tiles_type = pltpu.VMEM((2 * slots, BLK * BLK // LANES, LANES), jnp.bfloat16)
    work = 4 * slots * BLK * BLK * LANES // stage_count
    state = []

    def run_stage(kernel, sources, tables, outs, flops):
        rows = len(sources) * sources[0].shape[0]
        scratch = [pltpu.VMEM((rows, LANES), jnp.bfloat16), pltpu.SemaphoreType.DMA((3,))]
        ins, specs = [*tables, *sources], [SMEM] * len(tables) + [HBM] * len(sources)
        made, aliases = [half_type], {}
        if state:
            aliases = {len(ins) + 1: 0}
            ins, specs = ins + [pinned(state[1]), pinned(state[0])], specs + [VMEM] * 2
        else:
            ins, specs = [*tables, *sources, *tile_sets], specs + [HBM] * 2
            made = [half_type, tiles_type]
        results = call(kernel, ins, specs, made + outs, scratch, aliases, flops, 2 * rows * LANES)
        state[:] = [results[0], state[1] if state else results[1]]
        return results[len(made) :]

    def add(stage, sources):
        kernel = functools.partial(stage_kernel, stage, len(sources), pieces)
        run_stage(kernel, sources, [ordered, bounds], [], work)

    def meanwhile(step, index, arrived, moved):
        if (step, index) == RAW_AT:
            moved, *raw_sets[:] = tie(moved, *raw_sets)
            lay_tiles()
        if (step, index) == LAY_AT:
            moved, *tile_sets[:] = tie(moved, *tile_sets)
        if (step, index) in ADD_AT:
            stage = ADD_AT[step, index]
            add(stage, arrived(stage))
            moved, state[0] = tie(moved, state[0])
        return moved

    if lined:
        stages = spread(parts, meanwhile)
        for stage in range(len(ADD_AT), LINE):
            add(stage, stages[stage])
    else:
        lay_tiles()
        stages = [[lax.all_gather(part, "aux", axis_index_groups=same_core, axis=0, tiled=True) for part in parts]]

    group = 1 if lined else chips

    def window_types(plan, keeps):
        return [pltpu.VMEM((group, shard, WIN), jnp.float32 if keeps else jnp.bfloat16) for _ in plan]

    def first_sends(plan):
        weights, *blocks = run_stage(
            functools.partial(window_kernel, stage_count - 1, len(stages[-1]), pieces, shard, plan),
            stages[-1],
            [ordered, bounds, chip_of_slot, cores],
            [pltpu.VMEM((2 * LANES, WIN), jnp.bfloat16)] + window_types(plan, False),
            work + len(plan) * group * shard * width * WIN * 2,
        )
        state.append(weights)
        return blocks

    def blocks_of(plan, keeps):
        if len(state) < 3:
            blocks = first_sends(plan)
        else:
            blocks = call(
                functools.partial(rest_kernel, shard, plan, keeps),
                [chip_of_slot, cores, pinned(state[0]), pinned(state[2])],
                [SMEM] * 2 + [VMEM] * 2,
                window_types(plan, keeps),
                [],
                {},
                len(plan) * group * shard * width * WIN * 2,
            )
        return [block[0] for block in blocks] if lined else blocks

    def hold(*arrays):
        state[0], *arrays = tie(state[0], *arrays)
        return arrays

    blocks_of.hold = hold
    factor = 1.0 / math.sqrt(owners * width)
    if lined:
        return collect(blocks_of, swap) * factor
    (send,), (keep,) = blocks_of([0], False), blocks_of([0], True)
    pair_sum = (keep + move(send, swap).astype(jnp.float32)).astype(jnp.bfloat16)
    block_sum = lax.psum_scatter(
        pair_sum.reshape(total // 2, WIN), "aux", axis_index_groups=same_core, scatter_dimension=0, tiled=True
    )
    return block_sum.astype(jnp.float32) * factor


def solution(mesh):
    placed = (
        P(("groups", "aux"), None),
        P(("groups", "aux"), None),
        P(("groups", "aux")),
        P(("groups", "aux"), None),
    )
    return jax.shard_map(
        local, mesh=mesh, in_specs=placed, out_specs=P(("groups", "aux"), None), check_vma=False
    )
```

```python
import functools
import math

import jax
import jax.numpy as jnp
from jax import lax
from jax.experimental import pallas as pl
from jax.experimental.pallas import tpu as pltpu
from jax.sharding import PartitionSpec as P

BLK = 64
WIN = 128
LANES = 128
UNROLL = 16
LINE = 4
SCOPED_BYTES = 6 * 1024 * 1024


def place(z, x, core):
    return (z * 2 + x) * 2 + core


def pairs_of(step):
    return [
        (place(z, x, core), place(*step(z, x), core)) for z in range(LINE) for x in range(2) for core in range(2)
    ]


def tie(*arrays):
    return lax.optimization_barrier(arrays)


def move(array, pairs):
    return lax.ppermute(array, "aux", pairs)


ALONG = pairs_of(lambda z, x: ((z + 1) % LINE, x))
BACK = pairs_of(lambda z, x: ((z - 1) % LINE, x))
ACROSS = pairs_of(lambda z, x: (z, 1 - x))
NEAR0, NEAR1, NEAR2, NEAR3, FAR0, FAR1, FAR2, FAR3 = range(2 * LINE)
ADD_AT = {(2, 1): 0, (3, 0): 1}
RAW_AT, LAY_AT = (0, 1), (1, 1)


def spread(parts, meanwhile):
    lines, others = [[part] for part in parts], [[] for _ in parts]

    def arrived(stage):
        held = [line[stage] for line in lines] if stage < LINE else []
        return held + ([other[stage - 1] for other in others] if stage else [])

    for step in range(LINE):
        for index, (line, other) in enumerate(zip(lines, others)):
            if other:
                line[-1], other[-1] = tie(line[-1], other[-1])
            turn = step == LINE - 1 and index == 0
            source = other if turn else line
            source[-1] = meanwhile(step, index, arrived, source[-1])
            now = source[-1]
            if step + 1 < LINE:
                line.append(move(now, ALONG))
            other.append(move(now, ALONG if turn else ACROSS))
    return [arrived(stage) for stage in range(LINE + 1)]


def collect(blocks_of, swap):
    def halves(array):
        return array[: array.shape[0] // 2], array[array.shape[0] // 2 :]

    def narrow(array):
        return array.astype(jnp.bfloat16)

    def wide(array):
        return array.astype(jnp.float32)

    def paired(send, keep):
        return keep + wide(move(send, swap))

    first = [FAR2, FAR1, NEAR2]
    rest = [FAR3, NEAR1, FAR0, NEAR3, NEAR0]
    sends = blocks_of(first, False)
    total = {name: paired(*pair) for name, *pair in zip(first, sends, blocks_of(first, True))}
    crossing, aside = list(map(narrow, halves(total[FAR2]))), narrow(total[FAR1])
    *crossing, aside = blocks_of.hold(*crossing, aside)
    two_on = [move(part, ACROSS) for part in crossing]
    joining = move(aside, ALONG)
    total.update({name: paired(*pair) for name, *pair in zip(rest, blocks_of(rest, False), blocks_of(rest, True))})

    crossing, two_on[1] = tie(narrow(total[FAR3]), two_on[1])
    three_on = move(crossing, ACROSS)
    crossing, three_on = tie(narrow(total[FAR0] + wide(joining)), three_on)
    straight = move(crossing, ACROSS)
    two_on = [move(narrow(own + wide(part)), ALONG) for own, part in zip(halves(total[NEAR2]), two_on)]
    later, two_on[0] = tie(total[NEAR1], two_on[0])
    one_on = [
        move(narrow(halves(own)[index] + wide(two_on[index])), ALONG)
        for index, own in enumerate((total[NEAR1], later))
    ]
    one_back = move(narrow(total[NEAR3] + wide(three_on)), BACK)
    (result,) = tie(total[NEAR0] + wide(jnp.concatenate(one_on)))
    return result + wide(straight) + wide(one_back)


def clear(half):
    whole = half.shape[0] // (4 * BLK) * (4 * BLK)

    @pl.loop(0, whole // (4 * BLK))
    def _(index):
        half[pl.ds(pl.multiple_of(index * 4 * BLK, BLK), 4 * BLK), :] = jnp.zeros((4 * BLK, LANES), jnp.float32)

    half[pl.ds(whole, half.shape[0] - whole), :] = jnp.zeros((half.shape[0] - whole, LANES), jnp.float32)


def add_tiles(stage, pieces, table_ref, bounds_ref, tiles, half, occ, sem):
    pltpu.make_async_copy(occ, occ, sem).wait()
    begin, end = bounds_ref[stage], bounds_ref[stage + 1]
    low = lax.broadcasted_iota(jnp.int32, tiles.shape[1:], 1) < BLK
    zero = jnp.zeros(tiles.shape[1:], jnp.bfloat16)
    spill = half.shape[0] - BLK
    entries = table_ref.shape[0] // (2 + pieces)
    piece = BLK // pieces

    @pl.loop(0, (end - begin + UNROLL - 1) // UNROLL)
    def _(group):
        products, starts = [], []
        for lane in range(UNROLL):
            entry = begin + group * UNROLL + lane
            tile = table_ref[entry]
            starts.append(jnp.where(entry < end, table_ref[entries + entry], spill))
            spots = [jnp.where(entry < end, table_ref[(2 + cut) * entries + entry], 0) for cut in range(pieces)]
            parts = [occ[pl.ds(pl.multiple_of(spot, piece), piece), :] for spot in spots]
            pair = tiles[tile]
            left = jnp.concatenate([jnp.where(low, pair, zero), jnp.where(low, zero, pair)], axis=0)
            block = jnp.concatenate(parts * 2, axis=0)
            products.append(jnp.dot(left, block, preferred_element_type=jnp.float32))
        for product, start in zip(products, starts):
            start = pl.multiple_of(start, BLK)
            for odd in range(2):
                span = pl.ds(start + odd, BLK // 2, stride=2)
                half[span, :] += product[odd * (BLK // 2) : (odd + 1) * (BLK // 2)]


def fill_window(half, weights, shard, chips_ref, first, parity, out):
    side_rows = (half.shape[0] - BLK) // 2

    @pl.loop(0, out.shape[0])
    def _(index):
        start = pl.multiple_of((2 * chips_ref[first + index] + parity) * shard, 32)
        both = jnp.concatenate(
            [half[pl.ds(side * side_rows + start, shard), :].astype(jnp.bfloat16) for side in range(2)], axis=1
        )
        out[index] = jnp.dot(both, weights[...], preferred_element_type=jnp.float32).astype(out.dtype)


def load_tiles(tile_sets, tiles, sems):
    slots = tile_sets[0].shape[0]
    copies = [
        pltpu.make_async_copy(source, tiles.at[pl.ds(index * slots, slots)], sems.at[index])
        for index, source in enumerate(tile_sets)
    ]
    for copy in copies:
        copy.start()
    return copies


def add_stage(stage, count, pieces, table_ref, bounds_ref, refs):
    sources = refs[:count]
    *_, occ, sems = refs
    rows = sources[0].shape[0]
    for index, source in enumerate(sources):
        pltpu.make_async_copy(source, occ.at[pl.ds(index * rows, rows)], sems.at[2]).start()
    if stage:
        tiles, _, half, *outs = refs[count:-2]
        copies = []
    else:
        *tile_sets, half, tiles = refs[count : count + 4]
        outs = refs[count + 4 : -2]
        copies = load_tiles(tile_sets, tiles, sems)
        clear(half)
    for copy in copies:
        copy.wait()
    add_tiles(stage, pieces, table_ref, bounds_ref, tiles, half, occ, sems.at[2])
    return half, outs


def stage_kernel(stage, count, pieces, table_ref, bounds_ref, *refs):
    add_stage(stage, count, pieces, table_ref, bounds_ref, refs)


def window_kernel(stage, count, pieces, shard, plan, table_ref, bounds_ref, chips_ref, core_ref, *refs):
    half, (weights, *outs) = add_stage(stage, count, pieces, table_ref, bounds_ref, refs)
    side_rows = (half.shape[0] - BLK) // 2
    for side in range(2):
        weights[pl.ds(side * LANES, LANES), :] = half[pl.ds(side * side_rows, WIN), :].T.astype(jnp.bfloat16)
    rest_kernel(shard, plan, False, chips_ref, core_ref, half, weights, *outs)


def rest_kernel(shard, plan, keeps, chips_ref, core_ref, half, weights, *outs):
    for first, out in zip(plan, outs):
        fill_window(half, weights, shard, chips_ref, first, core_ref[0] if keeps else 1 - core_ref[0], out)


SMEM = pl.BlockSpec(memory_space=pltpu.SMEM)
HBM = pl.BlockSpec(memory_space=pl.ANY)
VMEM = pl.BlockSpec(memory_space=pltpu.VMEM)


def pinned(array):
    return pltpu.with_memory_space_constraint(array, pltpu.VMEM)


def held(array):
    return pltpu.with_memory_space_constraint(array, pltpu.HBM)


def call(kernel, ins, in_specs, outs, scratch, aliases, flops, scoped=0):
    return pl.pallas_call(
        kernel,
        out_shape=outs,
        in_specs=in_specs,
        out_specs=[VMEM] * len(outs),
        scratch_shapes=scratch,
        input_output_aliases=aliases,
        compiler_params=pltpu.CompilerParams(vmem_limit_bytes=SCOPED_BYTES + scoped),
        cost_estimate=pl.CostEstimate(flops=flops, bytes_accessed=4 << 20, transcendentals=0),
    )(*ins)


def local(block_values, block_pairs, live_counts, occupied):
    owners = lax.axis_size("aux")
    me = lax.axis_index("aux")
    core, chip = me % 2, me // 2
    shard, width = occupied.shape
    total = owners * shard
    slots = block_values.shape[0]
    piece = math.gcd(BLK, shard)
    pieces = BLK // piece
    chips = owners // 2
    lined = chips == 2 * LINE
    same_core = [[2 * i + k for i in range(chips)] for k in range(2)]
    swap = [(i, i ^ 1) for i in range(owners)]

    mine = lax.dynamic_slice_in_dim(occupied, core * LANES, LANES, 1)
    given = lax.dynamic_slice_in_dim(occupied, (1 - core) * LANES, LANES, 1)
    parts = [mine, move(given, swap)]
    others = [move(array, swap) for array in (block_values, block_pairs, live_counts)]
    raw_sets = [block_values, others[0]]
    tile_sets = []

    def lay_tiles():
        tile_sets[:] = [values.reshape(slots, BLK * BLK // LANES, LANES) for values in raw_sets]

    slot_ids = jnp.arange(chips, dtype=jnp.int32)
    chip_of_slot = slot_ids
    stage_count = 1
    if lined:
        chip_of_slot = (slot_ids + chip // 2) % LINE * 2 + ((slot_ids // LINE) ^ (chip % 2))
        stage_count = LINE + 1

    tile_ids = jnp.arange(2 * slots, dtype=jnp.int32)
    pairs = jnp.concatenate([block_pairs, others[1]])
    live = tile_ids % slots < jnp.where(tile_ids < slots, live_counts[0], others[2][0])
    first = pairs[:, 1][:, None] * BLK + jnp.arange(pieces, dtype=jnp.int32) * piece
    owner = first // shard
    part = (owner % 2) ^ core
    owner_chip = owner // 2
    if lined:
        back = (chip // 2 - owner_chip // 2) % LINE
        side = (owner_chip % 2) ^ (chip % 2)
        stage = (back + side)[:, 0]
        slot_of = part + 2 * jnp.where(back + side < LINE, side, 0)
    else:
        stage = jnp.zeros_like(tile_ids)
        slot_of = part * chips + owner_chip
    spots = slot_of * shard + first % shard
    stage = jnp.where(live, stage, stage_count)
    rows = pairs[:, 0] * BLK + tile_ids // slots * total
    ahead = (stage[None, :] < stage[:, None]) | (
        (stage[None, :] == stage[:, None]) & (tile_ids[None, :] < tile_ids[:, None])
    )
    rank = jnp.sum(ahead.astype(jnp.int32), axis=1)
    entries = jnp.arange(2 * slots + UNROLL, dtype=jnp.int32)
    chosen = rank[None, :] == entries[:, None]
    columns = [tile_ids, rows] + [spots[:, cut] for cut in range(pieces)]
    ordered = jnp.concatenate([jnp.sum(jnp.where(chosen, column[None, :], 0), axis=1) for column in columns])
    bounds = jnp.sum((stage[None, :] < jnp.arange(stage_count + 1)[:, None]).astype(jnp.int32), axis=1)
    cores = core.astype(jnp.int32).reshape(1)

    half_type = pltpu.VMEM((2 * total + BLK, LANES), jnp.float32)
    tiles_type = pltpu.VMEM((2 * slots, BLK * BLK // LANES, LANES), jnp.bfloat16)
    work = 4 * slots * BLK * BLK * LANES // stage_count
    state = []

    def run_stage(kernel, sources, tables, outs, flops):
        rows = len(sources) * sources[0].shape[0]
        scratch = [pltpu.VMEM((rows, LANES), jnp.bfloat16), pltpu.SemaphoreType.DMA((3,))]
        ins, specs = [*tables, *sources], [SMEM] * len(tables) + [HBM] * len(sources)
        made, aliases = [half_type], {}
        if state:
            aliases = {len(ins) + 1: 0}
            ins, specs = ins + [pinned(state[1]), pinned(state[0])], specs + [VMEM] * 2
        else:
            ins = [*tables, *map(held, sources), tile_sets[0], held(tile_sets[1])]
            specs = specs + [HBM] * 2
            made = [half_type, tiles_type]
        results = call(kernel, ins, specs, made + outs, scratch, aliases, flops, 2 * rows * LANES)
        state[:] = [results[0], state[1] if state else results[1]]
        return results[len(made) :]

    def add(stage, sources):
        kernel = functools.partial(stage_kernel, stage, len(sources), pieces)
        run_stage(kernel, sources, [ordered, bounds], [], work)

    def meanwhile(step, index, arrived, moved):
        if (step, index) == RAW_AT:
            moved, *raw_sets[:] = tie(moved, *raw_sets)
            lay_tiles()
        if (step, index) == LAY_AT:
            moved, *tile_sets[:] = tie(moved, *tile_sets)
        if (step, index) in ADD_AT:
            stage = ADD_AT[step, index]
            add(stage, arrived(stage))
            moved, state[0] = tie(moved, state[0])
        return moved

    if lined:
        stages = spread(parts, meanwhile)
        for stage in range(len(ADD_AT), LINE):
            add(stage, stages[stage])
    else:
        lay_tiles()
        stages = [[lax.all_gather(part, "aux", axis_index_groups=same_core, axis=0, tiled=True) for part in parts]]

    group = 1 if lined else chips

    def window_types(plan, keeps):
        return [pltpu.VMEM((group, shard, WIN), jnp.float32 if keeps else jnp.bfloat16) for _ in plan]

    def first_sends(plan):
        weights, *blocks = run_stage(
            functools.partial(window_kernel, stage_count - 1, len(stages[-1]), pieces, shard, plan),
            stages[-1],
            [ordered, bounds, chip_of_slot, cores],
            [pltpu.VMEM((2 * LANES, WIN), jnp.bfloat16)] + window_types(plan, False),
            work + len(plan) * group * shard * width * WIN * 2,
        )
        state.append(weights)
        return blocks

    def blocks_of(plan, keeps):
        if len(state) < 3:
            blocks = first_sends(plan)
        else:
            blocks = call(
                functools.partial(rest_kernel, shard, plan, keeps),
                [chip_of_slot, cores, pinned(state[0]), pinned(state[2])],
                [SMEM] * 2 + [VMEM] * 2,
                window_types(plan, keeps),
                [],
                {},
                len(plan) * group * shard * width * WIN * 2,
            )
        return [block[0] for block in blocks] if lined else blocks

    def hold(*arrays):
        state[0], *arrays = tie(state[0], *arrays)
        return arrays

    blocks_of.hold = hold
    factor = 1.0 / math.sqrt(owners * width)
    if lined:
        return collect(blocks_of, swap) * factor
    (send,), (keep,) = blocks_of([0], False), blocks_of([0], True)
    pair_sum = (keep + move(send, swap).astype(jnp.float32)).astype(jnp.bfloat16)
    block_sum = lax.psum_scatter(
        pair_sum.reshape(total // 2, WIN), "aux", axis_index_groups=same_core, scatter_dimension=0, tiled=True
    )
    return block_sum.astype(jnp.float32) * factor


def solution(mesh):
    placed = (
        P(("groups", "aux"), None),
        P(("groups", "aux"), None),
        P(("groups", "aux")),
        P(("groups", "aux"), None),
    )
    return jax.shard_map(
        local, mesh=mesh, in_specs=placed, out_specs=P(("groups", "aux"), None), check_vma=False
    )
```

```python
import functools
import math

import jax
import jax.numpy as jnp
from jax import lax
from jax.experimental import pallas as pl
from jax.experimental.pallas import tpu as pltpu
from jax.sharding import PartitionSpec as P

BLK = 64
WIN = 128
LANES = 128
UNROLL = 16
LINE = 4
SCOPED_BYTES = 6 * 1024 * 1024


def place(z, x, core):
    return (z * 2 + x) * 2 + core


def pairs_of(step):
    return [
        (place(z, x, core), place(*step(z, x), core)) for z in range(LINE) for x in range(2) for core in range(2)
    ]


def tie(*arrays):
    return lax.optimization_barrier(arrays)


def move(array, pairs):
    return lax.ppermute(array, "aux", pairs)


ALONG = pairs_of(lambda z, x: ((z + 1) % LINE, x))
BACK = pairs_of(lambda z, x: ((z - 1) % LINE, x))
ACROSS = pairs_of(lambda z, x: (z, 1 - x))
NEAR0, NEAR1, NEAR2, NEAR3, FAR0, FAR1, FAR2, FAR3 = range(2 * LINE)
ADD_AT = {(2, 1): 0, (3, 0): 1}
RAW_AT, LAY_AT = (0, 1), (1, 1)


def spread(parts, meanwhile):
    lines, others = [[part] for part in parts], [[] for _ in parts]

    def arrived(stage):
        held = [line[stage] for line in lines] if stage < LINE else []
        return held + ([other[stage - 1] for other in others] if stage else [])

    for step in range(LINE):
        for index, (line, other) in enumerate(zip(lines, others)):
            if other:
                line[-1], other[-1] = tie(line[-1], other[-1])
            turn = step == LINE - 1 and index == 0
            source = other if turn else line
            source[-1] = meanwhile(step, index, arrived, source[-1])
            now = source[-1]
            if step + 1 < LINE:
                line.append(move(now, ALONG))
            other.append(move(now, ALONG if turn else ACROSS))
    return [arrived(stage) for stage in range(LINE + 1)]


def collect(blocks_of, swap):
    def halves(array):
        return array[: array.shape[0] // 2], array[array.shape[0] // 2 :]

    def narrow(array):
        return array.astype(jnp.bfloat16)

    def wide(array):
        return array.astype(jnp.float32)

    def paired(send, keep):
        return keep + wide(move(send, swap))

    first = [FAR2, FAR1, NEAR2]
    rest = [FAR3, NEAR1, FAR0, NEAR3, NEAR0]
    sends = blocks_of(first, False)
    total = {name: paired(*pair) for name, *pair in zip(first, sends, blocks_of(first, True))}
    crossing, aside = list(map(narrow, halves(total[FAR2]))), narrow(total[FAR1])
    two_on = [move(part, ACROSS) for part in crossing]
    joining = move(aside, ALONG)
    (joining,) = blocks_of.hold(joining)
    total.update({name: paired(*pair) for name, *pair in zip(rest, blocks_of(rest, False), blocks_of(rest, True))})

    crossing, two_on[1] = tie(narrow(total[FAR3]), two_on[1])
    three_on = move(crossing, ACROSS)
    crossing, three_on = tie(narrow(total[FAR0] + wide(joining)), three_on)
    straight = move(crossing, ACROSS)
    two_on = [move(narrow(own + wide(part)), ALONG) for own, part in zip(halves(total[NEAR2]), two_on)]
    later, two_on[0] = tie(total[NEAR1], two_on[0])
    one_on = [
        move(narrow(halves(own)[index] + wide(two_on[index])), ALONG)
        for index, own in enumerate((total[NEAR1], later))
    ]
    one_back = move(narrow(total[NEAR3] + wide(three_on)), BACK)
    (result,) = tie(total[NEAR0] + wide(jnp.concatenate(one_on)))
    return result + wide(straight) + wide(one_back)


def clear(half):
    whole = half.shape[0] // (4 * BLK) * (4 * BLK)

    @pl.loop(0, whole // (4 * BLK))
    def _(index):
        half[pl.ds(pl.multiple_of(index * 4 * BLK, BLK), 4 * BLK), :] = jnp.zeros((4 * BLK, LANES), jnp.float32)

    half[pl.ds(whole, half.shape[0] - whole), :] = jnp.zeros((half.shape[0] - whole, LANES), jnp.float32)


def add_tiles(stage, pieces, table_ref, bounds_ref, tiles, half, occ, sem):
    pltpu.make_async_copy(occ, occ, sem).wait()
    begin, end = bounds_ref[stage], bounds_ref[stage + 1]
    low = lax.broadcasted_iota(jnp.int32, tiles.shape[1:], 1) < BLK
    zero = jnp.zeros(tiles.shape[1:], jnp.bfloat16)
    spill = half.shape[0] - BLK
    entries = table_ref.shape[0] // (2 + pieces)
    piece = BLK // pieces

    @pl.loop(0, (end - begin + UNROLL - 1) // UNROLL)
    def _(group):
        products, starts = [], []
        for lane in range(UNROLL):
            entry = begin + group * UNROLL + lane
            tile = table_ref[entry]
            starts.append(jnp.where(entry < end, table_ref[entries + entry], spill))
            spots = [jnp.where(entry < end, table_ref[(2 + cut) * entries + entry], 0) for cut in range(pieces)]
            parts = [occ[pl.ds(pl.multiple_of(spot, piece), piece), :] for spot in spots]
            pair = tiles[tile]
            left = jnp.concatenate([jnp.where(low, pair, zero), jnp.where(low, zero, pair)], axis=0)
            block = jnp.concatenate(parts * 2, axis=0)
            products.append(jnp.dot(left, block, preferred_element_type=jnp.float32))
        for product, start in zip(products, starts):
            start = pl.multiple_of(start, BLK)
            for odd in range(2):
                span = pl.ds(start + odd, BLK // 2, stride=2)
                half[span, :] += product[odd * (BLK // 2) : (odd + 1) * (BLK // 2)]


def fill_window(half, weights, shard, chips_ref, first, parity, out):
    side_rows = (half.shape[0] - BLK) // 2

    @pl.loop(0, out.shape[0])
    def _(index):
        start = pl.multiple_of((2 * chips_ref[first + index] + parity) * shard, 32)
        both = jnp.concatenate(
            [half[pl.ds(side * side_rows + start, shard), :].astype(jnp.bfloat16) for side in range(2)], axis=1
        )
        out[index] = jnp.dot(both, weights[...], preferred_element_type=jnp.float32).astype(out.dtype)


def load_tiles(tile_sets, tiles, sems):
    slots = tile_sets[0].shape[0]
    copies = [
        pltpu.make_async_copy(source, tiles.at[pl.ds(index * slots, slots)], sems.at[index])
        for index, source in enumerate(tile_sets)
    ]
    for copy in copies:
        copy.start()
    return copies


def add_stage(stage, count, pieces, table_ref, bounds_ref, refs):
    sources = refs[:count]
    *_, occ, sems = refs
    rows = sources[0].shape[0]
    for index, source in enumerate(sources):
        pltpu.make_async_copy(source, occ.at[pl.ds(index * rows, rows)], sems.at[2]).start()
    if stage:
        tiles, _, half, *outs = refs[count:-2]
        copies = []
    else:
        *tile_sets, half, tiles = refs[count : count + 4]
        outs = refs[count + 4 : -2]
        copies = load_tiles(tile_sets, tiles, sems)
        clear(half)
    for copy in copies:
        copy.wait()
    add_tiles(stage, pieces, table_ref, bounds_ref, tiles, half, occ, sems.at[2])
    return half, outs


def stage_kernel(stage, count, pieces, table_ref, bounds_ref, *refs):
    add_stage(stage, count, pieces, table_ref, bounds_ref, refs)


def window_kernel(stage, count, pieces, shard, plan, table_ref, bounds_ref, chips_ref, core_ref, *refs):
    half, (weights, *outs) = add_stage(stage, count, pieces, table_ref, bounds_ref, refs)
    side_rows = (half.shape[0] - BLK) // 2
    for side in range(2):
        weights[pl.ds(side * LANES, LANES), :] = half[pl.ds(side * side_rows, WIN), :].T.astype(jnp.bfloat16)
    rest_kernel(shard, plan, False, chips_ref, core_ref, half, weights, *outs)


def rest_kernel(shard, plan, keeps, chips_ref, core_ref, half, weights, *outs):
    for first, out in zip(plan, outs):
        fill_window(half, weights, shard, chips_ref, first, core_ref[0] if keeps else 1 - core_ref[0], out)


SMEM = pl.BlockSpec(memory_space=pltpu.SMEM)
HBM = pl.BlockSpec(memory_space=pl.ANY)
VMEM = pl.BlockSpec(memory_space=pltpu.VMEM)


def pinned(array):
    return pltpu.with_memory_space_constraint(array, pltpu.VMEM)


def held(array):
    return pltpu.with_memory_space_constraint(array, pltpu.HBM)


def call(kernel, ins, in_specs, outs, scratch, aliases, flops, scoped=0):
    return pl.pallas_call(
        kernel,
        out_shape=outs,
        in_specs=in_specs,
        out_specs=[VMEM] * len(outs),
        scratch_shapes=scratch,
        input_output_aliases=aliases,
        compiler_params=pltpu.CompilerParams(vmem_limit_bytes=SCOPED_BYTES + scoped),
        cost_estimate=pl.CostEstimate(flops=flops, bytes_accessed=4 << 20, transcendentals=0),
    )(*ins)


def local(block_values, block_pairs, live_counts, occupied):
    owners = lax.axis_size("aux")
    me = lax.axis_index("aux")
    core, chip = me % 2, me // 2
    shard, width = occupied.shape
    total = owners * shard
    slots = block_values.shape[0]
    piece = math.gcd(BLK, shard)
    pieces = BLK // piece
    chips = owners // 2
    lined = chips == 2 * LINE
    same_core = [[2 * i + k for i in range(chips)] for k in range(2)]
    swap = [(i, i ^ 1) for i in range(owners)]

    mine = lax.dynamic_slice_in_dim(occupied, core * LANES, LANES, 1)
    given = lax.dynamic_slice_in_dim(occupied, (1 - core) * LANES, LANES, 1)
    parts = [mine, move(given, swap)]
    others = [move(array, swap) for array in (block_values, block_pairs, live_counts)]
    raw_sets = [block_values, others[0]]
    tile_sets = []

    def lay_tiles():
        tile_sets[:] = [values.reshape(slots, BLK * BLK // LANES, LANES) for values in raw_sets]

    slot_ids = jnp.arange(chips, dtype=jnp.int32)
    chip_of_slot = slot_ids
    stage_count = 1
    if lined:
        chip_of_slot = (slot_ids + chip // 2) % LINE * 2 + ((slot_ids // LINE) ^ (chip % 2))
        stage_count = LINE + 1

    tile_ids = jnp.arange(2 * slots, dtype=jnp.int32)
    pairs = jnp.concatenate([block_pairs, others[1]])
    live = tile_ids % slots < jnp.where(tile_ids < slots, live_counts[0], others[2][0])
    first = pairs[:, 1][:, None] * BLK + jnp.arange(pieces, dtype=jnp.int32) * piece
    owner = first // shard
    part = (owner % 2) ^ core
    owner_chip = owner // 2
    if lined:
        back = (chip // 2 - owner_chip // 2) % LINE
        side = (owner_chip % 2) ^ (chip % 2)
        stage = (back + side)[:, 0]
        slot_of = part + 2 * jnp.where(back + side < LINE, side, 0)
    else:
        stage = jnp.zeros_like(tile_ids)
        slot_of = part * chips + owner_chip
    spots = slot_of * shard + first % shard
    stage = jnp.where(live, stage, stage_count)
    rows = pairs[:, 0] * BLK + tile_ids // slots * total
    ahead = (stage[None, :] < stage[:, None]) | (
        (stage[None, :] == stage[:, None]) & (tile_ids[None, :] < tile_ids[:, None])
    )
    rank = jnp.sum(ahead.astype(jnp.int32), axis=1)
    entries = jnp.arange(2 * slots + UNROLL, dtype=jnp.int32)
    chosen = rank[None, :] == entries[:, None]
    columns = [tile_ids, rows] + [spots[:, cut] for cut in range(pieces)]
    ordered = jnp.concatenate([jnp.sum(jnp.where(chosen, column[None, :], 0), axis=1) for column in columns])
    bounds = jnp.sum((stage[None, :] < jnp.arange(stage_count + 1)[:, None]).astype(jnp.int32), axis=1)
    cores = core.astype(jnp.int32).reshape(1)

    half_type = pltpu.VMEM((2 * total + BLK, LANES), jnp.float32)
    tiles_type = pltpu.VMEM((2 * slots, BLK * BLK // LANES, LANES), jnp.bfloat16)
    work = 4 * slots * BLK * BLK * LANES // stage_count
    state = []

    def run_stage(kernel, sources, tables, outs, flops):
        rows = len(sources) * sources[0].shape[0]
        scratch = [pltpu.VMEM((rows, LANES), jnp.bfloat16), pltpu.SemaphoreType.DMA((3,))]
        ins, specs = [*tables, *sources], [SMEM] * len(tables) + [HBM] * len(sources)
        made, aliases = [half_type], {}
        if state:
            aliases = {len(ins) + 1: 0}
            ins, specs = ins + [pinned(state[1]), pinned(state[0])], specs + [VMEM] * 2
        else:
            ins = [*tables, *map(held, sources), tile_sets[0], held(tile_sets[1])]
            specs = specs + [HBM] * 2
            made = [half_type, tiles_type]
        results = call(kernel, ins, specs, made + outs, scratch, aliases, flops, 2 * rows * LANES)
        state[:] = [results[0], state[1] if state else results[1]]
        return results[len(made) :]

    def add(stage, sources):
        kernel = functools.partial(stage_kernel, stage, len(sources), pieces)
        run_stage(kernel, sources, [ordered, bounds], [], work)

    def meanwhile(step, index, arrived, moved):
        if (step, index) == RAW_AT:
            moved, *raw_sets[:] = tie(moved, *raw_sets)
            lay_tiles()
        if (step, index) == LAY_AT:
            moved, *tile_sets[:] = tie(moved, *tile_sets)
        if (step, index) in ADD_AT:
            stage = ADD_AT[step, index]
            add(stage, arrived(stage))
            moved, state[0] = tie(moved, state[0])
        return moved

    if lined:
        stages = spread(parts, meanwhile)
        for stage in range(len(ADD_AT), LINE):
            add(stage, stages[stage])
    else:
        lay_tiles()
        stages = [[lax.all_gather(part, "aux", axis_index_groups=same_core, axis=0, tiled=True) for part in parts]]

    group = 1 if lined else chips

    def window_types(plan, keeps):
        return [pltpu.VMEM((group, shard, WIN), jnp.float32 if keeps else jnp.bfloat16) for _ in plan]

    def first_sends(plan):
        weights, *blocks = run_stage(
            functools.partial(window_kernel, stage_count - 1, len(stages[-1]), pieces, shard, plan),
            stages[-1],
            [ordered, bounds, chip_of_slot, cores],
            [pltpu.VMEM((2 * LANES, WIN), jnp.bfloat16)] + window_types(plan, False),
            work + len(plan) * group * shard * width * WIN * 2,
        )
        state.append(weights)
        return blocks

    def blocks_of(plan, keeps):
        if len(state) < 3:
            blocks = first_sends(plan)
        else:
            blocks = call(
                functools.partial(rest_kernel, shard, plan, keeps),
                [chip_of_slot, cores, pinned(state[0]), pinned(state[2])],
                [SMEM] * 2 + [VMEM] * 2,
                window_types(plan, keeps),
                [],
                {},
                len(plan) * group * shard * width * WIN * 2,
            )
        return [block[0] for block in blocks] if lined else blocks

    def hold(*arrays):
        state[0], *arrays = tie(state[0], *arrays)
        return arrays

    blocks_of.hold = hold
    factor = 1.0 / math.sqrt(owners * width)
    if lined:
        return collect(blocks_of, swap) * factor
    (send,), (keep,) = blocks_of([0], False), blocks_of([0], True)
    pair_sum = (keep + move(send, swap).astype(jnp.float32)).astype(jnp.bfloat16)
    block_sum = lax.psum_scatter(
        pair_sum.reshape(total // 2, WIN), "aux", axis_index_groups=same_core, scatter_dimension=0, tiled=True
    )
    return block_sum.astype(jnp.float32) * factor


def solution(mesh):
    placed = (
        P(("groups", "aux"), None),
        P(("groups", "aux"), None),
        P(("groups", "aux")),
        P(("groups", "aux"), None),
    )
    return jax.shard_map(
        local, mesh=mesh, in_specs=placed, out_specs=P(("groups", "aux"), None), check_vma=False
    )
```

```python
import functools
import math

import jax
import jax.numpy as jnp
from jax import lax
from jax.experimental import pallas as pl
from jax.experimental.pallas import tpu as pltpu
from jax.sharding import PartitionSpec as P

BLK = 64
WIN = 128
LANES = 128
UNROLL = 16
LINE = 4
SCOPED_BYTES = 6 * 1024 * 1024


def place(z, x, core):
    return (z * 2 + x) * 2 + core


def pairs_of(step):
    return [
        (place(z, x, core), place(*step(z, x), core)) for z in range(LINE) for x in range(2) for core in range(2)
    ]


def tie(*arrays):
    return lax.optimization_barrier(arrays)


def move(array, pairs):
    return lax.ppermute(array, "aux", pairs)


ALONG = pairs_of(lambda z, x: ((z + 1) % LINE, x))
BACK = pairs_of(lambda z, x: ((z - 1) % LINE, x))
ACROSS = pairs_of(lambda z, x: (z, 1 - x))
NEAR0, NEAR1, NEAR2, NEAR3, FAR0, FAR1, FAR2, FAR3 = range(2 * LINE)
ADD_AT = {(2, 1): 0, (3, 0): 1}
RAW_AT, LAY_AT = (0, 1), (1, 1)


def spread(parts, meanwhile):
    lines, others = [[part] for part in parts], [[] for _ in parts]

    def arrived(stage):
        held = [line[stage] for line in lines] if stage < LINE else []
        return held + ([other[stage - 1] for other in others] if stage else [])

    for step in range(LINE):
        for index, (line, other) in enumerate(zip(lines, others)):
            if other:
                line[-1], other[-1] = tie(line[-1], other[-1])
            turn = step == LINE - 1 and index == 0
            source = other if turn else line
            source[-1] = meanwhile(step, index, arrived, source[-1])
            now = source[-1]
            if step + 1 < LINE:
                line.append(move(now, ALONG))
            other.append(move(now, ALONG if turn else ACROSS))
    return [arrived(stage) for stage in range(LINE + 1)]


def collect(blocks_of, swap):
    def halves(array):
        return array[: array.shape[0] // 2], array[array.shape[0] // 2 :]

    def narrow(array):
        return array.astype(jnp.bfloat16)

    def wide(array):
        return array.astype(jnp.float32)

    def paired(send, keep):
        return keep + wide(move(send, swap))

    first = [FAR2, FAR1, NEAR2]
    rest = [FAR3, NEAR1, FAR0, NEAR3, NEAR0]
    sends = blocks_of(first, False)
    total = {name: paired(*pair) for name, *pair in zip(first, sends, blocks_of(first, True))}
    crossing, aside = list(map(narrow, halves(total[FAR2]))), narrow(total[FAR1])
    *crossing, aside = blocks_of.hold(*crossing, aside)
    two_on = [move(part, ACROSS) for part in crossing]
    joining = move(aside, ALONG)
    total.update({name: paired(*pair) for name, *pair in zip(rest, blocks_of(rest, False), blocks_of(rest, True))})

    two_on[1], joining = tie(two_on[1], joining)
    crossing, two_on[0] = tie(narrow(total[FAR3]), two_on[0])
    three_on = move(crossing, ACROSS)
    crossing, three_on = tie(narrow(total[FAR0] + wide(joining)), three_on)
    straight = move(crossing, ACROSS)
    two_on = [move(narrow(own + wide(part)), ALONG) for own, part in zip(halves(total[NEAR2]), two_on)]
    later, two_on[0] = tie(total[NEAR1], two_on[0])
    one_on = [
        move(narrow(halves(own)[index] + wide(two_on[index])), ALONG)
        for index, own in enumerate((total[NEAR1], later))
    ]
    one_back = move(narrow(total[NEAR3] + wide(three_on)), BACK)
    (result,) = tie(total[NEAR0] + wide(jnp.concatenate(one_on)))
    return result + wide(straight) + wide(one_back)


def clear(half):
    whole = half.shape[0] // (4 * BLK) * (4 * BLK)

    @pl.loop(0, whole // (4 * BLK))
    def _(index):
        half[pl.ds(pl.multiple_of(index * 4 * BLK, BLK), 4 * BLK), :] = jnp.zeros((4 * BLK, LANES), jnp.float32)

    half[pl.ds(whole, half.shape[0] - whole), :] = jnp.zeros((half.shape[0] - whole, LANES), jnp.float32)


def add_tiles(stage, pieces, table_ref, bounds_ref, tiles, half, occ, sem):
    pltpu.make_async_copy(occ, occ, sem).wait()
    begin, end = bounds_ref[stage], bounds_ref[stage + 1]
    low = lax.broadcasted_iota(jnp.int32, tiles.shape[1:], 1) < BLK
    zero = jnp.zeros(tiles.shape[1:], jnp.bfloat16)
    spill = half.shape[0] - BLK
    entries = table_ref.shape[0] // (2 + pieces)
    piece = BLK // pieces

    @pl.loop(0, (end - begin + UNROLL - 1) // UNROLL)
    def _(group):
        products, starts = [], []
        for lane in range(UNROLL):
            entry = begin + group * UNROLL + lane
            tile = table_ref[entry]
            starts.append(jnp.where(entry < end, table_ref[entries + entry], spill))
            spots = [jnp.where(entry < end, table_ref[(2 + cut) * entries + entry], 0) for cut in range(pieces)]
            parts = [occ[pl.ds(pl.multiple_of(spot, piece), piece), :] for spot in spots]
            pair = tiles[tile]
            left = jnp.concatenate([jnp.where(low, pair, zero), jnp.where(low, zero, pair)], axis=0)
            block = jnp.concatenate(parts * 2, axis=0)
            products.append(jnp.dot(left, block, preferred_element_type=jnp.float32))
        for product, start in zip(products, starts):
            start = pl.multiple_of(start, BLK)
            for odd in range(2):
                span = pl.ds(start + odd, BLK // 2, stride=2)
                half[span, :] += product[odd * (BLK // 2) : (odd + 1) * (BLK // 2)]


def fill_window(half, weights, shard, chips_ref, first, parity, out):
    side_rows = (half.shape[0] - BLK) // 2

    @pl.loop(0, out.shape[0])
    def _(index):
        start = pl.multiple_of((2 * chips_ref[first + index] + parity) * shard, 32)
        both = jnp.concatenate(
            [half[pl.ds(side * side_rows + start, shard), :].astype(jnp.bfloat16) for side in range(2)], axis=1
        )
        out[index] = jnp.dot(both, weights[...], preferred_element_type=jnp.float32).astype(out.dtype)


def load_tiles(tile_sets, tiles, sems):
    slots = tile_sets[0].shape[0]
    copies = [
        pltpu.make_async_copy(source, tiles.at[pl.ds(index * slots, slots)], sems.at[index])
        for index, source in enumerate(tile_sets)
    ]
    for copy in copies:
        copy.start()
    return copies


def add_stage(stage, count, pieces, table_ref, bounds_ref, refs):
    sources = refs[:count]
    *_, occ, sems = refs
    rows = sources[0].shape[0]
    for index, source in enumerate(sources):
        pltpu.make_async_copy(source, occ.at[pl.ds(index * rows, rows)], sems.at[2]).start()
    if stage:
        tiles, _, half, *outs = refs[count:-2]
        copies = []
    else:
        *tile_sets, half, tiles = refs[count : count + 4]
        outs = refs[count + 4 : -2]
        copies = load_tiles(tile_sets, tiles, sems)
        clear(half)
    for copy in copies:
        copy.wait()
    add_tiles(stage, pieces, table_ref, bounds_ref, tiles, half, occ, sems.at[2])
    return half, outs


def stage_kernel(stage, count, pieces, table_ref, bounds_ref, *refs):
    add_stage(stage, count, pieces, table_ref, bounds_ref, refs)


def window_kernel(stage, count, pieces, shard, plan, table_ref, bounds_ref, chips_ref, core_ref, *refs):
    half, (weights, *outs) = add_stage(stage, count, pieces, table_ref, bounds_ref, refs)
    side_rows = (half.shape[0] - BLK) // 2
    for side in range(2):
        weights[pl.ds(side * LANES, LANES), :] = half[pl.ds(side * side_rows, WIN), :].T.astype(jnp.bfloat16)
    rest_kernel(shard, plan, False, chips_ref, core_ref, half, weights, *outs)


def rest_kernel(shard, plan, keeps, chips_ref, core_ref, half, weights, *outs):
    for first, out in zip(plan, outs):
        fill_window(half, weights, shard, chips_ref, first, core_ref[0] if keeps else 1 - core_ref[0], out)


SMEM = pl.BlockSpec(memory_space=pltpu.SMEM)
HBM = pl.BlockSpec(memory_space=pl.ANY)
VMEM = pl.BlockSpec(memory_space=pltpu.VMEM)


def pinned(array):
    return pltpu.with_memory_space_constraint(array, pltpu.VMEM)


def held(array):
    return pltpu.with_memory_space_constraint(array, pltpu.HBM)


def call(kernel, ins, in_specs, outs, scratch, aliases, flops, scoped=0):
    return pl.pallas_call(
        kernel,
        out_shape=outs,
        in_specs=in_specs,
        out_specs=[VMEM] * len(outs),
        scratch_shapes=scratch,
        input_output_aliases=aliases,
        compiler_params=pltpu.CompilerParams(vmem_limit_bytes=SCOPED_BYTES + scoped),
        cost_estimate=pl.CostEstimate(flops=flops, bytes_accessed=4 << 20, transcendentals=0),
    )(*ins)


def local(block_values, block_pairs, live_counts, occupied):
    owners = lax.axis_size("aux")
    me = lax.axis_index("aux")
    core, chip = me % 2, me // 2
    shard, width = occupied.shape
    total = owners * shard
    slots = block_values.shape[0]
    piece = math.gcd(BLK, shard)
    pieces = BLK // piece
    chips = owners // 2
    lined = chips == 2 * LINE
    same_core = [[2 * i + k for i in range(chips)] for k in range(2)]
    swap = [(i, i ^ 1) for i in range(owners)]

    mine = lax.dynamic_slice_in_dim(occupied, core * LANES, LANES, 1)
    given = lax.dynamic_slice_in_dim(occupied, (1 - core) * LANES, LANES, 1)
    parts = [mine, move(given, swap)]
    others = [move(array, swap) for array in (block_values, block_pairs, live_counts)]
    raw_sets = [block_values, others[0]]
    tile_sets = []

    def lay_tiles():
        tile_sets[:] = [values.reshape(slots, BLK * BLK // LANES, LANES) for values in raw_sets]

    slot_ids = jnp.arange(chips, dtype=jnp.int32)
    chip_of_slot = slot_ids
    stage_count = 1
    if lined:
        chip_of_slot = (slot_ids + chip // 2) % LINE * 2 + ((slot_ids // LINE) ^ (chip % 2))
        stage_count = LINE + 1

    tile_ids = jnp.arange(2 * slots, dtype=jnp.int32)
    pairs = jnp.concatenate([block_pairs, others[1]])
    live = tile_ids % slots < jnp.where(tile_ids < slots, live_counts[0], others[2][0])
    first = pairs[:, 1][:, None] * BLK + jnp.arange(pieces, dtype=jnp.int32) * piece
    owner = first // shard
    part = (owner % 2) ^ core
    owner_chip = owner // 2
    if lined:
        back = (chip // 2 - owner_chip // 2) % LINE
        side = (owner_chip % 2) ^ (chip % 2)
        stage = (back + side)[:, 0]
        slot_of = part + 2 * jnp.where(back + side < LINE, side, 0)
    else:
        stage = jnp.zeros_like(tile_ids)
        slot_of = part * chips + owner_chip
    spots = slot_of * shard + first % shard
    stage = jnp.where(live, stage, stage_count)
    rows = pairs[:, 0] * BLK + tile_ids // slots * total
    ahead = (stage[None, :] < stage[:, None]) | (
        (stage[None, :] == stage[:, None]) & (tile_ids[None, :] < tile_ids[:, None])
    )
    rank = jnp.sum(ahead.astype(jnp.int32), axis=1)
    entries = jnp.arange(2 * slots + UNROLL, dtype=jnp.int32)
    chosen = rank[None, :] == entries[:, None]
    columns = [tile_ids, rows] + [spots[:, cut] for cut in range(pieces)]
    ordered = jnp.concatenate([jnp.sum(jnp.where(chosen, column[None, :], 0), axis=1) for column in columns])
    bounds = jnp.sum((stage[None, :] < jnp.arange(stage_count + 1)[:, None]).astype(jnp.int32), axis=1)
    cores = core.astype(jnp.int32).reshape(1)

    half_type = pltpu.VMEM((2 * total + BLK, LANES), jnp.float32)
    tiles_type = pltpu.VMEM((2 * slots, BLK * BLK // LANES, LANES), jnp.bfloat16)
    work = 4 * slots * BLK * BLK * LANES // stage_count
    state = []

    def run_stage(kernel, sources, tables, outs, flops):
        rows = len(sources) * sources[0].shape[0]
        scratch = [pltpu.VMEM((rows, LANES), jnp.bfloat16), pltpu.SemaphoreType.DMA((3,))]
        ins, specs = [*tables, *sources], [SMEM] * len(tables) + [HBM] * len(sources)
        made, aliases = [half_type], {}
        if state:
            aliases = {len(ins) + 1: 0}
            ins, specs = ins + [pinned(state[1]), pinned(state[0])], specs + [VMEM] * 2
        else:
            ins = [*tables, *map(held, sources), tile_sets[0], held(tile_sets[1])]
            specs = specs + [HBM] * 2
            made = [half_type, tiles_type]
        results = call(kernel, ins, specs, made + outs, scratch, aliases, flops, 2 * rows * LANES)
        state[:] = [results[0], state[1] if state else results[1]]
        return results[len(made) :]

    def add(stage, sources):
        kernel = functools.partial(stage_kernel, stage, len(sources), pieces)
        run_stage(kernel, sources, [ordered, bounds], [], work)

    def meanwhile(step, index, arrived, moved):
        if (step, index) == RAW_AT:
            moved, *raw_sets[:] = tie(moved, *raw_sets)
            lay_tiles()
        if (step, index) == LAY_AT:
            moved, *tile_sets[:] = tie(moved, *tile_sets)
        if (step, index) in ADD_AT:
            stage = ADD_AT[step, index]
            add(stage, arrived(stage))
            moved, state[0] = tie(moved, state[0])
        return moved

    if lined:
        stages = spread(parts, meanwhile)
        for stage in range(len(ADD_AT), LINE):
            add(stage, stages[stage])
    else:
        lay_tiles()
        stages = [[lax.all_gather(part, "aux", axis_index_groups=same_core, axis=0, tiled=True) for part in parts]]

    group = 1 if lined else chips

    def window_types(plan, keeps):
        return [pltpu.VMEM((group, shard, WIN), jnp.float32 if keeps else jnp.bfloat16) for _ in plan]

    def first_sends(plan):
        weights, *blocks = run_stage(
            functools.partial(window_kernel, stage_count - 1, len(stages[-1]), pieces, shard, plan),
            stages[-1],
            [ordered, bounds, chip_of_slot, cores],
            [pltpu.VMEM((2 * LANES, WIN), jnp.bfloat16)] + window_types(plan, False),
            work + len(plan) * group * shard * width * WIN * 2,
        )
        state.append(weights)
        return blocks

    def blocks_of(plan, keeps):
        if len(state) < 3:
            blocks = first_sends(plan)
        else:
            blocks = call(
                functools.partial(rest_kernel, shard, plan, keeps),
                [chip_of_slot, cores, pinned(state[0]), pinned(state[2])],
                [SMEM] * 2 + [VMEM] * 2,
                window_types(plan, keeps),
                [],
                {},
                len(plan) * group * shard * width * WIN * 2,
            )
        return [block[0] for block in blocks] if lined else blocks

    def hold(*arrays):
        state[0], *arrays = tie(state[0], *arrays)
        return arrays

    blocks_of.hold = hold
    factor = 1.0 / math.sqrt(owners * width)
    if lined:
        return collect(blocks_of, swap) * factor
    (send,), (keep,) = blocks_of([0], False), blocks_of([0], True)
    pair_sum = (keep + move(send, swap).astype(jnp.float32)).astype(jnp.bfloat16)
    block_sum = lax.psum_scatter(
        pair_sum.reshape(total // 2, WIN), "aux", axis_index_groups=same_core, scatter_dimension=0, tiled=True
    )
    return block_sum.astype(jnp.float32) * factor


def solution(mesh):
    placed = (
        P(("groups", "aux"), None),
        P(("groups", "aux"), None),
        P(("groups", "aux")),
        P(("groups", "aux"), None),
    )
    return jax.shard_map(
        local, mesh=mesh, in_specs=placed, out_specs=P(("groups", "aux"), None), check_vma=False
    )
```

```python
import functools
import math

import jax
import jax.numpy as jnp
from jax import lax
from jax.experimental import pallas as pl
from jax.experimental.pallas import tpu as pltpu
from jax.sharding import PartitionSpec as P

BLK = 64
WIN = 128
LANES = 128
UNROLL = 16
LINE = 4
SCOPED_BYTES = 6 * 1024 * 1024


def place(z, x, core):
    return (z * 2 + x) * 2 + core


def pairs_of(step):
    return [
        (place(z, x, core), place(*step(z, x), core)) for z in range(LINE) for x in range(2) for core in range(2)
    ]


def tie(*arrays):
    return lax.optimization_barrier(arrays)


def move(array, pairs):
    return lax.ppermute(array, "aux", pairs)


ALONG = pairs_of(lambda z, x: ((z + 1) % LINE, x))
BACK = pairs_of(lambda z, x: ((z - 1) % LINE, x))
ACROSS = pairs_of(lambda z, x: (z, 1 - x))
NEAR0, NEAR1, NEAR2, NEAR3, FAR0, FAR1, FAR2, FAR3 = range(2 * LINE)
ADD_AT = {(2, 1): 0, (3, 0): 1}
RAW_AT, LAY_AT = (0, 1), (1, 1)


def spread(parts, meanwhile):
    lines, others = [[part] for part in parts], [[] for _ in parts]

    def arrived(stage):
        held = [line[stage] for line in lines] if stage < LINE else []
        return held + ([other[stage - 1] for other in others] if stage else [])

    for step in range(LINE):
        for index, (line, other) in enumerate(zip(lines, others)):
            if other:
                line[-1], other[-1] = tie(line[-1], other[-1])
            turn = step == LINE - 1 and index == 0
            source = other if turn else line
            source[-1] = meanwhile(step, index, arrived, source[-1])
            now = source[-1]
            if step + 1 < LINE:
                line.append(move(now, ALONG))
            other.append(move(now, ALONG if turn else ACROSS))
    return [arrived(stage) for stage in range(LINE + 1)]


def collect(blocks_of, swap):
    def halves(array):
        return array[: array.shape[0] // 2], array[array.shape[0] // 2 :]

    def narrow(array):
        return array.astype(jnp.bfloat16)

    def wide(array):
        return array.astype(jnp.float32)

    def paired(send, keep):
        return keep + wide(move(send, swap))

    first = [FAR2, FAR1, FAR3, NEAR2]
    rest = [NEAR1, FAR0, NEAR3, NEAR0]
    sends = blocks_of(first, False)
    total = {name: paired(*pair) for name, *pair in zip(first, sends, blocks_of(first, True))}
    crossing, aside = list(map(narrow, halves(total[FAR2]))), narrow(total[FAR1])
    *crossing, aside = blocks_of.hold(*crossing, aside)
    two_on = [move(part, ACROSS) for part in crossing]
    joining = move(aside, ALONG)
    total.update({name: paired(*pair) for name, *pair in zip(rest, blocks_of(rest, False), blocks_of(rest, True))})

    two_on[1], joining = tie(two_on[1], joining)
    crossing, two_on[0] = tie(narrow(total[FAR3]), two_on[0])
    three_on = move(crossing, ACROSS)
    crossing, three_on = tie(narrow(total[FAR0] + wide(joining)), three_on)
    straight = move(crossing, ACROSS)
    two_on = [move(narrow(own + wide(part)), ALONG) for own, part in zip(halves(total[NEAR2]), two_on)]
    later, two_on[0] = tie(total[NEAR1], two_on[0])
    one_on = [
        move(narrow(halves(own)[index] + wide(two_on[index])), ALONG)
        for index, own in enumerate((total[NEAR1], later))
    ]
    one_back = move(narrow(total[NEAR3] + wide(three_on)), BACK)
    (result,) = tie(total[NEAR0] + wide(jnp.concatenate(one_on)))
    return result + wide(straight) + wide(one_back)


def clear(half):
    whole = half.shape[0] // (4 * BLK) * (4 * BLK)

    @pl.loop(0, whole // (4 * BLK))
    def _(index):
        half[pl.ds(pl.multiple_of(index * 4 * BLK, BLK), 4 * BLK), :] = jnp.zeros((4 * BLK, LANES), jnp.float32)

    half[pl.ds(whole, half.shape[0] - whole), :] = jnp.zeros((half.shape[0] - whole, LANES), jnp.float32)


def add_tiles(stage, pieces, table_ref, bounds_ref, tiles, half, occ, sem):
    pltpu.make_async_copy(occ, occ, sem).wait()
    begin, end = bounds_ref[stage], bounds_ref[stage + 1]
    low = lax.broadcasted_iota(jnp.int32, tiles.shape[1:], 1) < BLK
    zero = jnp.zeros(tiles.shape[1:], jnp.bfloat16)
    spill = half.shape[0] - BLK
    entries = table_ref.shape[0] // (2 + pieces)
    piece = BLK // pieces

    @pl.loop(0, (end - begin + UNROLL - 1) // UNROLL)
    def _(group):
        products, starts = [], []
        for lane in range(UNROLL):
            entry = begin + group * UNROLL + lane
            tile = table_ref[entry]
            starts.append(jnp.where(entry < end, table_ref[entries + entry], spill))
            spots = [jnp.where(entry < end, table_ref[(2 + cut) * entries + entry], 0) for cut in range(pieces)]
            parts = [occ[pl.ds(pl.multiple_of(spot, piece), piece), :] for spot in spots]
            pair = tiles[tile]
            left = jnp.concatenate([jnp.where(low, pair, zero), jnp.where(low, zero, pair)], axis=0)
            block = jnp.concatenate(parts * 2, axis=0)
            products.append(jnp.dot(left, block, preferred_element_type=jnp.float32))
        for product, start in zip(products, starts):
            start = pl.multiple_of(start, BLK)
            for odd in range(2):
                span = pl.ds(start + odd, BLK // 2, stride=2)
                half[span, :] += product[odd * (BLK // 2) : (odd + 1) * (BLK // 2)]


def fill_window(half, weights, shard, chips_ref, first, parity, out):
    side_rows = (half.shape[0] - BLK) // 2

    @pl.loop(0, out.shape[0])
    def _(index):
        start = pl.multiple_of((2 * chips_ref[first + index] + parity) * shard, 32)
        both = jnp.concatenate(
            [half[pl.ds(side * side_rows + start, shard), :].astype(jnp.bfloat16) for side in range(2)], axis=1
        )
        out[index] = jnp.dot(both, weights[...], preferred_element_type=jnp.float32).astype(out.dtype)


def load_tiles(tile_sets, tiles, sems):
    slots = tile_sets[0].shape[0]
    copies = [
        pltpu.make_async_copy(source, tiles.at[pl.ds(index * slots, slots)], sems.at[index])
        for index, source in enumerate(tile_sets)
    ]
    for copy in copies:
        copy.start()
    return copies


def add_stage(stage, count, pieces, table_ref, bounds_ref, refs):
    sources = refs[:count]
    *_, occ, sems = refs
    rows = sources[0].shape[0]
    for index, source in enumerate(sources):
        pltpu.make_async_copy(source, occ.at[pl.ds(index * rows, rows)], sems.at[2]).start()
    if stage:
        tiles, _, half, *outs = refs[count:-2]
        copies = []
    else:
        *tile_sets, half, tiles = refs[count : count + 4]
        outs = refs[count + 4 : -2]
        copies = load_tiles(tile_sets, tiles, sems)
        clear(half)
    for copy in copies:
        copy.wait()
    add_tiles(stage, pieces, table_ref, bounds_ref, tiles, half, occ, sems.at[2])
    return half, outs


def stage_kernel(stage, count, pieces, table_ref, bounds_ref, *refs):
    add_stage(stage, count, pieces, table_ref, bounds_ref, refs)


def window_kernel(stage, count, pieces, shard, plan, table_ref, bounds_ref, chips_ref, core_ref, *refs):
    half, (weights, *outs) = add_stage(stage, count, pieces, table_ref, bounds_ref, refs)
    side_rows = (half.shape[0] - BLK) // 2
    for side in range(2):
        weights[pl.ds(side * LANES, LANES), :] = half[pl.ds(side * side_rows, WIN), :].T.astype(jnp.bfloat16)
    rest_kernel(shard, plan, False, chips_ref, core_ref, half, weights, *outs)


def rest_kernel(shard, plan, keeps, chips_ref, core_ref, half, weights, *outs):
    for first, out in zip(plan, outs):
        fill_window(half, weights, shard, chips_ref, first, core_ref[0] if keeps else 1 - core_ref[0], out)


SMEM = pl.BlockSpec(memory_space=pltpu.SMEM)
HBM = pl.BlockSpec(memory_space=pl.ANY)
VMEM = pl.BlockSpec(memory_space=pltpu.VMEM)


def pinned(array):
    return pltpu.with_memory_space_constraint(array, pltpu.VMEM)


def held(array):
    return pltpu.with_memory_space_constraint(array, pltpu.HBM)


def call(kernel, ins, in_specs, outs, scratch, aliases, flops, scoped=0):
    return pl.pallas_call(
        kernel,
        out_shape=outs,
        in_specs=in_specs,
        out_specs=[VMEM] * len(outs),
        scratch_shapes=scratch,
        input_output_aliases=aliases,
        compiler_params=pltpu.CompilerParams(vmem_limit_bytes=SCOPED_BYTES + scoped),
        cost_estimate=pl.CostEstimate(flops=flops, bytes_accessed=4 << 20, transcendentals=0),
    )(*ins)


def local(block_values, block_pairs, live_counts, occupied):
    owners = lax.axis_size("aux")
    me = lax.axis_index("aux")
    core, chip = me % 2, me // 2
    shard, width = occupied.shape
    total = owners * shard
    slots = block_values.shape[0]
    piece = math.gcd(BLK, shard)
    pieces = BLK // piece
    chips = owners // 2
    lined = chips == 2 * LINE
    same_core = [[2 * i + k for i in range(chips)] for k in range(2)]
    swap = [(i, i ^ 1) for i in range(owners)]

    mine = lax.dynamic_slice_in_dim(occupied, core * LANES, LANES, 1)
    given = lax.dynamic_slice_in_dim(occupied, (1 - core) * LANES, LANES, 1)
    parts = [mine, move(given, swap)]
    others = [move(array, swap) for array in (block_values, block_pairs, live_counts)]
    raw_sets = [block_values, others[0]]
    tile_sets = []

    def lay_tiles():
        tile_sets[:] = [values.reshape(slots, BLK * BLK // LANES, LANES) for values in raw_sets]

    slot_ids = jnp.arange(chips, dtype=jnp.int32)
    chip_of_slot = slot_ids
    stage_count = 1
    if lined:
        chip_of_slot = (slot_ids + chip // 2) % LINE * 2 + ((slot_ids // LINE) ^ (chip % 2))
        stage_count = LINE + 1

    tile_ids = jnp.arange(2 * slots, dtype=jnp.int32)
    pairs = jnp.concatenate([block_pairs, others[1]])
    live = tile_ids % slots < jnp.where(tile_ids < slots, live_counts[0], others[2][0])
    first = pairs[:, 1][:, None] * BLK + jnp.arange(pieces, dtype=jnp.int32) * piece
    owner = first // shard
    part = (owner % 2) ^ core
    owner_chip = owner // 2
    if lined:
        back = (chip // 2 - owner_chip // 2) % LINE
        side = (owner_chip % 2) ^ (chip % 2)
        stage = (back + side)[:, 0]
        slot_of = part + 2 * jnp.where(back + side < LINE, side, 0)
    else:
        stage = jnp.zeros_like(tile_ids)
        slot_of = part * chips + owner_chip
    spots = slot_of * shard + first % shard
    stage = jnp.where(live, stage, stage_count)
    rows = pairs[:, 0] * BLK + tile_ids // slots * total
    ahead = (stage[None, :] < stage[:, None]) | (
        (stage[None, :] == stage[:, None]) & (tile_ids[None, :] < tile_ids[:, None])
    )
    rank = jnp.sum(ahead.astype(jnp.int32), axis=1)
    entries = jnp.arange(2 * slots + UNROLL, dtype=jnp.int32)
    chosen = rank[None, :] == entries[:, None]
    columns = [tile_ids, rows] + [spots[:, cut] for cut in range(pieces)]
    ordered = jnp.concatenate([jnp.sum(jnp.where(chosen, column[None, :], 0), axis=1) for column in columns])
    bounds = jnp.sum((stage[None, :] < jnp.arange(stage_count + 1)[:, None]).astype(jnp.int32), axis=1)
    cores = core.astype(jnp.int32).reshape(1)

    half_type = pltpu.VMEM((2 * total + BLK, LANES), jnp.float32)
    tiles_type = pltpu.VMEM((2 * slots, BLK * BLK // LANES, LANES), jnp.bfloat16)
    work = 4 * slots * BLK * BLK * LANES // stage_count
    state = []

    def run_stage(kernel, sources, tables, outs, flops):
        rows = len(sources) * sources[0].shape[0]
        scratch = [pltpu.VMEM((rows, LANES), jnp.bfloat16), pltpu.SemaphoreType.DMA((3,))]
        ins, specs = [*tables, *sources], [SMEM] * len(tables) + [HBM] * len(sources)
        made, aliases = [half_type], {}
        if state:
            aliases = {len(ins) + 1: 0}
            ins, specs = ins + [pinned(state[1]), pinned(state[0])], specs + [VMEM] * 2
        else:
            ins = [*tables, *map(held, sources), tile_sets[0], held(tile_sets[1])]
            specs = specs + [HBM] * 2
            made = [half_type, tiles_type]
        results = call(kernel, ins, specs, made + outs, scratch, aliases, flops, 2 * rows * LANES)
        state[:] = [results[0], state[1] if state else results[1]]
        return results[len(made) :]

    def add(stage, sources):
        kernel = functools.partial(stage_kernel, stage, len(sources), pieces)
        run_stage(kernel, sources, [ordered, bounds], [], work)

    def meanwhile(step, index, arrived, moved):
        if (step, index) == RAW_AT:
            moved, *raw_sets[:] = tie(moved, *raw_sets)
            lay_tiles()
        if (step, index) == LAY_AT:
            moved, *tile_sets[:] = tie(moved, *tile_sets)
        if (step, index) in ADD_AT:
            stage = ADD_AT[step, index]
            add(stage, arrived(stage))
            moved, state[0] = tie(moved, state[0])
        return moved

    if lined:
        stages = spread(parts, meanwhile)
        for stage in range(len(ADD_AT), LINE):
            add(stage, stages[stage])
    else:
        lay_tiles()
        stages = [[lax.all_gather(part, "aux", axis_index_groups=same_core, axis=0, tiled=True) for part in parts]]

    group = 1 if lined else chips

    def window_types(plan, keeps):
        return [pltpu.VMEM((group, shard, WIN), jnp.float32 if keeps else jnp.bfloat16) for _ in plan]

    def first_sends(plan):
        weights, *blocks = run_stage(
            functools.partial(window_kernel, stage_count - 1, len(stages[-1]), pieces, shard, plan),
            stages[-1],
            [ordered, bounds, chip_of_slot, cores],
            [pltpu.VMEM((2 * LANES, WIN), jnp.bfloat16)] + window_types(plan, False),
            work + len(plan) * group * shard * width * WIN * 2,
        )
        state.append(weights)
        return blocks

    def blocks_of(plan, keeps):
        if len(state) < 3:
            blocks = first_sends(plan)
        else:
            blocks = call(
                functools.partial(rest_kernel, shard, plan, keeps),
                [chip_of_slot, cores, pinned(state[0]), pinned(state[2])],
                [SMEM] * 2 + [VMEM] * 2,
                window_types(plan, keeps),
                [],
                {},
                len(plan) * group * shard * width * WIN * 2,
            )
        return [block[0] for block in blocks] if lined else blocks

    def hold(*arrays):
        state[0], *arrays = tie(state[0], *arrays)
        return arrays

    blocks_of.hold = hold
    factor = 1.0 / math.sqrt(owners * width)
    if lined:
        return collect(blocks_of, swap) * factor
    (send,), (keep,) = blocks_of([0], False), blocks_of([0], True)
    pair_sum = (keep + move(send, swap).astype(jnp.float32)).astype(jnp.bfloat16)
    block_sum = lax.psum_scatter(
        pair_sum.reshape(total // 2, WIN), "aux", axis_index_groups=same_core, scatter_dimension=0, tiled=True
    )
    return block_sum.astype(jnp.float32) * factor


def solution(mesh):
    placed = (
        P(("groups", "aux"), None),
        P(("groups", "aux"), None),
        P(("groups", "aux")),
        P(("groups", "aux"), None),
    )
    return jax.shard_map(
        local, mesh=mesh, in_specs=placed, out_specs=P(("groups", "aux"), None), check_vma=False
    )
```

```python
import functools
import math

import jax
import jax.numpy as jnp
from jax import lax
from jax.experimental import pallas as pl
from jax.experimental.pallas import tpu as pltpu
from jax.sharding import PartitionSpec as P

BLK = 64
WIN = 128
LANES = 128
UNROLL = 16
LINE = 4
SCOPED_BYTES = 6 * 1024 * 1024


def place(z, x, core):
    return (z * 2 + x) * 2 + core


def pairs_of(step):
    return [
        (place(z, x, core), place(*step(z, x), core)) for z in range(LINE) for x in range(2) for core in range(2)
    ]


def tie(*arrays):
    return lax.optimization_barrier(arrays)


def move(array, pairs):
    return lax.ppermute(array, "aux", pairs)


ALONG = pairs_of(lambda z, x: ((z + 1) % LINE, x))
BACK = pairs_of(lambda z, x: ((z - 1) % LINE, x))
ACROSS = pairs_of(lambda z, x: (z, 1 - x))
NEAR0, NEAR1, NEAR2, NEAR3, FAR0, FAR1, FAR2, FAR3 = range(2 * LINE)
ADD_AT = {(2, 1): 0, (3, 0): 1}
RAW_AT, LAY_AT = (0, 1), (1, 1)


def spread(parts, meanwhile):
    lines, others = [[part] for part in parts], [[] for _ in parts]

    def arrived(stage):
        held = [line[stage] for line in lines] if stage < LINE else []
        return held + ([other[stage - 1] for other in others] if stage else [])

    for step in range(LINE):
        for index, (line, other) in enumerate(zip(lines, others)):
            if other:
                line[-1], other[-1] = tie(line[-1], other[-1])
            turn = step == LINE - 1 and index == 0
            source = other if turn else line
            source[-1] = meanwhile(step, index, arrived, source[-1])
            now = source[-1]
            if step + 1 < LINE:
                line.append(move(now, ALONG))
            other.append(move(now, ALONG if turn else ACROSS))
    return [arrived(stage) for stage in range(LINE + 1)]


def collect(blocks_of, swap):
    def halves(array):
        return array[: array.shape[0] // 2], array[array.shape[0] // 2 :]

    def narrow(array):
        return array.astype(jnp.bfloat16)

    def wide(array):
        return array.astype(jnp.float32)

    def paired(send, keep):
        return keep + wide(move(send, swap))

    first = [FAR2, FAR1, FAR3, NEAR2]
    rest = [NEAR1, FAR0, NEAR3, NEAR0]
    sends = blocks_of(first, False)
    total = {name: paired(*pair) for name, *pair in zip(first, sends, blocks_of(first, True))}
    aside, beside = map(narrow, halves(total[FAR1]))
    crossing = narrow(total[FAR2])
    crossing, aside, beside = blocks_of.hold(crossing, aside, beside)
    two_on = move(crossing, ACROSS)
    joining = move(aside, ALONG)
    total.update({name: paired(*pair) for name, *pair in zip(rest, blocks_of(rest, False), blocks_of(rest, True))})

    two_on, joining = tie(two_on, joining)
    beside, two_on = tie(beside, two_on)
    beside = move(beside, ACROSS)
    three_on, two_on = tie(narrow(total[FAR3]), two_on)
    three_on = move(three_on, ACROSS)
    two_on = move(narrow(total[NEAR2] + wide(two_on)), ALONG)
    rows = beside.shape[0]
    beside, joining = jnp.pad(wide(beside), ((rows, 0), (0, 0))), jnp.pad(wide(joining), ((0, rows), (0, 0)))
    one_on = move(narrow(total[NEAR1] + wide(two_on) + beside), ALONG)
    total[FAR0], two_on = tie(total[FAR0], two_on)
    crossing, three_on = tie(narrow(total[FAR0] + joining), three_on)
    straight = move(crossing, ACROSS)
    one_back = move(narrow(total[NEAR3] + wide(three_on)), BACK)
    return total[NEAR0] + wide(one_on) + wide(straight) + wide(one_back)


def clear(half):
    whole = half.shape[0] // (4 * BLK) * (4 * BLK)

    @pl.loop(0, whole // (4 * BLK))
    def _(index):
        half[pl.ds(pl.multiple_of(index * 4 * BLK, BLK), 4 * BLK), :] = jnp.zeros((4 * BLK, LANES), jnp.float32)

    half[pl.ds(whole, half.shape[0] - whole), :] = jnp.zeros((half.shape[0] - whole, LANES), jnp.float32)


def add_tiles(stage, pieces, table_ref, bounds_ref, tiles, half, occ, sem):
    pltpu.make_async_copy(occ, occ, sem).wait()
    begin, end = bounds_ref[stage], bounds_ref[stage + 1]
    low = lax.broadcasted_iota(jnp.int32, tiles.shape[1:], 1) < BLK
    zero = jnp.zeros(tiles.shape[1:], jnp.bfloat16)
    spill = half.shape[0] - BLK
    entries = table_ref.shape[0] // (2 + pieces)
    piece = BLK // pieces

    @pl.loop(0, (end - begin + UNROLL - 1) // UNROLL)
    def _(group):
        products, starts = [], []
        for lane in range(UNROLL):
            entry = begin + group * UNROLL + lane
            tile = table_ref[entry]
            starts.append(jnp.where(entry < end, table_ref[entries + entry], spill))
            spots = [jnp.where(entry < end, table_ref[(2 + cut) * entries + entry], 0) for cut in range(pieces)]
            parts = [occ[pl.ds(pl.multiple_of(spot, piece), piece), :] for spot in spots]
            pair = tiles[tile]
            left = jnp.concatenate([jnp.where(low, pair, zero), jnp.where(low, zero, pair)], axis=0)
            block = jnp.concatenate(parts * 2, axis=0)
            products.append(jnp.dot(left, block, preferred_element_type=jnp.float32))
        for product, start in zip(products, starts):
            start = pl.multiple_of(start, BLK)
            for odd in range(2):
                span = pl.ds(start + odd, BLK // 2, stride=2)
                half[span, :] += product[odd * (BLK // 2) : (odd + 1) * (BLK // 2)]


def fill_window(half, weights, shard, chips_ref, first, parity, out):
    side_rows = (half.shape[0] - BLK) // 2

    @pl.loop(0, out.shape[0])
    def _(index):
        start = pl.multiple_of((2 * chips_ref[first + index] + parity) * shard, 32)
        both = jnp.concatenate(
            [half[pl.ds(side * side_rows + start, shard), :].astype(jnp.bfloat16) for side in range(2)], axis=1
        )
        out[index] = jnp.dot(both, weights[...], preferred_element_type=jnp.float32).astype(out.dtype)


def load_tiles(tile_sets, tiles, sems):
    slots = tile_sets[0].shape[0]
    copies = [
        pltpu.make_async_copy(source, tiles.at[pl.ds(index * slots, slots)], sems.at[index])
        for index, source in enumerate(tile_sets)
    ]
    for copy in copies:
        copy.start()
    return copies


def add_stage(stage, count, pieces, table_ref, bounds_ref, refs):
    sources = refs[:count]
    *_, occ, sems = refs
    rows = sources[0].shape[0]
    for index, source in enumerate(sources):
        pltpu.make_async_copy(source, occ.at[pl.ds(index * rows, rows)], sems.at[2]).start()
    if stage:
        tiles, _, half, *outs = refs[count:-2]
        copies = []
    else:
        *tile_sets, half, tiles = refs[count : count + 4]
        outs = refs[count + 4 : -2]
        copies = load_tiles(tile_sets, tiles, sems)
        clear(half)
    for copy in copies:
        copy.wait()
    add_tiles(stage, pieces, table_ref, bounds_ref, tiles, half, occ, sems.at[2])
    return half, outs


def stage_kernel(stage, count, pieces, table_ref, bounds_ref, *refs):
    add_stage(stage, count, pieces, table_ref, bounds_ref, refs)


def window_kernel(stage, count, pieces, shard, plan, table_ref, bounds_ref, chips_ref, core_ref, *refs):
    half, (weights, *outs) = add_stage(stage, count, pieces, table_ref, bounds_ref, refs)
    side_rows = (half.shape[0] - BLK) // 2
    for side in range(2):
        weights[pl.ds(side * LANES, LANES), :] = half[pl.ds(side * side_rows, WIN), :].T.astype(jnp.bfloat16)
    rest_kernel(shard, plan, False, chips_ref, core_ref, half, weights, *outs)


def rest_kernel(shard, plan, keeps, chips_ref, core_ref, half, weights, *outs):
    for first, out in zip(plan, outs):
        fill_window(half, weights, shard, chips_ref, first, core_ref[0] if keeps else 1 - core_ref[0], out)


SMEM = pl.BlockSpec(memory_space=pltpu.SMEM)
HBM = pl.BlockSpec(memory_space=pl.ANY)
VMEM = pl.BlockSpec(memory_space=pltpu.VMEM)


def pinned(array):
    return pltpu.with_memory_space_constraint(array, pltpu.VMEM)


def held(array):
    return pltpu.with_memory_space_constraint(array, pltpu.HBM)


def call(kernel, ins, in_specs, outs, scratch, aliases, flops, scoped=0):
    return pl.pallas_call(
        kernel,
        out_shape=outs,
        in_specs=in_specs,
        out_specs=[VMEM] * len(outs),
        scratch_shapes=scratch,
        input_output_aliases=aliases,
        compiler_params=pltpu.CompilerParams(vmem_limit_bytes=SCOPED_BYTES + scoped),
        cost_estimate=pl.CostEstimate(flops=flops, bytes_accessed=4 << 20, transcendentals=0),
    )(*ins)


def local(block_values, block_pairs, live_counts, occupied):
    owners = lax.axis_size("aux")
    me = lax.axis_index("aux")
    core, chip = me % 2, me // 2
    shard, width = occupied.shape
    total = owners * shard
    slots = block_values.shape[0]
    piece = math.gcd(BLK, shard)
    pieces = BLK // piece
    chips = owners // 2
    lined = chips == 2 * LINE
    same_core = [[2 * i + k for i in range(chips)] for k in range(2)]
    swap = [(i, i ^ 1) for i in range(owners)]

    mine = lax.dynamic_slice_in_dim(occupied, core * LANES, LANES, 1)
    given = lax.dynamic_slice_in_dim(occupied, (1 - core) * LANES, LANES, 1)
    parts = [mine, move(given, swap)]
    others = [move(array, swap) for array in (block_values, block_pairs, live_counts)]
    raw_sets = [block_values, others[0]]
    tile_sets = []

    def lay_tiles():
        tile_sets[:] = [values.reshape(slots, BLK * BLK // LANES, LANES) for values in raw_sets]

    slot_ids = jnp.arange(chips, dtype=jnp.int32)
    chip_of_slot = slot_ids
    stage_count = 1
    if lined:
        chip_of_slot = (slot_ids + chip // 2) % LINE * 2 + ((slot_ids // LINE) ^ (chip % 2))
        stage_count = LINE + 1

    tile_ids = jnp.arange(2 * slots, dtype=jnp.int32)
    pairs = jnp.concatenate([block_pairs, others[1]])
    live = tile_ids % slots < jnp.where(tile_ids < slots, live_counts[0], others[2][0])
    first = pairs[:, 1][:, None] * BLK + jnp.arange(pieces, dtype=jnp.int32) * piece
    owner = first // shard
    part = (owner % 2) ^ core
    owner_chip = owner // 2
    if lined:
        back = (chip // 2 - owner_chip // 2) % LINE
        side = (owner_chip % 2) ^ (chip % 2)
        stage = (back + side)[:, 0]
        slot_of = part + 2 * jnp.where(back + side < LINE, side, 0)
    else:
        stage = jnp.zeros_like(tile_ids)
        slot_of = part * chips + owner_chip
    spots = slot_of * shard + first % shard
    stage = jnp.where(live, stage, stage_count)
    rows = pairs[:, 0] * BLK + tile_ids // slots * total
    ahead = (stage[None, :] < stage[:, None]) | (
        (stage[None, :] == stage[:, None]) & (tile_ids[None, :] < tile_ids[:, None])
    )
    rank = jnp.sum(ahead.astype(jnp.int32), axis=1)
    entries = jnp.arange(2 * slots + UNROLL, dtype=jnp.int32)
    chosen = rank[None, :] == entries[:, None]
    columns = [tile_ids, rows] + [spots[:, cut] for cut in range(pieces)]
    ordered = jnp.concatenate([jnp.sum(jnp.where(chosen, column[None, :], 0), axis=1) for column in columns])
    bounds = jnp.sum((stage[None, :] < jnp.arange(stage_count + 1)[:, None]).astype(jnp.int32), axis=1)
    cores = core.astype(jnp.int32).reshape(1)

    half_type = pltpu.VMEM((2 * total + BLK, LANES), jnp.float32)
    tiles_type = pltpu.VMEM((2 * slots, BLK * BLK // LANES, LANES), jnp.bfloat16)
    work = 4 * slots * BLK * BLK * LANES // stage_count
    state = []

    def run_stage(kernel, sources, tables, outs, flops):
        rows = len(sources) * sources[0].shape[0]
        scratch = [pltpu.VMEM((rows, LANES), jnp.bfloat16), pltpu.SemaphoreType.DMA((3,))]
        ins, specs = [*tables, *sources], [SMEM] * len(tables) + [HBM] * len(sources)
        made, aliases = [half_type], {}
        if state:
            aliases = {len(ins) + 1: 0}
            ins, specs = ins + [pinned(state[1]), pinned(state[0])], specs + [VMEM] * 2
        else:
            ins = [*tables, *map(held, sources), tile_sets[0], held(tile_sets[1])]
            specs = specs + [HBM] * 2
            made = [half_type, tiles_type]
        results = call(kernel, ins, specs, made + outs, scratch, aliases, flops, 2 * rows * LANES)
        state[:] = [results[0], state[1] if state else results[1]]
        return results[len(made) :]

    def add(stage, sources):
        kernel = functools.partial(stage_kernel, stage, len(sources), pieces)
        run_stage(kernel, sources, [ordered, bounds], [], work)

    def meanwhile(step, index, arrived, moved):
        if (step, index) == RAW_AT:
            moved, *raw_sets[:] = tie(moved, *raw_sets)
            lay_tiles()
        if (step, index) == LAY_AT:
            moved, *tile_sets[:] = tie(moved, *tile_sets)
        if (step, index) in ADD_AT:
            stage = ADD_AT[step, index]
            add(stage, arrived(stage))
            moved, state[0] = tie(moved, state[0])
        return moved

    if lined:
        stages = spread(parts, meanwhile)
        for stage in range(len(ADD_AT), LINE):
            add(stage, stages[stage])
    else:
        lay_tiles()
        stages = [[lax.all_gather(part, "aux", axis_index_groups=same_core, axis=0, tiled=True) for part in parts]]

    group = 1 if lined else chips

    def window_types(plan, keeps):
        return [pltpu.VMEM((group, shard, WIN), jnp.float32 if keeps else jnp.bfloat16) for _ in plan]

    def first_sends(plan):
        weights, *blocks = run_stage(
            functools.partial(window_kernel, stage_count - 1, len(stages[-1]), pieces, shard, plan),
            stages[-1],
            [ordered, bounds, chip_of_slot, cores],
            [pltpu.VMEM((2 * LANES, WIN), jnp.bfloat16)] + window_types(plan, False),
            work + len(plan) * group * shard * width * WIN * 2,
        )
        state.append(weights)
        return blocks

    def blocks_of(plan, keeps):
        if len(state) < 3:
            blocks = first_sends(plan)
        else:
            blocks = call(
                functools.partial(rest_kernel, shard, plan, keeps),
                [chip_of_slot, cores, pinned(state[0]), pinned(state[2])],
                [SMEM] * 2 + [VMEM] * 2,
                window_types(plan, keeps),
                [],
                {},
                len(plan) * group * shard * width * WIN * 2,
            )
        return [block[0] for block in blocks] if lined else blocks

    def hold(*arrays):
        state[0], *arrays = tie(state[0], *arrays)
        return arrays

    blocks_of.hold = hold
    factor = 1.0 / math.sqrt(owners * width)
    if lined:
        return collect(blocks_of, swap) * factor
    (send,), (keep,) = blocks_of([0], False), blocks_of([0], True)
    pair_sum = (keep + move(send, swap).astype(jnp.float32)).astype(jnp.bfloat16)
    block_sum = lax.psum_scatter(
        pair_sum.reshape(total // 2, WIN), "aux", axis_index_groups=same_core, scatter_dimension=0, tiled=True
    )
    return block_sum.astype(jnp.float32) * factor


def solution(mesh):
    placed = (
        P(("groups", "aux"), None),
        P(("groups", "aux"), None),
        P(("groups", "aux")),
        P(("groups", "aux"), None),
    )
    return jax.shard_map(
        local, mesh=mesh, in_specs=placed, out_specs=P(("groups", "aux"), None), check_vma=False
    )
```

```python
import functools
import math

import jax
import jax.numpy as jnp
from jax import lax
from jax.experimental import pallas as pl
from jax.experimental.pallas import tpu as pltpu
from jax.sharding import PartitionSpec as P

BLK = 64
WIN = 128
LANES = 128
UNROLL = 16
LINE = 4
SCOPED_BYTES = 6 * 1024 * 1024


def place(z, x, core):
    return (z * 2 + x) * 2 + core


def pairs_of(step):
    return [
        (place(z, x, core), place(*step(z, x), core)) for z in range(LINE) for x in range(2) for core in range(2)
    ]


def tie(*arrays):
    return lax.optimization_barrier(arrays)


def move(array, pairs):
    return lax.ppermute(array, "aux", pairs)


ALONG = pairs_of(lambda z, x: ((z + 1) % LINE, x))
BACK = pairs_of(lambda z, x: ((z - 1) % LINE, x))
ACROSS = pairs_of(lambda z, x: (z, 1 - x))
NEAR0, NEAR1, NEAR2, NEAR3, FAR0, FAR1, FAR2, FAR3 = range(2 * LINE)
ADD_AT = {(2, 1): 0, (3, 0): 1}
RAW_AT, LAY_AT = (0, 1), (1, 1)


def spread(parts, meanwhile):
    lines, others = [[part] for part in parts], [[] for _ in parts]

    def arrived(stage):
        held = [line[stage] for line in lines] if stage < LINE else []
        return held + ([other[stage - 1] for other in others] if stage else [])

    for step in range(LINE):
        for index, (line, other) in enumerate(zip(lines, others)):
            if other:
                line[-1], other[-1] = tie(line[-1], other[-1])
            turn = step == LINE - 1 and index == 0
            source = other if turn else line
            source[-1] = meanwhile(step, index, arrived, source[-1])
            now = source[-1]
            if step + 1 < LINE:
                line.append(move(now, ALONG))
            other.append(move(now, ALONG if turn else ACROSS))
    return [arrived(stage) for stage in range(LINE + 1)]


def collect(blocks_of, swap):
    def halves(array):
        return array[: array.shape[0] // 2], array[array.shape[0] // 2 :]

    def narrow(array):
        return array.astype(jnp.bfloat16)

    def wide(array):
        return array.astype(jnp.float32)

    def paired(send, keep):
        return keep + wide(move(send, swap))

    first = [FAR2, FAR1, FAR3, NEAR2]
    rest = [NEAR1, FAR0, NEAR3, NEAR0]
    sends = blocks_of(first, False)
    total = {name: paired(*pair) for name, *pair in zip(first, sends, blocks_of(first, True))}
    aside, beside = map(narrow, halves(total[FAR1]))
    crossing = narrow(total[FAR2])
    crossing, aside, beside = blocks_of.hold(crossing, aside, beside)
    two_on = move(crossing, ACROSS)
    joining = move(aside, ALONG)
    total.update({name: paired(*pair) for name, *pair in zip(rest, blocks_of(rest, False), blocks_of(rest, True))})

    two_on, joining = tie(two_on, joining)
    beside, two_on = tie(beside, two_on)
    beside = move(beside, ACROSS)
    three_on, two_on = tie(narrow(total[FAR3]), two_on)
    three_on = move(three_on, ACROSS)
    two_on = [move(narrow(own + wide(part)), ALONG) for own, part in zip(halves(total[NEAR2]), halves(two_on))]
    two_on[1], three_on = tie(two_on[1], three_on)
    later, two_on[0] = tie(total[NEAR1], two_on[0])
    one_on = [
        move(narrow(halves(total[NEAR1])[0] + wide(two_on[0])), ALONG),
        move(narrow(halves(later)[1] + wide(two_on[1]) + wide(beside)), ALONG),
    ]
    joining = jnp.pad(wide(joining), ((0, joining.shape[0]), (0, 0)))
    total[FAR0], two_on[0] = tie(total[FAR0], two_on[0])
    crossing, three_on = tie(narrow(total[FAR0] + joining), three_on)
    straight = move(crossing, ACROSS)
    one_back = move(narrow(total[NEAR3] + wide(three_on)), BACK)
    return total[NEAR0] + wide(jnp.concatenate(one_on)) + wide(straight) + wide(one_back)


def clear(half):
    whole = half.shape[0] // (4 * BLK) * (4 * BLK)

    @pl.loop(0, whole // (4 * BLK))
    def _(index):
        half[pl.ds(pl.multiple_of(index * 4 * BLK, BLK), 4 * BLK), :] = jnp.zeros((4 * BLK, LANES), jnp.float32)

    half[pl.ds(whole, half.shape[0] - whole), :] = jnp.zeros((half.shape[0] - whole, LANES), jnp.float32)


def add_tiles(stage, pieces, table_ref, bounds_ref, tiles, half, occ, sem):
    pltpu.make_async_copy(occ, occ, sem).wait()
    begin, end = bounds_ref[stage], bounds_ref[stage + 1]
    low = lax.broadcasted_iota(jnp.int32, tiles.shape[1:], 1) < BLK
    zero = jnp.zeros(tiles.shape[1:], jnp.bfloat16)
    spill = half.shape[0] - BLK
    entries = table_ref.shape[0] // (2 + pieces)
    piece = BLK // pieces

    @pl.loop(0, (end - begin + UNROLL - 1) // UNROLL)
    def _(group):
        products, starts = [], []
        for lane in range(UNROLL):
            entry = begin + group * UNROLL + lane
            tile = table_ref[entry]
            starts.append(jnp.where(entry < end, table_ref[entries + entry], spill))
            spots = [jnp.where(entry < end, table_ref[(2 + cut) * entries + entry], 0) for cut in range(pieces)]
            parts = [occ[pl.ds(pl.multiple_of(spot, piece), piece), :] for spot in spots]
            pair = tiles[tile]
            left = jnp.concatenate([jnp.where(low, pair, zero), jnp.where(low, zero, pair)], axis=0)
            block = jnp.concatenate(parts * 2, axis=0)
            products.append(jnp.dot(left, block, preferred_element_type=jnp.float32))
        for product, start in zip(products, starts):
            start = pl.multiple_of(start, BLK)
            for odd in range(2):
                span = pl.ds(start + odd, BLK // 2, stride=2)
                half[span, :] += product[odd * (BLK // 2) : (odd + 1) * (BLK // 2)]


def fill_window(half, weights, shard, chips_ref, first, parity, out):
    side_rows = (half.shape[0] - BLK) // 2

    @pl.loop(0, out.shape[0])
    def _(index):
        start = pl.multiple_of((2 * chips_ref[first + index] + parity) * shard, 32)
        both = jnp.concatenate(
            [half[pl.ds(side * side_rows + start, shard), :].astype(jnp.bfloat16) for side in range(2)], axis=1
        )
        out[index] = jnp.dot(both, weights[...], preferred_element_type=jnp.float32).astype(out.dtype)


def load_tiles(tile_sets, tiles, sems):
    slots = tile_sets[0].shape[0]
    copies = [
        pltpu.make_async_copy(source, tiles.at[pl.ds(index * slots, slots)], sems.at[index])
        for index, source in enumerate(tile_sets)
    ]
    for copy in copies:
        copy.start()
    return copies


def add_stage(stage, count, pieces, table_ref, bounds_ref, refs):
    sources = refs[:count]
    *_, occ, sems = refs
    rows = sources[0].shape[0]
    for index, source in enumerate(sources):
        pltpu.make_async_copy(source, occ.at[pl.ds(index * rows, rows)], sems.at[2]).start()
    if stage:
        tiles, _, half, *outs = refs[count:-2]
        copies = []
    else:
        *tile_sets, half, tiles = refs[count : count + 4]
        outs = refs[count + 4 : -2]
        copies = load_tiles(tile_sets, tiles, sems)
        clear(half)
    for copy in copies:
        copy.wait()
    add_tiles(stage, pieces, table_ref, bounds_ref, tiles, half, occ, sems.at[2])
    return half, outs


def stage_kernel(stage, count, pieces, table_ref, bounds_ref, *refs):
    add_stage(stage, count, pieces, table_ref, bounds_ref, refs)


def window_kernel(stage, count, pieces, shard, plan, table_ref, bounds_ref, chips_ref, core_ref, *refs):
    half, (weights, *outs) = add_stage(stage, count, pieces, table_ref, bounds_ref, refs)
    side_rows = (half.shape[0] - BLK) // 2
    for side in range(2):
        weights[pl.ds(side * LANES, LANES), :] = half[pl.ds(side * side_rows, WIN), :].T.astype(jnp.bfloat16)
    rest_kernel(shard, plan, False, chips_ref, core_ref, half, weights, *outs)


def rest_kernel(shard, plan, keeps, chips_ref, core_ref, half, weights, *outs):
    for first, out in zip(plan, outs):
        fill_window(half, weights, shard, chips_ref, first, core_ref[0] if keeps else 1 - core_ref[0], out)


SMEM = pl.BlockSpec(memory_space=pltpu.SMEM)
HBM = pl.BlockSpec(memory_space=pl.ANY)
VMEM = pl.BlockSpec(memory_space=pltpu.VMEM)


def pinned(array):
    return pltpu.with_memory_space_constraint(array, pltpu.VMEM)


def held(array):
    return pltpu.with_memory_space_constraint(array, pltpu.HBM)


def call(kernel, ins, in_specs, outs, scratch, aliases, flops, scoped=0):
    return pl.pallas_call(
        kernel,
        out_shape=outs,
        in_specs=in_specs,
        out_specs=[VMEM] * len(outs),
        scratch_shapes=scratch,
        input_output_aliases=aliases,
        compiler_params=pltpu.CompilerParams(vmem_limit_bytes=SCOPED_BYTES + scoped),
        cost_estimate=pl.CostEstimate(flops=flops, bytes_accessed=4 << 20, transcendentals=0),
    )(*ins)


def local(block_values, block_pairs, live_counts, occupied):
    owners = lax.axis_size("aux")
    me = lax.axis_index("aux")
    core, chip = me % 2, me // 2
    shard, width = occupied.shape
    total = owners * shard
    slots = block_values.shape[0]
    piece = math.gcd(BLK, shard)
    pieces = BLK // piece
    chips = owners // 2
    lined = chips == 2 * LINE
    same_core = [[2 * i + k for i in range(chips)] for k in range(2)]
    swap = [(i, i ^ 1) for i in range(owners)]

    mine = lax.dynamic_slice_in_dim(occupied, core * LANES, LANES, 1)
    given = lax.dynamic_slice_in_dim(occupied, (1 - core) * LANES, LANES, 1)
    parts = [mine, move(given, swap)]
    others = [move(array, swap) for array in (block_values, block_pairs, live_counts)]
    raw_sets = [block_values, others[0]]
    tile_sets = []

    def lay_tiles():
        tile_sets[:] = [values.reshape(slots, BLK * BLK // LANES, LANES) for values in raw_sets]

    slot_ids = jnp.arange(chips, dtype=jnp.int32)
    chip_of_slot = slot_ids
    stage_count = 1
    if lined:
        chip_of_slot = (slot_ids + chip // 2) % LINE * 2 + ((slot_ids // LINE) ^ (chip % 2))
        stage_count = LINE + 1

    tile_ids = jnp.arange(2 * slots, dtype=jnp.int32)
    pairs = jnp.concatenate([block_pairs, others[1]])
    live = tile_ids % slots < jnp.where(tile_ids < slots, live_counts[0], others[2][0])
    first = pairs[:, 1][:, None] * BLK + jnp.arange(pieces, dtype=jnp.int32) * piece
    owner = first // shard
    part = (owner % 2) ^ core
    owner_chip = owner // 2
    if lined:
        back = (chip // 2 - owner_chip // 2) % LINE
        side = (owner_chip % 2) ^ (chip % 2)
        stage = (back + side)[:, 0]
        slot_of = part + 2 * jnp.where(back + side < LINE, side, 0)
    else:
        stage = jnp.zeros_like(tile_ids)
        slot_of = part * chips + owner_chip
    spots = slot_of * shard + first % shard
    stage = jnp.where(live, stage, stage_count)
    rows = pairs[:, 0] * BLK + tile_ids // slots * total
    ahead = (stage[None, :] < stage[:, None]) | (
        (stage[None, :] == stage[:, None]) & (tile_ids[None, :] < tile_ids[:, None])
    )
    rank = jnp.sum(ahead.astype(jnp.int32), axis=1)
    entries = jnp.arange(2 * slots + UNROLL, dtype=jnp.int32)
    chosen = rank[None, :] == entries[:, None]
    columns = [tile_ids, rows] + [spots[:, cut] for cut in range(pieces)]
    ordered = jnp.concatenate([jnp.sum(jnp.where(chosen, column[None, :], 0), axis=1) for column in columns])
    bounds = jnp.sum((stage[None, :] < jnp.arange(stage_count + 1)[:, None]).astype(jnp.int32), axis=1)
    cores = core.astype(jnp.int32).reshape(1)

    half_type = pltpu.VMEM((2 * total + BLK, LANES), jnp.float32)
    tiles_type = pltpu.VMEM((2 * slots, BLK * BLK // LANES, LANES), jnp.bfloat16)
    work = 4 * slots * BLK * BLK * LANES // stage_count
    state = []

    def run_stage(kernel, sources, tables, outs, flops):
        rows = len(sources) * sources[0].shape[0]
        scratch = [pltpu.VMEM((rows, LANES), jnp.bfloat16), pltpu.SemaphoreType.DMA((3,))]
        ins, specs = [*tables, *sources], [SMEM] * len(tables) + [HBM] * len(sources)
        made, aliases = [half_type], {}
        if state:
            aliases = {len(ins) + 1: 0}
            ins, specs = ins + [pinned(state[1]), pinned(state[0])], specs + [VMEM] * 2
        else:
            ins = [*tables, *map(held, sources), tile_sets[0], held(tile_sets[1])]
            specs = specs + [HBM] * 2
            made = [half_type, tiles_type]
        results = call(kernel, ins, specs, made + outs, scratch, aliases, flops, 2 * rows * LANES)
        state[:] = [results[0], state[1] if state else results[1]]
        return results[len(made) :]

    def add(stage, sources):
        kernel = functools.partial(stage_kernel, stage, len(sources), pieces)
        run_stage(kernel, sources, [ordered, bounds], [], work)

    def meanwhile(step, index, arrived, moved):
        if (step, index) == RAW_AT:
            moved, *raw_sets[:] = tie(moved, *raw_sets)
            lay_tiles()
        if (step, index) == LAY_AT:
            moved, *tile_sets[:] = tie(moved, *tile_sets)
        if (step, index) in ADD_AT:
            stage = ADD_AT[step, index]
            add(stage, arrived(stage))
            moved, state[0] = tie(moved, state[0])
        return moved

    if lined:
        stages = spread(parts, meanwhile)
        for stage in range(len(ADD_AT), LINE):
            add(stage, stages[stage])
    else:
        lay_tiles()
        stages = [[lax.all_gather(part, "aux", axis_index_groups=same_core, axis=0, tiled=True) for part in parts]]

    group = 1 if lined else chips

    def window_types(plan, keeps):
        return [pltpu.VMEM((group, shard, WIN), jnp.float32 if keeps else jnp.bfloat16) for _ in plan]

    def first_sends(plan):
        weights, *blocks = run_stage(
            functools.partial(window_kernel, stage_count - 1, len(stages[-1]), pieces, shard, plan),
            stages[-1],
            [ordered, bounds, chip_of_slot, cores],
            [pltpu.VMEM((2 * LANES, WIN), jnp.bfloat16)] + window_types(plan, False),
            work + len(plan) * group * shard * width * WIN * 2,
        )
        state.append(weights)
        return blocks

    def blocks_of(plan, keeps):
        if len(state) < 3:
            blocks = first_sends(plan)
        else:
            blocks = call(
                functools.partial(rest_kernel, shard, plan, keeps),
                [chip_of_slot, cores, pinned(state[0]), pinned(state[2])],
                [SMEM] * 2 + [VMEM] * 2,
                window_types(plan, keeps),
                [],
                {},
                len(plan) * group * shard * width * WIN * 2,
            )
        return [block[0] for block in blocks] if lined else blocks

    def hold(*arrays):
        state[0], *arrays = tie(state[0], *arrays)
        return arrays

    blocks_of.hold = hold
    factor = 1.0 / math.sqrt(owners * width)
    if lined:
        return collect(blocks_of, swap) * factor
    (send,), (keep,) = blocks_of([0], False), blocks_of([0], True)
    pair_sum = (keep + move(send, swap).astype(jnp.float32)).astype(jnp.bfloat16)
    block_sum = lax.psum_scatter(
        pair_sum.reshape(total // 2, WIN), "aux", axis_index_groups=same_core, scatter_dimension=0, tiled=True
    )
    return block_sum.astype(jnp.float32) * factor


def solution(mesh):
    placed = (
        P(("groups", "aux"), None),
        P(("groups", "aux"), None),
        P(("groups", "aux")),
        P(("groups", "aux"), None),
    )
    return jax.shard_map(
        local, mesh=mesh, in_specs=placed, out_specs=P(("groups", "aux"), None), check_vma=False
    )
```

```python
import functools
import math

import jax
import jax.numpy as jnp
from jax import lax
from jax.experimental import pallas as pl
from jax.experimental.pallas import tpu as pltpu
from jax.sharding import PartitionSpec as P

BLK = 64
WIN = 128
LANES = 128
UNROLL = 16
LINE = 4
SCOPED_BYTES = 6 * 1024 * 1024


def place(z, x, core):
    return (z * 2 + x) * 2 + core


def pairs_of(step):
    return [
        (place(z, x, core), place(*step(z, x), core)) for z in range(LINE) for x in range(2) for core in range(2)
    ]


def tie(*arrays):
    return lax.optimization_barrier(arrays)


def move(array, pairs):
    return lax.ppermute(array, "aux", pairs)


ALONG = pairs_of(lambda z, x: ((z + 1) % LINE, x))
BACK = pairs_of(lambda z, x: ((z - 1) % LINE, x))
ACROSS = pairs_of(lambda z, x: (z, 1 - x))
NEAR0, NEAR1, NEAR2, NEAR3, FAR0, FAR1, FAR2, FAR3 = range(2 * LINE)
ADD_AT = {(2, 1): 0, (3, 0): 1}
RAW_AT, LAY_AT = (0, 1), (1, 1)


def spread(parts, meanwhile):
    lines, others = [[part] for part in parts], [[] for _ in parts]

    def arrived(stage):
        held = [line[stage] for line in lines] if stage < LINE else []
        return held + ([other[stage - 1] for other in others] if stage else [])

    for step in range(LINE):
        for index, (line, other) in enumerate(zip(lines, others)):
            if other:
                line[-1], other[-1] = tie(line[-1], other[-1])
            turn = step == LINE - 1 and index == 0
            source = other if turn else line
            source[-1] = meanwhile(step, index, arrived, source[-1])
            now = source[-1]
            if step + 1 < LINE:
                line.append(move(now, ALONG))
            other.append(move(now, ALONG if turn else ACROSS))
    return [arrived(stage) for stage in range(LINE + 1)]


def collect(blocks_of, swap):
    def halves(array):
        return array[: array.shape[0] // 2], array[array.shape[0] // 2 :]

    def narrow(array):
        return array.astype(jnp.bfloat16)

    def wide(array):
        return array.astype(jnp.float32)

    def paired(send, keep):
        return keep + wide(move(send, swap))

    first = [FAR2, FAR1]
    rest = [NEAR2, FAR3, NEAR1, FAR0, NEAR3, NEAR0]
    sends = blocks_of(first, False)
    total = {name: paired(*pair) for name, *pair in zip(first, sends, blocks_of(first, True))}
    aside, beside = map(narrow, halves(total[FAR1]))
    crossing = narrow(total[FAR2])
    crossing, aside, beside = blocks_of.hold(crossing, aside, beside)
    two_on = move(crossing, ACROSS)
    joining = move(aside, ALONG)
    total.update({name: paired(*pair) for name, *pair in zip(rest, blocks_of(rest, False), blocks_of(rest, True))})

    two_on, joining = tie(two_on, joining)
    beside, two_on = tie(beside, two_on)
    beside = move(beside, ACROSS)
    three_on, two_on = tie(narrow(total[FAR3]), two_on)
    three_on = move(three_on, ACROSS)
    two_on = move(narrow(total[NEAR2] + wide(two_on)), ALONG)
    rows = beside.shape[0]
    beside, joining = jnp.pad(wide(beside), ((rows, 0), (0, 0))), jnp.pad(wide(joining), ((0, rows), (0, 0)))
    one_on = move(narrow(total[NEAR1] + wide(two_on) + beside), ALONG)
    total[FAR0], two_on = tie(total[FAR0], two_on)
    crossing, three_on = tie(narrow(total[FAR0] + joining), three_on)
    straight = move(crossing, ACROSS)
    one_back = move(narrow(total[NEAR3] + wide(three_on)), BACK)
    return total[NEAR0] + wide(one_on) + wide(straight) + wide(one_back)


def clear(half):
    whole = half.shape[0] // (4 * BLK) * (4 * BLK)

    @pl.loop(0, whole // (4 * BLK))
    def _(index):
        half[pl.ds(pl.multiple_of(index * 4 * BLK, BLK), 4 * BLK), :] = jnp.zeros((4 * BLK, LANES), jnp.float32)

    half[pl.ds(whole, half.shape[0] - whole), :] = jnp.zeros((half.shape[0] - whole, LANES), jnp.float32)


def add_tiles(stage, pieces, table_ref, bounds_ref, tiles, half, occ, sem):
    pltpu.make_async_copy(occ, occ, sem).wait()
    begin, end = bounds_ref[stage], bounds_ref[stage + 1]
    low = lax.broadcasted_iota(jnp.int32, tiles.shape[1:], 1) < BLK
    zero = jnp.zeros(tiles.shape[1:], jnp.bfloat16)
    spill = half.shape[0] - BLK
    entries = table_ref.shape[0] // (2 + pieces)
    piece = BLK // pieces

    @pl.loop(0, (end - begin + UNROLL - 1) // UNROLL)
    def _(group):
        products, starts = [], []
        for lane in range(UNROLL):
            entry = begin + group * UNROLL + lane
            tile = table_ref[entry]
            starts.append(jnp.where(entry < end, table_ref[entries + entry], spill))
            spots = [jnp.where(entry < end, table_ref[(2 + cut) * entries + entry], 0) for cut in range(pieces)]
            parts = [occ[pl.ds(pl.multiple_of(spot, piece), piece), :] for spot in spots]
            pair = tiles[tile]
            left = jnp.concatenate([jnp.where(low, pair, zero), jnp.where(low, zero, pair)], axis=0)
            block = jnp.concatenate(parts * 2, axis=0)
            products.append(jnp.dot(left, block, preferred_element_type=jnp.float32))
        for product, start in zip(products, starts):
            start = pl.multiple_of(start, BLK)
            for odd in range(2):
                span = pl.ds(start + odd, BLK // 2, stride=2)
                half[span, :] += product[odd * (BLK // 2) : (odd + 1) * (BLK // 2)]


def fill_window(half, weights, shard, chips_ref, first, parity, out):
    side_rows = (half.shape[0] - BLK) // 2

    @pl.loop(0, out.shape[0])
    def _(index):
        start = pl.multiple_of((2 * chips_ref[first + index] + parity) * shard, 32)
        both = jnp.concatenate(
            [half[pl.ds(side * side_rows + start, shard), :].astype(jnp.bfloat16) for side in range(2)], axis=1
        )
        out[index] = jnp.dot(both, weights[...], preferred_element_type=jnp.float32).astype(out.dtype)


def load_tiles(tile_sets, tiles, sems):
    slots = tile_sets[0].shape[0]
    copies = [
        pltpu.make_async_copy(source, tiles.at[pl.ds(index * slots, slots)], sems.at[index])
        for index, source in enumerate(tile_sets)
    ]
    for copy in copies:
        copy.start()
    return copies


def add_stage(stage, count, pieces, table_ref, bounds_ref, refs):
    sources = refs[:count]
    *_, occ, sems = refs
    rows = sources[0].shape[0]
    for index, source in enumerate(sources):
        pltpu.make_async_copy(source, occ.at[pl.ds(index * rows, rows)], sems.at[2]).start()
    if stage:
        tiles, _, half, *outs = refs[count:-2]
        copies = []
    else:
        *tile_sets, half, tiles = refs[count : count + 4]
        outs = refs[count + 4 : -2]
        copies = load_tiles(tile_sets, tiles, sems)
        clear(half)
    for copy in copies:
        copy.wait()
    add_tiles(stage, pieces, table_ref, bounds_ref, tiles, half, occ, sems.at[2])
    return half, outs


def stage_kernel(stage, count, pieces, table_ref, bounds_ref, *refs):
    add_stage(stage, count, pieces, table_ref, bounds_ref, refs)


def window_kernel(stage, count, pieces, shard, plan, table_ref, bounds_ref, chips_ref, core_ref, *refs):
    half, (weights, *outs) = add_stage(stage, count, pieces, table_ref, bounds_ref, refs)
    side_rows = (half.shape[0] - BLK) // 2
    for side in range(2):
        weights[pl.ds(side * LANES, LANES), :] = half[pl.ds(side * side_rows, WIN), :].T.astype(jnp.bfloat16)
    rest_kernel(shard, plan, False, chips_ref, core_ref, half, weights, *outs)


def rest_kernel(shard, plan, keeps, chips_ref, core_ref, half, weights, *outs):
    for first, out in zip(plan, outs):
        fill_window(half, weights, shard, chips_ref, first, core_ref[0] if keeps else 1 - core_ref[0], out)


SMEM = pl.BlockSpec(memory_space=pltpu.SMEM)
HBM = pl.BlockSpec(memory_space=pl.ANY)
VMEM = pl.BlockSpec(memory_space=pltpu.VMEM)


def pinned(array):
    return pltpu.with_memory_space_constraint(array, pltpu.VMEM)


def held(array):
    return pltpu.with_memory_space_constraint(array, pltpu.HBM)


def call(kernel, ins, in_specs, outs, scratch, aliases, flops, scoped=0):
    return pl.pallas_call(
        kernel,
        out_shape=outs,
        in_specs=in_specs,
        out_specs=[VMEM] * len(outs),
        scratch_shapes=scratch,
        input_output_aliases=aliases,
        compiler_params=pltpu.CompilerParams(vmem_limit_bytes=SCOPED_BYTES + scoped),
        cost_estimate=pl.CostEstimate(flops=flops, bytes_accessed=4 << 20, transcendentals=0),
    )(*ins)


def local(block_values, block_pairs, live_counts, occupied):
    owners = lax.axis_size("aux")
    me = lax.axis_index("aux")
    core, chip = me % 2, me // 2
    shard, width = occupied.shape
    total = owners * shard
    slots = block_values.shape[0]
    piece = math.gcd(BLK, shard)
    pieces = BLK // piece
    chips = owners // 2
    lined = chips == 2 * LINE
    same_core = [[2 * i + k for i in range(chips)] for k in range(2)]
    swap = [(i, i ^ 1) for i in range(owners)]

    mine = lax.dynamic_slice_in_dim(occupied, core * LANES, LANES, 1)
    given = lax.dynamic_slice_in_dim(occupied, (1 - core) * LANES, LANES, 1)
    parts = [mine, move(given, swap)]
    others = [move(array, swap) for array in (block_values, block_pairs, live_counts)]
    raw_sets = [block_values, others[0]]
    tile_sets = []

    def lay_tiles():
        tile_sets[:] = [values.reshape(slots, BLK * BLK // LANES, LANES) for values in raw_sets]

    slot_ids = jnp.arange(chips, dtype=jnp.int32)
    chip_of_slot = slot_ids
    stage_count = 1
    if lined:
        chip_of_slot = (slot_ids + chip // 2) % LINE * 2 + ((slot_ids // LINE) ^ (chip % 2))
        stage_count = LINE + 1

    tile_ids = jnp.arange(2 * slots, dtype=jnp.int32)
    pairs = jnp.concatenate([block_pairs, others[1]])
    live = tile_ids % slots < jnp.where(tile_ids < slots, live_counts[0], others[2][0])
    first = pairs[:, 1][:, None] * BLK + jnp.arange(pieces, dtype=jnp.int32) * piece
    owner = first // shard
    part = (owner % 2) ^ core
    owner_chip = owner // 2
    if lined:
        back = (chip // 2 - owner_chip // 2) % LINE
        side = (owner_chip % 2) ^ (chip % 2)
        stage = (back + side)[:, 0]
        slot_of = part + 2 * jnp.where(back + side < LINE, side, 0)
    else:
        stage = jnp.zeros_like(tile_ids)
        slot_of = part * chips + owner_chip
    spots = slot_of * shard + first % shard
    stage = jnp.where(live, stage, stage_count)
    rows = pairs[:, 0] * BLK + tile_ids // slots * total
    ahead = (stage[None, :] < stage[:, None]) | (
        (stage[None, :] == stage[:, None]) & (tile_ids[None, :] < tile_ids[:, None])
    )
    rank = jnp.sum(ahead.astype(jnp.int32), axis=1)
    entries = jnp.arange(2 * slots + UNROLL, dtype=jnp.int32)
    chosen = rank[None, :] == entries[:, None]
    columns = [tile_ids, rows] + [spots[:, cut] for cut in range(pieces)]
    ordered = jnp.concatenate([jnp.sum(jnp.where(chosen, column[None, :], 0), axis=1) for column in columns])
    bounds = jnp.sum((stage[None, :] < jnp.arange(stage_count + 1)[:, None]).astype(jnp.int32), axis=1)
    cores = core.astype(jnp.int32).reshape(1)

    half_type = pltpu.VMEM((2 * total + BLK, LANES), jnp.float32)
    tiles_type = pltpu.VMEM((2 * slots, BLK * BLK // LANES, LANES), jnp.bfloat16)
    work = 4 * slots * BLK * BLK * LANES // stage_count
    state = []

    def run_stage(kernel, sources, tables, outs, flops):
        rows = len(sources) * sources[0].shape[0]
        scratch = [pltpu.VMEM((rows, LANES), jnp.bfloat16), pltpu.SemaphoreType.DMA((3,))]
        ins, specs = [*tables, *sources], [SMEM] * len(tables) + [HBM] * len(sources)
        made, aliases = [half_type], {}
        if state:
            aliases = {len(ins) + 1: 0}
            ins, specs = ins + [pinned(state[1]), pinned(state[0])], specs + [VMEM] * 2
        else:
            ins = [*tables, *map(held, sources), tile_sets[0], held(tile_sets[1])]
            specs = specs + [HBM] * 2
            made = [half_type, tiles_type]
        results = call(kernel, ins, specs, made + outs, scratch, aliases, flops, 2 * rows * LANES)
        state[:] = [results[0], state[1] if state else results[1]]
        return results[len(made) :]

    def add(stage, sources):
        kernel = functools.partial(stage_kernel, stage, len(sources), pieces)
        run_stage(kernel, sources, [ordered, bounds], [], work)

    def meanwhile(step, index, arrived, moved):
        if (step, index) == RAW_AT:
            moved, *raw_sets[:] = tie(moved, *raw_sets)
            lay_tiles()
        if (step, index) == LAY_AT:
            moved, *tile_sets[:] = tie(moved, *tile_sets)
        if (step, index) in ADD_AT:
            stage = ADD_AT[step, index]
            add(stage, arrived(stage))
            moved, state[0] = tie(moved, state[0])
        return moved

    if lined:
        stages = spread(parts, meanwhile)
        for stage in range(len(ADD_AT), LINE):
            add(stage, stages[stage])
    else:
        lay_tiles()
        stages = [[lax.all_gather(part, "aux", axis_index_groups=same_core, axis=0, tiled=True) for part in parts]]

    group = 1 if lined else chips

    def window_types(plan, keeps):
        return [pltpu.VMEM((group, shard, WIN), jnp.float32 if keeps else jnp.bfloat16) for _ in plan]

    def first_sends(plan):
        weights, *blocks = run_stage(
            functools.partial(window_kernel, stage_count - 1, len(stages[-1]), pieces, shard, plan),
            stages[-1],
            [ordered, bounds, chip_of_slot, cores],
            [pltpu.VMEM((2 * LANES, WIN), jnp.bfloat16)] + window_types(plan, False),
            work + len(plan) * group * shard * width * WIN * 2,
        )
        state.append(weights)
        return blocks

    def blocks_of(plan, keeps):
        if len(state) < 3:
            blocks = first_sends(plan)
        else:
            blocks = call(
                functools.partial(rest_kernel, shard, plan, keeps),
                [chip_of_slot, cores, pinned(state[0]), pinned(state[2])],
                [SMEM] * 2 + [VMEM] * 2,
                window_types(plan, keeps),
                [],
                {},
                len(plan) * group * shard * width * WIN * 2,
            )
        return [block[0] for block in blocks] if lined else blocks

    def hold(*arrays):
        state[0], *arrays = tie(state[0], *arrays)
        return arrays

    blocks_of.hold = hold
    factor = 1.0 / math.sqrt(owners * width)
    if lined:
        return collect(blocks_of, swap) * factor
    (send,), (keep,) = blocks_of([0], False), blocks_of([0], True)
    pair_sum = (keep + move(send, swap).astype(jnp.float32)).astype(jnp.bfloat16)
    block_sum = lax.psum_scatter(
        pair_sum.reshape(total // 2, WIN), "aux", axis_index_groups=same_core, scatter_dimension=0, tiled=True
    )
    return block_sum.astype(jnp.float32) * factor


def solution(mesh):
    placed = (
        P(("groups", "aux"), None),
        P(("groups", "aux"), None),
        P(("groups", "aux")),
        P(("groups", "aux"), None),
    )
    return jax.shard_map(
        local, mesh=mesh, in_specs=placed, out_specs=P(("groups", "aux"), None), check_vma=False
    )
```

```python
import functools
import math

import jax
import jax.numpy as jnp
from jax import lax
from jax.experimental import pallas as pl
from jax.experimental.pallas import tpu as pltpu
from jax.sharding import PartitionSpec as P

BLK = 64
WIN = 128
LANES = 128
UNROLL = 16
TAIL = 2 * BLK
LINE = 4
SCOPED_BYTES = 6 * 1024 * 1024


def place(z, x, core):
    return (z * 2 + x) * 2 + core


def pairs_of(step):
    return [
        (place(z, x, core), place(*step(z, x), core)) for z in range(LINE) for x in range(2) for core in range(2)
    ]


def tie(*arrays):
    return lax.optimization_barrier(arrays)


def move(array, pairs):
    return lax.ppermute(array, "aux", pairs)


ALONG = pairs_of(lambda z, x: ((z + 1) % LINE, x))
BACK = pairs_of(lambda z, x: ((z - 1) % LINE, x))
ACROSS = pairs_of(lambda z, x: (z, 1 - x))
NEAR0, NEAR1, NEAR2, NEAR3, FAR0, FAR1, FAR2, FAR3 = range(2 * LINE)
ADD_AT = {(2, 1): 0, (3, 0): 1}
RAW_AT, LAY_AT = (0, 1), (1, 1)


def spread(parts, meanwhile):
    lines, others = [[part] for part in parts], [[] for _ in parts]

    def arrived(stage):
        held = [line[stage] for line in lines] if stage < LINE else []
        return held + ([other[stage - 1] for other in others] if stage else [])

    for step in range(LINE):
        for index, (line, other) in enumerate(zip(lines, others)):
            if other:
                line[-1], other[-1] = tie(line[-1], other[-1])
            turn = step == LINE - 1 and index == 0
            source = other if turn else line
            source[-1] = meanwhile(step, index, arrived, source[-1])
            now = source[-1]
            if step + 1 < LINE:
                line.append(move(now, ALONG))
            other.append(move(now, ALONG if turn else ACROSS))
    return [arrived(stage) for stage in range(LINE + 1)]


def collect(blocks_of, swap):
    def halves(array):
        return array[: array.shape[0] // 2], array[array.shape[0] // 2 :]

    def narrow(array):
        return array.astype(jnp.bfloat16)

    def wide(array):
        return array.astype(jnp.float32)

    def paired(send, keep):
        return keep + wide(move(send, swap))

    first = [FAR2, FAR1, NEAR2]
    rest = [FAR3, NEAR1, FAR0, NEAR3, NEAR0]
    sends = blocks_of(first, False)
    total = {name: paired(*pair) for name, *pair in zip(first, sends, blocks_of(first, True))}
    crossing, aside = list(map(narrow, halves(total[FAR2]))), narrow(total[FAR1])
    *crossing, aside = blocks_of.hold(*crossing, aside)
    two_on = [move(part, ACROSS) for part in crossing]
    joining = move(aside, ALONG)
    total.update({name: paired(*pair) for name, *pair in zip(rest, blocks_of(rest, False), blocks_of(rest, True))})

    crossing, two_on[1] = tie(narrow(total[FAR3]), two_on[1])
    three_on = move(crossing, ACROSS)
    crossing, three_on = tie(narrow(total[FAR0] + wide(joining)), three_on)
    straight = move(crossing, ACROSS)
    two_on = [move(narrow(own + wide(part)), ALONG) for own, part in zip(halves(total[NEAR2]), two_on)]
    later, two_on[0] = tie(total[NEAR1], two_on[0])
    one_on = [
        move(narrow(halves(own)[index] + wide(two_on[index])), ALONG)
        for index, own in enumerate((total[NEAR1], later))
    ]
    one_back = move(narrow(total[NEAR3] + wide(three_on)), BACK)
    (result,) = tie(total[NEAR0] + wide(jnp.concatenate(one_on)))
    return result + wide(straight) + wide(one_back)


def clear(half):
    whole = half.shape[0] // (4 * BLK) * (4 * BLK)

    @pl.loop(0, whole // (4 * BLK))
    def _(index):
        half[pl.ds(pl.multiple_of(index * 4 * BLK, BLK), 4 * BLK), :] = jnp.zeros((4 * BLK, LANES), jnp.float32)

    half[pl.ds(whole, half.shape[0] - whole), :] = jnp.zeros((half.shape[0] - whole, LANES), jnp.float32)


def add_tiles(stage, pieces, table_ref, bounds_ref, tiles, half, occ, sem):
    pltpu.make_async_copy(occ, occ, sem).wait()
    begin, end = bounds_ref[stage], bounds_ref[stage + 1]
    low = lax.broadcasted_iota(jnp.int32, tiles.shape[1:], 1) < BLK
    zero = jnp.zeros(tiles.shape[1:], jnp.bfloat16)
    spill = half.shape[0] - TAIL
    entries = table_ref.shape[0] // (2 + pieces)
    piece = BLK // pieces

    @pl.loop(0, (end - begin + UNROLL - 1) // UNROLL)
    def _(group):
        products, starts = [], []
        for lane in range(UNROLL):
            entry = begin + group * UNROLL + lane
            tile = table_ref[entry]
            starts.append(jnp.where(entry < end, table_ref[entries + entry], spill))
            spots = [jnp.where(entry < end, table_ref[(2 + cut) * entries + entry], 0) for cut in range(pieces)]
            parts = [occ[pl.ds(pl.multiple_of(spot, piece), piece), :] for spot in spots]
            pair = tiles[tile]
            left = jnp.concatenate([jnp.where(low, pair, zero), jnp.where(low, zero, pair)], axis=0)
            block = jnp.concatenate(parts * 2, axis=0)
            products.append(jnp.dot(left, block, preferred_element_type=jnp.float32))
        for product, start in zip(products, starts):
            start = pl.multiple_of(start, BLK)
            for odd in range(2):
                span = pl.ds(start + odd, BLK // 2, stride=2)
                half[span, :] += product[odd * (BLK // 2) : (odd + 1) * (BLK // 2)]


def fill_window(half, weights, shard, chips_ref, first, parity, out):
    side_rows = (half.shape[0] - TAIL) // 2

    @pl.loop(0, out.shape[0])
    def _(index):
        start = pl.multiple_of((2 * chips_ref[first + index] + parity) * shard, 32)
        both = jnp.concatenate(
            [half[pl.ds(side * side_rows + start, shard), :].astype(jnp.bfloat16) for side in range(2)], axis=1
        )
        out[index] = jnp.dot(both, weights[...], preferred_element_type=jnp.float32).astype(out.dtype)


def load_tiles(tile_sets, tiles, sems):
    slots = tile_sets[0].shape[0]
    copies = [
        pltpu.make_async_copy(source, tiles.at[pl.ds(index * slots, slots)], sems.at[index])
        for index, source in enumerate(tile_sets)
    ]
    for copy in copies:
        copy.start()
    return copies


def add_stage(stage, count, pieces, table_ref, bounds_ref, refs):
    sources = refs[:count]
    *_, occ, sems = refs
    rows = sources[0].shape[0]
    for index, source in enumerate(sources):
        pltpu.make_async_copy(source, occ.at[pl.ds(index * rows, rows)], sems.at[2]).start()
    if stage:
        tiles, _, half, *outs = refs[count:-2]
        copies = []
    else:
        *tile_sets, half, tiles = refs[count : count + 4]
        outs = refs[count + 4 : -2]
        copies = load_tiles(tile_sets, tiles, sems)
        clear(half)
    for copy in copies:
        copy.wait()
    add_tiles(stage, pieces, table_ref, bounds_ref, tiles, half, occ, sems.at[2])
    return half, outs


def stage_kernel(stage, count, pieces, table_ref, bounds_ref, *refs):
    add_stage(stage, count, pieces, table_ref, bounds_ref, refs)


def window_kernel(stage, count, pieces, shard, plan, table_ref, bounds_ref, chips_ref, core_ref, *refs):
    half, (weights, *outs) = add_stage(stage, count, pieces, table_ref, bounds_ref, refs)
    side_rows = (half.shape[0] - TAIL) // 2
    for side in range(2):
        weights[pl.ds(side * LANES, LANES), :] = half[pl.ds(side * side_rows, WIN), :].T.astype(jnp.bfloat16)
    rest_kernel(shard, plan, False, chips_ref, core_ref, half, weights, *outs)


def rest_kernel(shard, plan, keeps, chips_ref, core_ref, half, weights, *outs):
    for first, out in zip(plan, outs):
        fill_window(half, weights, shard, chips_ref, first, core_ref[0] if keeps else 1 - core_ref[0], out)


SMEM = pl.BlockSpec(memory_space=pltpu.SMEM)
HBM = pl.BlockSpec(memory_space=pl.ANY)
VMEM = pl.BlockSpec(memory_space=pltpu.VMEM)


def pinned(array):
    return pltpu.with_memory_space_constraint(array, pltpu.VMEM)


def held(array):
    return pltpu.with_memory_space_constraint(array, pltpu.HBM)


def call(kernel, ins, in_specs, outs, scratch, aliases, flops, scoped=0):
    return pl.pallas_call(
        kernel,
        out_shape=outs,
        in_specs=in_specs,
        out_specs=[VMEM] * len(outs),
        scratch_shapes=scratch,
        input_output_aliases=aliases,
        compiler_params=pltpu.CompilerParams(vmem_limit_bytes=SCOPED_BYTES + scoped),
        cost_estimate=pl.CostEstimate(flops=flops, bytes_accessed=4 << 20, transcendentals=0),
    )(*ins)


def local(block_values, block_pairs, live_counts, occupied):
    owners = lax.axis_size("aux")
    me = lax.axis_index("aux")
    core, chip = me % 2, me // 2
    shard, width = occupied.shape
    total = owners * shard
    slots = block_values.shape[0]
    piece = math.gcd(BLK, shard)
    pieces = BLK // piece
    chips = owners // 2
    lined = chips == 2 * LINE
    same_core = [[2 * i + k for i in range(chips)] for k in range(2)]
    swap = [(i, i ^ 1) for i in range(owners)]

    mine = lax.dynamic_slice_in_dim(occupied, core * LANES, LANES, 1)
    given = lax.dynamic_slice_in_dim(occupied, (1 - core) * LANES, LANES, 1)
    parts = [mine, move(given, swap)]
    others = [move(array, swap) for array in (block_values, block_pairs, live_counts)]
    raw_sets = [block_values, others[0]]
    tile_sets = []

    def lay_tiles():
        tile_sets[:] = [values.reshape(slots, BLK * BLK // LANES, LANES) for values in raw_sets]

    slot_ids = jnp.arange(chips, dtype=jnp.int32)
    chip_of_slot = slot_ids
    stage_count = 1
    if lined:
        chip_of_slot = (slot_ids + chip // 2) % LINE * 2 + ((slot_ids // LINE) ^ (chip % 2))
        stage_count = LINE + 1

    tile_ids = jnp.arange(2 * slots, dtype=jnp.int32)
    pairs = jnp.concatenate([block_pairs, others[1]])
    live = tile_ids % slots < jnp.where(tile_ids < slots, live_counts[0], others[2][0])
    first = pairs[:, 1][:, None] * BLK + jnp.arange(pieces, dtype=jnp.int32) * piece
    owner = first // shard
    part = (owner % 2) ^ core
    owner_chip = owner // 2
    if lined:
        back = (chip // 2 - owner_chip // 2) % LINE
        side = (owner_chip % 2) ^ (chip % 2)
        stage = (back + side)[:, 0]
        slot_of = part + 2 * jnp.where(back + side < LINE, side, 0)
    else:
        stage = jnp.zeros_like(tile_ids)
        slot_of = part * chips + owner_chip
    spots = slot_of * shard + first % shard
    stage = jnp.where(live, stage, stage_count)
    rows = pairs[:, 0] * BLK + tile_ids // slots * total
    ahead = (stage[None, :] < stage[:, None]) | (
        (stage[None, :] == stage[:, None]) & (tile_ids[None, :] < tile_ids[:, None])
    )
    rank = jnp.sum(ahead.astype(jnp.int32), axis=1)
    entries = jnp.arange(2 * slots + UNROLL, dtype=jnp.int32)
    chosen = rank[None, :] == entries[:, None]
    columns = [tile_ids, rows] + [spots[:, cut] for cut in range(pieces)]
    ordered = jnp.concatenate([jnp.sum(jnp.where(chosen, column[None, :], 0), axis=1) for column in columns])
    bounds = jnp.sum((stage[None, :] < jnp.arange(stage_count + 1)[:, None]).astype(jnp.int32), axis=1)
    cores = core.astype(jnp.int32).reshape(1)

    half_type = pltpu.VMEM((2 * total + TAIL, LANES), jnp.float32)
    tiles_type = pltpu.VMEM((2 * slots, BLK * BLK // LANES, LANES), jnp.bfloat16)
    work = 4 * slots * BLK * BLK * LANES // stage_count
    state = []

    def run_stage(kernel, sources, tables, outs, flops):
        rows = len(sources) * sources[0].shape[0]
        scratch = [pltpu.VMEM((rows, LANES), jnp.bfloat16), pltpu.SemaphoreType.DMA((3,))]
        ins, specs = [*tables, *sources], [SMEM] * len(tables) + [HBM] * len(sources)
        made, aliases = [half_type], {}
        if state:
            aliases = {len(ins) + 1: 0}
            ins, specs = ins + [pinned(state[1]), pinned(state[0])], specs + [VMEM] * 2
        else:
            ins = [*tables, *map(held, sources), tile_sets[0], held(tile_sets[1])]
            specs = specs + [HBM] * 2
            made = [half_type, tiles_type]
        results = call(kernel, ins, specs, made + outs, scratch, aliases, flops, 2 * rows * LANES)
        state[:] = [results[0], state[1] if state else results[1]]
        return results[len(made) :]

    def add(stage, sources):
        kernel = functools.partial(stage_kernel, stage, len(sources), pieces)
        run_stage(kernel, sources, [ordered, bounds], [], work)

    def meanwhile(step, index, arrived, moved):
        if (step, index) == RAW_AT:
            moved, *raw_sets[:] = tie(moved, *raw_sets)
            lay_tiles()
        if (step, index) == LAY_AT:
            moved, *tile_sets[:] = tie(moved, *tile_sets)
        if (step, index) in ADD_AT:
            stage = ADD_AT[step, index]
            add(stage, arrived(stage))
            moved, state[0] = tie(moved, state[0])
        return moved

    if lined:
        stages = spread(parts, meanwhile)
        for stage in range(len(ADD_AT), LINE):
            add(stage, stages[stage])
    else:
        lay_tiles()
        stages = [[lax.all_gather(part, "aux", axis_index_groups=same_core, axis=0, tiled=True) for part in parts]]

    group = 1 if lined else chips

    def window_types(plan, keeps):
        return [pltpu.VMEM((group, shard, WIN), jnp.float32 if keeps else jnp.bfloat16) for _ in plan]

    def first_sends(plan):
        weights, *blocks = run_stage(
            functools.partial(window_kernel, stage_count - 1, len(stages[-1]), pieces, shard, plan),
            stages[-1],
            [ordered, bounds, chip_of_slot, cores],
            [pltpu.VMEM((2 * LANES, WIN), jnp.bfloat16)] + window_types(plan, False),
            work + len(plan) * group * shard * width * WIN * 2,
        )
        state.append(weights)
        return blocks

    def blocks_of(plan, keeps):
        if len(state) < 3:
            blocks = first_sends(plan)
        else:
            blocks = call(
                functools.partial(rest_kernel, shard, plan, keeps),
                [chip_of_slot, cores, pinned(state[0]), pinned(state[2])],
                [SMEM] * 2 + [VMEM] * 2,
                window_types(plan, keeps),
                [],
                {},
                len(plan) * group * shard * width * WIN * 2,
            )
        return [block[0] for block in blocks] if lined else blocks

    def hold(*arrays):
        state[0], *arrays = tie(state[0], *arrays)
        return arrays

    blocks_of.hold = hold
    factor = 1.0 / math.sqrt(owners * width)
    if lined:
        return collect(blocks_of, swap) * factor
    (send,), (keep,) = blocks_of([0], False), blocks_of([0], True)
    pair_sum = (keep + move(send, swap).astype(jnp.float32)).astype(jnp.bfloat16)
    block_sum = lax.psum_scatter(
        pair_sum.reshape(total // 2, WIN), "aux", axis_index_groups=same_core, scatter_dimension=0, tiled=True
    )
    return block_sum.astype(jnp.float32) * factor


def solution(mesh):
    placed = (
        P(("groups", "aux"), None),
        P(("groups", "aux"), None),
        P(("groups", "aux")),
        P(("groups", "aux"), None),
    )
    return jax.shard_map(
        local, mesh=mesh, in_specs=placed, out_specs=P(("groups", "aux"), None), check_vma=False
    )
```

```python
import functools
import math

import jax
import jax.numpy as jnp
from jax import lax
from jax.experimental import pallas as pl
from jax.experimental.pallas import tpu as pltpu
from jax.sharding import PartitionSpec as P

BLK = 64
WIN = 128
LANES = 128
UNROLL = 24
TAIL = 2 * BLK
LINE = 4
SCOPED_BYTES = 6 * 1024 * 1024


def place(z, x, core):
    return (z * 2 + x) * 2 + core


def pairs_of(step):
    return [
        (place(z, x, core), place(*step(z, x), core)) for z in range(LINE) for x in range(2) for core in range(2)
    ]


def tie(*arrays):
    return lax.optimization_barrier(arrays)


def move(array, pairs):
    return lax.ppermute(array, "aux", pairs)


ALONG = pairs_of(lambda z, x: ((z + 1) % LINE, x))
BACK = pairs_of(lambda z, x: ((z - 1) % LINE, x))
ACROSS = pairs_of(lambda z, x: (z, 1 - x))
NEAR0, NEAR1, NEAR2, NEAR3, FAR0, FAR1, FAR2, FAR3 = range(2 * LINE)
ADD_AT = {(2, 1): 0, (3, 0): 1}
RAW_AT, LAY_AT = (0, 1), (1, 1)


def spread(parts, meanwhile):
    lines, others = [[part] for part in parts], [[] for _ in parts]

    def arrived(stage):
        held = [line[stage] for line in lines] if stage < LINE else []
        return held + ([other[stage - 1] for other in others] if stage else [])

    for step in range(LINE):
        for index, (line, other) in enumerate(zip(lines, others)):
            if other:
                line[-1], other[-1] = tie(line[-1], other[-1])
            turn = step == LINE - 1 and index == 0
            source = other if turn else line
            source[-1] = meanwhile(step, index, arrived, source[-1])
            now = source[-1]
            if step + 1 < LINE:
                line.append(move(now, ALONG))
            other.append(move(now, ALONG if turn else ACROSS))
    return [arrived(stage) for stage in range(LINE + 1)]


def collect(blocks_of, swap):
    def halves(array):
        return array[: array.shape[0] // 2], array[array.shape[0] // 2 :]

    def narrow(array):
        return array.astype(jnp.bfloat16)

    def wide(array):
        return array.astype(jnp.float32)

    def paired(send, keep):
        return keep + wide(move(send, swap))

    first = [FAR2, FAR1, NEAR2]
    rest = [FAR3, NEAR1, FAR0, NEAR3, NEAR0]
    sends = blocks_of(first, False)
    total = {name: paired(*pair) for name, *pair in zip(first, sends, blocks_of(first, True))}
    crossing, aside = list(map(narrow, halves(total[FAR2]))), narrow(total[FAR1])
    *crossing, aside = blocks_of.hold(*crossing, aside)
    two_on = [move(part, ACROSS) for part in crossing]
    joining = move(aside, ALONG)
    total.update({name: paired(*pair) for name, *pair in zip(rest, blocks_of(rest, False), blocks_of(rest, True))})

    crossing, two_on[1] = tie(narrow(total[FAR3]), two_on[1])
    three_on = move(crossing, ACROSS)
    crossing, three_on = tie(narrow(total[FAR0] + wide(joining)), three_on)
    straight = move(crossing, ACROSS)
    two_on = [move(narrow(own + wide(part)), ALONG) for own, part in zip(halves(total[NEAR2]), two_on)]
    later, two_on[0] = tie(total[NEAR1], two_on[0])
    one_on = [
        move(narrow(halves(own)[index] + wide(two_on[index])), ALONG)
        for index, own in enumerate((total[NEAR1], later))
    ]
    one_back = move(narrow(total[NEAR3] + wide(three_on)), BACK)
    (result,) = tie(total[NEAR0] + wide(jnp.concatenate(one_on)))
    return result + wide(straight) + wide(one_back)


def clear(half):
    whole = half.shape[0] // (4 * BLK) * (4 * BLK)

    @pl.loop(0, whole // (4 * BLK))
    def _(index):
        half[pl.ds(pl.multiple_of(index * 4 * BLK, BLK), 4 * BLK), :] = jnp.zeros((4 * BLK, LANES), jnp.float32)

    half[pl.ds(whole, half.shape[0] - whole), :] = jnp.zeros((half.shape[0] - whole, LANES), jnp.float32)


def add_tiles(stage, pieces, table_ref, bounds_ref, tiles, half, occ, sem):
    pltpu.make_async_copy(occ, occ, sem).wait()
    begin, end = bounds_ref[stage], bounds_ref[stage + 1]
    low = lax.broadcasted_iota(jnp.int32, tiles.shape[1:], 1) < BLK
    zero = jnp.zeros(tiles.shape[1:], jnp.bfloat16)
    spill = half.shape[0] - TAIL
    entries = table_ref.shape[0] // (2 + pieces)
    piece = BLK // pieces

    @pl.loop(0, (end - begin + UNROLL - 1) // UNROLL)
    def _(group):
        products, starts = [], []
        for lane in range(UNROLL):
            entry = begin + group * UNROLL + lane
            tile = table_ref[entry]
            starts.append(jnp.where(entry < end, table_ref[entries + entry], spill))
            spots = [jnp.where(entry < end, table_ref[(2 + cut) * entries + entry], 0) for cut in range(pieces)]
            parts = [occ[pl.ds(pl.multiple_of(spot, piece), piece), :] for spot in spots]
            pair = tiles[tile]
            left = jnp.concatenate([jnp.where(low, pair, zero), jnp.where(low, zero, pair)], axis=0)
            block = jnp.concatenate(parts * 2, axis=0)
            products.append(jnp.dot(left, block, preferred_element_type=jnp.float32))
        for product, start in zip(products, starts):
            start = pl.multiple_of(start, BLK)
            for odd in range(2):
                span = pl.ds(start + odd, BLK // 2, stride=2)
                half[span, :] += product[odd * (BLK // 2) : (odd + 1) * (BLK // 2)]


def fill_window(half, weights, shard, chips_ref, first, parity, out):
    side_rows = (half.shape[0] - TAIL) // 2

    @pl.loop(0, out.shape[0])
    def _(index):
        start = pl.multiple_of((2 * chips_ref[first + index] + parity) * shard, 32)
        both = jnp.concatenate(
            [half[pl.ds(side * side_rows + start, shard), :].astype(jnp.bfloat16) for side in range(2)], axis=1
        )
        out[index] = jnp.dot(both, weights[...], preferred_element_type=jnp.float32).astype(out.dtype)


def load_tiles(tile_sets, tiles, sems):
    slots = tile_sets[0].shape[0]
    copies = [
        pltpu.make_async_copy(source, tiles.at[pl.ds(index * slots, slots)], sems.at[index])
        for index, source in enumerate(tile_sets)
    ]
    for copy in copies:
        copy.start()
    return copies


def add_stage(stage, count, pieces, table_ref, bounds_ref, refs):
    sources = refs[:count]
    *_, occ, sems = refs
    rows = sources[0].shape[0]
    for index, source in enumerate(sources):
        pltpu.make_async_copy(source, occ.at[pl.ds(index * rows, rows)], sems.at[2]).start()
    if stage:
        tiles, _, half, *outs = refs[count:-2]
        copies = []
    else:
        *tile_sets, half, tiles = refs[count : count + 4]
        outs = refs[count + 4 : -2]
        copies = load_tiles(tile_sets, tiles, sems)
        clear(half)
    for copy in copies:
        copy.wait()
    add_tiles(stage, pieces, table_ref, bounds_ref, tiles, half, occ, sems.at[2])
    return half, outs


def stage_kernel(stage, count, pieces, table_ref, bounds_ref, *refs):
    add_stage(stage, count, pieces, table_ref, bounds_ref, refs)


def window_kernel(stage, count, pieces, shard, plan, table_ref, bounds_ref, chips_ref, core_ref, *refs):
    half, (weights, *outs) = add_stage(stage, count, pieces, table_ref, bounds_ref, refs)
    side_rows = (half.shape[0] - TAIL) // 2
    for side in range(2):
        weights[pl.ds(side * LANES, LANES), :] = half[pl.ds(side * side_rows, WIN), :].T.astype(jnp.bfloat16)
    rest_kernel(shard, plan, False, chips_ref, core_ref, half, weights, *outs)


def rest_kernel(shard, plan, keeps, chips_ref, core_ref, half, weights, *outs):
    for first, out in zip(plan, outs):
        fill_window(half, weights, shard, chips_ref, first, core_ref[0] if keeps else 1 - core_ref[0], out)


SMEM = pl.BlockSpec(memory_space=pltpu.SMEM)
HBM = pl.BlockSpec(memory_space=pl.ANY)
VMEM = pl.BlockSpec(memory_space=pltpu.VMEM)


def pinned(array):
    return pltpu.with_memory_space_constraint(array, pltpu.VMEM)


def held(array):
    return pltpu.with_memory_space_constraint(array, pltpu.HBM)


def call(kernel, ins, in_specs, outs, scratch, aliases, flops, scoped=0):
    return pl.pallas_call(
        kernel,
        out_shape=outs,
        in_specs=in_specs,
        out_specs=[VMEM] * len(outs),
        scratch_shapes=scratch,
        input_output_aliases=aliases,
        compiler_params=pltpu.CompilerParams(vmem_limit_bytes=SCOPED_BYTES + scoped),
        cost_estimate=pl.CostEstimate(flops=flops, bytes_accessed=4 << 20, transcendentals=0),
    )(*ins)


def local(block_values, block_pairs, live_counts, occupied):
    owners = lax.axis_size("aux")
    me = lax.axis_index("aux")
    core, chip = me % 2, me // 2
    shard, width = occupied.shape
    total = owners * shard
    slots = block_values.shape[0]
    piece = math.gcd(BLK, shard)
    pieces = BLK // piece
    chips = owners // 2
    lined = chips == 2 * LINE
    same_core = [[2 * i + k for i in range(chips)] for k in range(2)]
    swap = [(i, i ^ 1) for i in range(owners)]

    mine = lax.dynamic_slice_in_dim(occupied, core * LANES, LANES, 1)
    given = lax.dynamic_slice_in_dim(occupied, (1 - core) * LANES, LANES, 1)
    parts = [mine, move(given, swap)]
    others = [move(array, swap) for array in (block_values, block_pairs, live_counts)]
    raw_sets = [block_values, others[0]]
    tile_sets = []

    def lay_tiles():
        tile_sets[:] = [values.reshape(slots, BLK * BLK // LANES, LANES) for values in raw_sets]

    slot_ids = jnp.arange(chips, dtype=jnp.int32)
    chip_of_slot = slot_ids
    stage_count = 1
    if lined:
        chip_of_slot = (slot_ids + chip // 2) % LINE * 2 + ((slot_ids // LINE) ^ (chip % 2))
        stage_count = LINE + 1

    tile_ids = jnp.arange(2 * slots, dtype=jnp.int32)
    pairs = jnp.concatenate([block_pairs, others[1]])
    live = tile_ids % slots < jnp.where(tile_ids < slots, live_counts[0], others[2][0])
    first = pairs[:, 1][:, None] * BLK + jnp.arange(pieces, dtype=jnp.int32) * piece
    owner = first // shard
    part = (owner % 2) ^ core
    owner_chip = owner // 2
    if lined:
        back = (chip // 2 - owner_chip // 2) % LINE
        side = (owner_chip % 2) ^ (chip % 2)
        stage = (back + side)[:, 0]
        slot_of = part + 2 * jnp.where(back + side < LINE, side, 0)
    else:
        stage = jnp.zeros_like(tile_ids)
        slot_of = part * chips + owner_chip
    spots = slot_of * shard + first % shard
    stage = jnp.where(live, stage, stage_count)
    rows = pairs[:, 0] * BLK + tile_ids // slots * total
    ahead = (stage[None, :] < stage[:, None]) | (
        (stage[None, :] == stage[:, None]) & (tile_ids[None, :] < tile_ids[:, None])
    )
    rank = jnp.sum(ahead.astype(jnp.int32), axis=1)
    entries = jnp.arange(2 * slots + UNROLL, dtype=jnp.int32)
    chosen = rank[None, :] == entries[:, None]
    columns = [tile_ids, rows] + [spots[:, cut] for cut in range(pieces)]
    ordered = jnp.concatenate([jnp.sum(jnp.where(chosen, column[None, :], 0), axis=1) for column in columns])
    bounds = jnp.sum((stage[None, :] < jnp.arange(stage_count + 1)[:, None]).astype(jnp.int32), axis=1)
    cores = core.astype(jnp.int32).reshape(1)

    half_type = pltpu.VMEM((2 * total + TAIL, LANES), jnp.float32)
    tiles_type = pltpu.VMEM((2 * slots, BLK * BLK // LANES, LANES), jnp.bfloat16)
    work = 4 * slots * BLK * BLK * LANES // stage_count
    state = []

    def run_stage(kernel, sources, tables, outs, flops):
        rows = len(sources) * sources[0].shape[0]
        scratch = [pltpu.VMEM((rows, LANES), jnp.bfloat16), pltpu.SemaphoreType.DMA((3,))]
        ins, specs = [*tables, *sources], [SMEM] * len(tables) + [HBM] * len(sources)
        made, aliases = [half_type], {}
        if state:
            aliases = {len(ins) + 1: 0}
            ins, specs = ins + [pinned(state[1]), pinned(state[0])], specs + [VMEM] * 2
        else:
            ins = [*tables, *map(held, sources), tile_sets[0], held(tile_sets[1])]
            specs = specs + [HBM] * 2
            made = [half_type, tiles_type]
        results = call(kernel, ins, specs, made + outs, scratch, aliases, flops, 2 * rows * LANES)
        state[:] = [results[0], state[1] if state else results[1]]
        return results[len(made) :]

    def add(stage, sources):
        kernel = functools.partial(stage_kernel, stage, len(sources), pieces)
        run_stage(kernel, sources, [ordered, bounds], [], work)

    def meanwhile(step, index, arrived, moved):
        if (step, index) == RAW_AT:
            moved, *raw_sets[:] = tie(moved, *raw_sets)
            lay_tiles()
        if (step, index) == LAY_AT:
            moved, *tile_sets[:] = tie(moved, *tile_sets)
        if (step, index) in ADD_AT:
            stage = ADD_AT[step, index]
            add(stage, arrived(stage))
            moved, state[0] = tie(moved, state[0])
        return moved

    if lined:
        stages = spread(parts, meanwhile)
        for stage in range(len(ADD_AT), LINE):
            add(stage, stages[stage])
    else:
        lay_tiles()
        stages = [[lax.all_gather(part, "aux", axis_index_groups=same_core, axis=0, tiled=True) for part in parts]]

    group = 1 if lined else chips

    def window_types(plan, keeps):
        return [pltpu.VMEM((group, shard, WIN), jnp.float32 if keeps else jnp.bfloat16) for _ in plan]

    def first_sends(plan):
        weights, *blocks = run_stage(
            functools.partial(window_kernel, stage_count - 1, len(stages[-1]), pieces, shard, plan),
            stages[-1],
            [ordered, bounds, chip_of_slot, cores],
            [pltpu.VMEM((2 * LANES, WIN), jnp.bfloat16)] + window_types(plan, False),
            work + len(plan) * group * shard * width * WIN * 2,
        )
        state.append(weights)
        return blocks

    def blocks_of(plan, keeps):
        if len(state) < 3:
            blocks = first_sends(plan)
        else:
            blocks = call(
                functools.partial(rest_kernel, shard, plan, keeps),
                [chip_of_slot, cores, pinned(state[0]), pinned(state[2])],
                [SMEM] * 2 + [VMEM] * 2,
                window_types(plan, keeps),
                [],
                {},
                len(plan) * group * shard * width * WIN * 2,
            )
        return [block[0] for block in blocks] if lined else blocks

    def hold(*arrays):
        state[0], *arrays = tie(state[0], *arrays)
        return arrays

    blocks_of.hold = hold
    factor = 1.0 / math.sqrt(owners * width)
    if lined:
        return collect(blocks_of, swap) * factor
    (send,), (keep,) = blocks_of([0], False), blocks_of([0], True)
    pair_sum = (keep + move(send, swap).astype(jnp.float32)).astype(jnp.bfloat16)
    block_sum = lax.psum_scatter(
        pair_sum.reshape(total // 2, WIN), "aux", axis_index_groups=same_core, scatter_dimension=0, tiled=True
    )
    return block_sum.astype(jnp.float32) * factor


def solution(mesh):
    placed = (
        P(("groups", "aux"), None),
        P(("groups", "aux"), None),
        P(("groups", "aux")),
        P(("groups", "aux"), None),
    )
    return jax.shard_map(
        local, mesh=mesh, in_specs=placed, out_specs=P(("groups", "aux"), None), check_vma=False
    )
```
